512 devices in a mesh: gy: 8 (over y_hi, core), gx: 8 (over y_lo, x), img: 8 (over z).
Axes of the slice: x: 4, y: 8 (y_hi: 4, y_lo: 2; y = y_hi * 2 + y_lo), z: 8, core: 2. Of those that a mesh axis runs over, the one named last changes fastest.
Arguments:
- inputs: bfloat16 [8, 64, 128, 512], P('img', 'gy', 'gx'), may hold values from -6 to 6
- cotangent: bfloat16 [8, 64, 128, 512], P('img', 'gy', 'gx'), may hold values from -6 to 6
- norm_gain: float32 [512], replicated, may hold values from 0.1 to 1.9
- w_qkv: bfloat16 [512, 1536], replicated, may hold values from -0.25 to 0.25
- w_out: bfloat16 [512, 512], replicated, may hold values from -0.25 to 0.25
- head_scale: float32 [8], replicated, may hold values from 2 to 10
Outputs:
- mixed: bfloat16 [8, 64, 128, 512], P('img', 'gy', 'gx')
- grad_input: bfloat16 [8, 64, 128, 512], P('img', 'gy', 'gx')
- grad_qkv: float32 [512, 1536], P(('gy', 'gx'))
- grad_out: float32 [512, 512], P(('gy', 'gx'))
The draws below stay inside these ranges and needn't reach their ends.
All inputs are finite; a program needn't handle non-finite values.
Results may differ from the reference program's by a relative error of at most 0.012.
Values may be sent and summed in bfloat16 or wider, within the bound.
A program may use at most 64 MiB of HBM per device.

```python
import math
import jax
import jax.numpy as jnp
from jax import lax

D = 512
HEADS = 8
IMAGES = 8
NY = 64
NX = 128


def shard_levels(rng, extent, shards, smallest, top_value):
    def one(dim, parts):
        draws = jax.random.uniform(jax.random.fold_in(jax.random.fold_in(rng, 6), dim), (parts,), jnp.float32, smallest / len(shards), top_value / len(shards))
        return jnp.repeat(jnp.exp(draws), extent[dim] // parts).reshape((-1,) + (1,) * (len(extent) - dim - 1))

    gain = one(*shards[0])
    for cut in shards[1:]:
        gain = gain * one(*cut)
    return gain


def gaussian(rng, shape, deviation, most, pieces=(), kind=jnp.bfloat16):
    values = jax.random.normal(rng, shape, jnp.float32) * deviation
    if len(pieces) > 0:
        values = shard_levels(rng, shape, pieces, -0.22, 0.18) * values
    return jnp.clip(values, min=-most, max=most).astype(kind)


def setup_inputs(seed: int = 0) -> dict:
    seeds = jax.random.split(jax.random.key(seed), 7)
    inputs = gaussian(seeds[0], (IMAGES, NY, NX, D), 1.0, 6.0, ((0, 8), (1, 8), (2, 8)))
    cotangent = gaussian(seeds[1], (IMAGES, NY, NX, D), 1.0, 6.0, ((0, 8), (1, 8), (2, 8)))
    norm_gain = jnp.clip(1.0 + 0.18 * jax.random.normal(seeds[2], (D,), jnp.float32), 0.1, 1.9)
    w_qkv = gaussian(seeds[3], (D, 3 * D), D ** -0.5, 0.25)
    w_out = gaussian(seeds[4], (D, D), D ** -0.5, 0.25)
    head_scale = jnp.clip(jnp.exp(jax.random.uniform(seeds[5], (HEADS,), jnp.float32, math.log(2.0), math.log(10.0))), 2.0, 10.0)
    return {"inputs": inputs, "cotangent": cotangent, "norm_gain": norm_gain, "w_qkv": w_qkv, "w_out": w_out, "head_scale": head_scale}


def windows(values, axis_at):
    length = values.shape[axis_at] - 6
    blocks = length // 8
    widths = [(0, 0)] * values.ndim
    widths[axis_at] = (0, 2)
    padded = jnp.pad(values, widths)
    split_shape = values.shape[:axis_at] + (blocks, 8) + values.shape[axis_at + 1:]
    leading = lax.slice_in_dim(padded, 0, length, axis=axis_at).reshape(split_shape)
    trailing = lax.slice_in_dim(padded, 8, length + 8, axis=axis_at).reshape(split_shape)
    trailing = lax.slice_in_dim(trailing, 0, 6, axis=axis_at + 1)
    return jnp.concatenate([leading, trailing], axis=axis_at + 1)

def unwindows(gradient, axis_at):
    blocks = gradient.shape[axis_at]
    length = blocks * 8
    merged = gradient.shape[:axis_at] + (length,) + gradient.shape[axis_at + 2:]
    leading = lax.slice_in_dim(gradient, 0, 8, axis=axis_at + 1).reshape(merged)
    widths = [(0, 0)] * gradient.ndim
    widths[axis_at + 1] = (0, 2)
    trailing = jnp.pad(lax.slice_in_dim(gradient, 8, 14, axis=axis_at + 1), widths).reshape(merged)
    front_pad = [(0, 0)] * len(merged)
    front_pad[axis_at] = (0, 8)
    back_pad = [(0, 0)] * len(merged)
    back_pad[axis_at] = (8, 0)
    summed = jnp.pad(leading, front_pad) + jnp.pad(trailing, back_pad)
    return lax.slice_in_dim(summed, 0, length + 6, axis=axis_at)

def key_tiles(extended):
    both_win = windows(windows(extended, 0), 2)
    return both_win.transpose(0, 2, 1, 3, 4).reshape(-1, 196, extended.shape[-1])

def untile_keys(tiled, row_blocks, col_blocks):
    stacked = tiled.reshape(row_blocks, col_blocks, 14, 14, tiled.shape[-1]).transpose(0, 2, 1, 3, 4)
    return unwindows(unwindows(stacked, 2), 0)

def query_tiles(values):
    tile_rows, tile_cols, feats = values.shape
    shaped = values.reshape(tile_rows // 8, 8, tile_cols // 8, 8, feats)
    return shaped.transpose(0, 2, 1, 3, 4).reshape(-1, 64, feats)

def untile_queries(tiled, row_blocks, col_blocks):
    feats = tiled.shape[-1]
    shaped = tiled.reshape(row_blocks, col_blocks, 8, 8, feats).transpose(0, 2, 1, 3, 4)
    return shaped.reshape(row_blocks * 8, col_blocks * 8, feats)

def local_mask():
    query_ids = jnp.arange(64, dtype=jnp.int32)
    key_ids = jnp.arange(196, dtype=jnp.int32)
    row_gap = key_ids[None, :] // 14 - 3 - query_ids[:, None] // 8
    col_gap = key_ids[None, :] % 14 - 3 - query_ids[:, None] % 8
    return (jnp.abs(row_gap) <= 3) & (jnp.abs(col_gap) <= 3)

def tile_attention(queries, grad_attn, kv_ext, valid_ext, head_count):
    width = queries.shape[-1]
    head_dim = width // head_count
    q_tiles = query_tiles(queries)
    tiles = q_tiles.shape[0]
    q_heads = q_tiles.reshape(tiles, 64, head_count, head_dim).astype(jnp.float32)
    g_heads = query_tiles(grad_attn).reshape(tiles, 64, head_count, head_dim).astype(jnp.float32)
    keyed = key_tiles(kv_ext)
    k_heads = keyed[..., :width].reshape(tiles, 196, head_count, head_dim).astype(jnp.float32)
    v_heads = keyed[..., width:].reshape(tiles, 196, head_count, head_dim).astype(jnp.float32)
    allowed = local_mask()[None] & (key_tiles(valid_ext)[:, None, :, 0] > 0.5)
    scores = jnp.einsum('bqhd,bkhd->bhqk', q_heads, k_heads)
    raw_weights = jnp.where(allowed[:, None], jnp.exp(scores), 0.0)
    probs = raw_weights / lax.optimization_barrier(jnp.sum(raw_weights, -1, keepdims=True))
    probs_round = lax.optimization_barrier(probs.astype(jnp.bfloat16)).astype(jnp.float32)
    attended = jnp.einsum('bhqk,bkhd->bqhd', probs_round, v_heads).astype(jnp.bfloat16)
    grad_probs = jnp.einsum('bqhd,bkhd->bhqk', g_heads, v_heads)
    grad_v = jnp.einsum('bhqk,bqhd->bkhd', probs_round, g_heads)
    centred = lax.optimization_barrier(jnp.sum(probs * grad_probs, -1, keepdims=True))
    grad_scores = lax.optimization_barrier((probs * (grad_probs - centred)).astype(jnp.bfloat16)).astype(jnp.float32)
    grad_q = jnp.einsum('bhqk,bkhd->bqhd', grad_scores, k_heads)
    grad_k = jnp.einsum('bhqk,bqhd->bkhd', grad_scores, q_heads)
    grad_kv = jnp.concatenate([grad_k.reshape(tiles, 196, width), grad_v.reshape(tiles, 196, width)], -1)
    return (attended.reshape(tiles, 64, width), grad_q.reshape(tiles, 64, width), grad_kv)

def prepare(flat_x, norm_gain, w_qkv, head_scale):
    tokens_here, width = flat_x.shape
    head_count = head_scale.shape[0]
    head_dim = width // head_count
    x_float = flat_x.astype(jnp.float32)
    inv_rms = lax.rsqrt(lax.optimization_barrier(jnp.mean(x_float * x_float, -1, keepdims=True)) + 1e-06)
    normed = (x_float * inv_rms * norm_gain).astype(jnp.bfloat16)
    qkv = jnp.dot(normed, w_qkv, preferred_element_type=jnp.float32)
    q_raw = qkv[:, :width].reshape(tokens_here, head_count, head_dim)
    k_raw = qkv[:, width:2 * width].reshape(tokens_here, head_count, head_dim)
    v_raw = qkv[:, 2 * width:]
    q_norm = lax.rsqrt(lax.optimization_barrier(jnp.sum(q_raw * q_raw, -1, keepdims=True)) + 1e-06)
    k_norm = lax.rsqrt(lax.optimization_barrier(jnp.sum(k_raw * k_raw, -1, keepdims=True)) + 1e-06)
    q_scaled = (q_raw * q_norm * head_scale[:, None]).astype(jnp.bfloat16).reshape(tokens_here, width)
    k_unit = (k_raw * k_norm).astype(jnp.bfloat16).reshape(tokens_here, width)
    kv_pair = jnp.concatenate([k_unit, v_raw.astype(jnp.bfloat16)], 1)
    return (x_float, inv_rms, normed, q_raw, k_raw, q_norm, k_norm, q_scaled, kv_pair)

def finish(flat_x, flat_dy, saved, attended, grad_qs, grad_kv, norm_gain, w_qkv, w_out, head_scale):
    x_float, inv_rms, normed, q_raw, k_raw, q_norm, k_norm = saved
    tokens_here, width = flat_x.shape
    head_count = head_scale.shape[0]
    head_dim = width // head_count
    grad_qs3 = grad_qs.reshape(tokens_here, head_count, head_dim)
    grad_ku3 = grad_kv[:, :width].reshape(tokens_here, head_count, head_dim)
    grad_q = head_scale[:, None] * (q_norm * grad_qs3 - q_raw * q_norm * q_norm * q_norm * lax.optimization_barrier(jnp.sum(q_raw * grad_qs3, -1, keepdims=True)))
    grad_k = k_norm * grad_ku3 - k_raw * k_norm * k_norm * k_norm * lax.optimization_barrier(jnp.sum(k_raw * grad_ku3, -1, keepdims=True))
    grad_act = jnp.concatenate([grad_q.reshape(tokens_here, width), grad_k.reshape(tokens_here, width), grad_kv[:, width:]], 1).astype(jnp.bfloat16)
    grad_normed = jnp.dot(grad_act, w_qkv.T, preferred_element_type=jnp.float32)
    part_qkv = jnp.dot(normed.T, grad_act, preferred_element_type=jnp.float32)
    scaled_grad = grad_normed * norm_gain
    grad_input = (flat_dy.astype(jnp.float32) + inv_rms * scaled_grad - x_float * inv_rms * inv_rms * inv_rms * lax.optimization_barrier(jnp.mean(x_float * scaled_grad, -1, keepdims=True))).astype(jnp.bfloat16)
    mixed = (x_float + jnp.dot(attended, w_out, preferred_element_type=jnp.float32)).astype(jnp.bfloat16)
    part_out = jnp.dot(attended.T, flat_dy, preferred_element_type=jnp.float32)
    return (mixed, grad_input, part_qkv, part_out)

def reference(inputs, cotangent, norm_gain, w_qkv, w_out, head_scale):
    images, grid_rows, grid_cols, width = inputs.shape
    head_count = head_scale.shape[0]
    tokens_image = grid_rows * grid_cols
    col_blocks = grid_cols // 8

    def one_image(sums, pair):
        image_x, image_dy = pair
        flat_x = image_x.reshape(tokens_image, width)
        flat_dy = image_dy.reshape(tokens_image, width)
        prepared = prepare(flat_x, norm_gain, w_qkv, head_scale)
        q_scaled, kv_pair = (prepared[7], prepared[8])
        grad_attn = jnp.dot(flat_dy, w_out.T, preferred_element_type=jnp.float32).astype(jnp.bfloat16)
        q_grid = q_scaled.reshape(grid_rows, grid_cols, width)
        g_grid = grad_attn.reshape(grid_rows, grid_cols, width)
        kv_padded = jnp.pad(kv_pair.reshape(grid_rows, grid_cols, 2 * width), ((3, 3), (3, 3), (0, 0)))
        valid_padded = jnp.pad(jnp.ones((grid_rows, grid_cols, 1), jnp.float32), ((3, 3), (3, 3), (0, 0)))

        def one_band(totals, band):
            start = band * 8
            q_band = lax.dynamic_slice_in_dim(q_grid, start, 8, 0)
            g_band = lax.dynamic_slice_in_dim(g_grid, start, 8, 0)
            kv_band = lax.dynamic_slice_in_dim(kv_padded, start, 14, 0)
            valid_band = lax.dynamic_slice_in_dim(valid_padded, start, 14, 0)
            out_tiles, dq_tiles, dkv_tiles = tile_attention(q_band, g_band, kv_band, valid_band, head_count)
            band_grad = untile_keys(dkv_tiles, 1, col_blocks)
            current = lax.dynamic_slice_in_dim(totals, start, 14, 0)
            totals = lax.dynamic_update_slice_in_dim(totals, current + band_grad, start, 0)
            return (totals, (untile_queries(out_tiles, 1, col_blocks), untile_queries(dq_tiles, 1, col_blocks)))
        start_totals = jnp.zeros((grid_rows + 6, grid_cols + 6, 2 * width), jnp.float32)
        totals, (out_bands, dq_bands) = lax.scan(one_band, start_totals, jnp.arange(grid_rows // 8, dtype=jnp.int32))
        attended = out_bands.reshape(tokens_image, width)
        grad_qs = dq_bands.reshape(tokens_image, width)
        grad_kv = totals[3:grid_rows + 3, 3:grid_cols + 3].reshape(tokens_image, 2 * width)
        mixed, grad_input, part_qkv, part_out = finish(flat_x, flat_dy, prepared[:7], attended, grad_qs, grad_kv, norm_gain, w_qkv, w_out, head_scale)
        new_sums = (sums[0] + part_qkv, sums[1] + part_out)
        return (new_sums, (mixed.reshape(grid_rows, grid_cols, width), grad_input.reshape(grid_rows, grid_cols, width)))
    start_sums = (jnp.zeros((width, 3 * width), jnp.float32), jnp.zeros((width, width), jnp.float32))
    sums, (mixed, grad_input) = lax.scan(one_image, start_sums, (inputs, cotangent))
    factor = 1.0 / math.sqrt(images * grid_rows * grid_cols)
    return (mixed, grad_input, sums[0] * factor, sums[1] * factor)
```

```python
import math

import jax
import jax.numpy as jnp
from jax import lax
from jax.experimental import pallas as pl
from jax.experimental.pallas import tpu as pltpu
from jax.sharding import PartitionSpec as P

F32, BF16 = jnp.float32, jnp.bfloat16


class Links:
    def __init__(self, send, recv):
        self.send, self.recv, self.used, self.all = send, recv, 0, []

    def start(self, src, dst, device):
        copy = pltpu.make_async_remote_copy(
            src_ref=src,
            dst_ref=dst,
            send_sem=self.send.at[self.used],
            recv_sem=self.recv.at[self.used],
            device_id=device,
            device_id_type=pl.DeviceIdType.MESH,
        )
        copy.start()
        self.used += 1
        self.all.append(copy)
        return copy

    def drain(self):
        for copy in self.all:
            copy.wait_send()


class Place:
    def __init__(self):
        gy, gx, self.z = lax.axis_index("gy"), lax.axis_index("gx"), lax.axis_index("img")
        self.gy, self.gx = gy, gx
        self.ngy, self.ngx, self.nz = (lax.axis_size(a) for a in ("gy", "gx", "img"))
        self.nx = self.ngx // 2
        self.ny = self.ngy
        self.core, self.x = gy % 2, gx % self.nx
        self.y = (gy // 2) * 2 + gx // self.nx

    def other_core(self):
        return (self.gy + 1 - 2 * self.core, self.gx, self.z)

    def x_peer(self, k):
        to = (self.x + k) % self.nx
        return to, (self.gy, self.gx - self.x + to, self.z)

    def y_peer(self, k):
        to = (self.y + k) % self.ny
        return to, ((to // 2) * 2 + self.core, (to % 2) * self.nx + self.x, self.z)

    def z_peer(self, k):
        to = (self.z + k) % self.nz
        return to, (self.gy, self.gx, to)

    def reduce_peers(self):
        return (
            [self.other_core()]
            + [self.x_peer(k)[1] for k in range(1, self.nx)]
            + [self.y_peer(k)[1] for k in range(1, self.ny)]
            + [self.z_peer(k)[1] for k in range(1, self.nz)]
        )


def enter(devices):
    barrier = pltpu.get_barrier_semaphore()
    for device in devices:
        pl.semaphore_signal(barrier, inc=1, device_id=device, device_id_type=pl.DeviceIdType.MESH)
    return lambda: pl.semaphore_wait(barrier, len(devices))


def reduce_scratch(nx, ny, nz):
    v = pltpu.VMEM
    return dict(
        r0a=v((ny, nx, 4, 16, 128), BF16),
        r0b=v((ny, 2, 8, 16, 128), BF16),
        s1a=v((ny, nx, 4, 16, 128), BF16),
        s1b=v((ny, 2, 8, 16, 128), BF16),
        rxa=v((nx - 1, ny, 4, 16, 128), BF16),
        s2a=v((ny, 4, 16, 128), BF16),
        rya=v((ny - 1, 4, 16, 128), BF16),
        ta=v((nz, 8, 128), F32),
        rza=v((nz - 1, 8, 128), F32),
        ga=v((nz, 8, 128), F32),
        ryb=v((ny - 1, 8, 16, 128), BF16),
        rzb=v((nz - 1, ny, 16, 128), BF16),
        syb=v((nz, 16, 128), BF16),
        szb=v((ny, 16, 128), BF16),
        r2z=v((nz - 1, 16, 128), BF16),
        r2y=v((ny - 1, 16, 128), BF16),
        ub=v((nx, 8, 128), F32),
        r3x=v((nx - 1, 8, 128), F32),
        gb=v((nz, 8, 128), F32),
    )


def reduce_count(nx, ny, nz):
    return 2 + 2 * (nx - 1) + 3 * (ny - 1) + 5 * (nz - 1)


def core_add(s1, own, got):
    def add(i, _):
        s1[i] = (own[i].astype(F32) + got[i].astype(F32)).astype(BF16)
        return 0

    lax.fori_loop(0, s1.shape[0], add, 0)


def reduce_tail(p, links, b, own_a, own_b, first_a, first_b, factor):
    nx, ny, nz = p.nx, p.ny, p.nz
    first_a.wait_recv()
    core_add(b["s1a"], own_a, b["r0a"])
    xs = []
    for k in range(1, nx):
        to, device = p.x_peer(k)
        xs.append(links.start(b["s1a"].at[:, to], b["rxa"].at[k - 1], device))

    first_b.wait_recv()
    core_add(b["s1b"], own_b, b["r0b"])
    ys, zs = [], []
    for k in range(1, max(ny, nz)):
        if k < ny:
            to, device = p.y_peer(k)
            ys.append(links.start(b["s1b"].at[to, 0], b["ryb"].at[k - 1], device))
        if k < nz:
            to, device = p.z_peer(k)
            zs.append(links.start(b["s1b"].at[:, 1, to], b["rzb"].at[k - 1], device))

    for c in xs:
        c.wait_recv()

    def add_x(i, _):
        total = b["s1a"][i, p.x].astype(F32)
        for k in range(nx - 1):
            total += b["rxa"][k, i].astype(F32)
        b["s2a"][i] = total.astype(BF16)
        return 0

    lax.fori_loop(0, ny, add_x, 0)
    y2 = []
    for k in range(1, ny):
        to, device = p.y_peer(k)
        y2.append(links.start(b["s2a"].at[to], b["rya"].at[k - 1], device))

    for c in ys:
        c.wait_recv()

    def add_y(i, _):
        total = b["s1b"][p.y, 0, i].astype(F32)
        for k in range(ny - 1):
            total += b["ryb"][k, i].astype(F32)
        b["syb"][i] = total.astype(BF16)
        return 0

    lax.fori_loop(0, nz, add_y, 0)
    z3 = []
    for k in range(1, nz):
        to, device = p.z_peer(k)
        z3.append(links.start(b["syb"].at[to], b["r2z"].at[k - 1], device))

    for c in zs:
        c.wait_recv()

    def add_z(i, _):
        total = b["s1b"][i, 1, p.z].astype(F32)
        for k in range(nz - 1):
            total += b["rzb"][k, i].astype(F32)
        b["szb"][i] = total.astype(BF16)
        return 0

    lax.fori_loop(0, ny, add_z, 0)
    y3 = []
    for k in range(1, ny):
        to, device = p.y_peer(k)
        y3.append(links.start(b["szb"].at[to], b["r2y"].at[k - 1], device))

    for c in y2:
        c.wait_recv()
    total = b["s2a"][p.y].astype(F32)
    for k in range(ny - 1):
        total += b["rya"][k].astype(F32)
    b["ta"][0:4] = total[:, 0:8]
    b["ta"][4:8] = total[:, 8:16]
    z2 = []
    for k in range(1, nz):
        to, device = p.z_peer(k)
        z2.append(links.start(b["ta"].at[to], b["rza"].at[k - 1], device))

    for c in z3:
        c.wait_recv()
    low = b["syb"][p.z].astype(F32)
    for k in range(nz - 1):
        low += b["r2z"][k].astype(F32)
    for c in y3:
        c.wait_recv()
    high = b["szb"][p.y].astype(F32)
    for k in range(ny - 1):
        high += b["r2y"][k].astype(F32)
    b["ub"][0] = low[0:8]
    b["ub"][1] = low[8:16]
    b["ub"][2] = high[0:8]
    b["ub"][3] = high[8:16]
    x3 = []
    for k in range(1, nx):
        to, device = p.x_peer(k)
        x3.append(links.start(b["ub"].at[to], b["r3x"].at[k - 1], device))

    for c in z2:
        c.wait_recv()
    total = b["ta"][p.z]
    for k in range(nz - 1):
        total += b["rza"][k]
    b["ga"][p.z] = total * factor
    last = []
    for k in range(1, nz):
        to, device = p.z_peer(k)
        last.append(links.start(b["ga"].at[p.z], b["ga"].at[p.z], device))

    for c in x3:
        c.wait_recv()
    total = b["ub"][p.x]
    for k in range(nx - 1):
        total += b["r3x"][k]
    b["gb"][p.z] = total * factor
    for k in range(1, nz):
        to, device = p.z_peer(k)
        last.append(links.start(b["gb"].at[p.z], b["gb"].at[p.z], device))
    for c in last:
        c.wait_recv()


def write_rows(b, qkv_ref, out_ref):
    for t in range(4):
        lanes = slice(t * 128, t * 128 + 128)
        qkv_ref[:, lanes] = b["ga"][t]
        out_ref[:, lanes] = b["ga"][4 + t]
    for t in range(8):
        qkv_ref[:, 512 + t * 128 : 640 + t * 128] = b["gb"][t]


def reduce_call(part_a, part_b, factor):
    nx, ny, nz = lax.axis_size("gx") // 2, lax.axis_size("gy"), lax.axis_size("img")
    scratch = reduce_scratch(nx, ny, nz)
    names = list(scratch)
    count = reduce_count(nx, ny, nz)

    def kernel(a_ref, b_ref, qkv_ref, out_ref, *rest):
        b = dict(zip(names, rest))
        links = Links(*rest[len(names) :])
        p = Place()
        wait = enter(p.reduce_peers())
        wait()
        first_a = links.start(a_ref.at[1 - p.core], b["r0a"], p.other_core())
        first_b = links.start(b_ref.at[1 - p.core], b["r0b"], p.other_core())
        reduce_tail(p, links, b, a_ref.at[p.core], b_ref.at[p.core], first_a, first_b, factor)
        write_rows(b, qkv_ref, out_ref)
        links.drain()

    vm = pl.BlockSpec(memory_space=pltpu.VMEM)
    return pl.pallas_call(
        kernel,
        out_shape=(jax.ShapeDtypeStruct((8, 1536), F32), jax.ShapeDtypeStruct((8, 512), F32)),
        in_specs=[vm, vm],
        out_specs=(vm, vm),
        scratch_shapes=[scratch[n] for n in names]
        + [pltpu.SemaphoreType.DMA((count,)), pltpu.SemaphoreType.DMA((count,))],
        compiler_params=pltpu.CompilerParams(
            collective_id=1, has_side_effects=True, vmem_limit_bytes=48 * 1024 * 1024
        ),
        cost_estimate=pl.CostEstimate(flops=10**7, bytes_accessed=4 * 10**6, transcendentals=0),
        name="reduce",
    )(part_a, part_b)


def fold_parts(part_qkv, part_out):
    ny, nx = lax.axis_size("gy"), lax.axis_size("gx") // 2
    split = lambda a: a.reshape(ny // 2, 2, 2, nx, 8, a.shape[-1]).transpose(1, 0, 2, 3, 4, 5)
    both = jnp.concatenate([split(part_qkv[:, :512]), split(part_out)], axis=4)
    part_a = both.reshape(2, ny, nx, 16, 4, 128).swapaxes(3, 4).astype(BF16)
    rest = split(part_qkv[:, 512:]).reshape(2, ny, nx // 2, 16, 8, 128)
    return (part_a, rest.swapaxes(3, 4).astype(BF16))


def padded_2(x, sides, width):
    for axis, dim in sides:
        peers, length = (lax.axis_size(axis), x.shape[dim])
        up = [(i, (i + 1) % peers) for i in range(peers - 1)]
        down = [(j, i) for i, j in up]
        last = lax.slice_in_dim(x, length - width, length, axis=dim)
        first = lax.slice_in_dim(x, 0, width, axis=dim)
        before = lax.ppermute(last, axis, up)
        after = lax.ppermute(first, axis, down)
        x = jnp.concatenate([before, x, after], axis=dim)
    return x


def windows(values, axis_at):
    length = values.shape[axis_at] - 6
    blocks = length // 8
    widths = [(0, 0)] * values.ndim
    widths[axis_at] = (0, 2)
    padded = jnp.pad(values, widths)
    split_shape = values.shape[:axis_at] + (blocks, 8) + values.shape[axis_at + 1 :]
    leading = lax.slice_in_dim(padded, 0, length, axis=axis_at).reshape(split_shape)
    trailing = lax.slice_in_dim(padded, 8, length + 8, axis=axis_at).reshape(split_shape)
    trailing = lax.slice_in_dim(trailing, 0, 6, axis=axis_at + 1)
    return jnp.concatenate([leading, trailing], axis=axis_at + 1)


def unwindows(gradient, axis_at):
    blocks = gradient.shape[axis_at]
    length = blocks * 8
    merged = gradient.shape[:axis_at] + (length,) + gradient.shape[axis_at + 2 :]
    leading = lax.slice_in_dim(gradient, 0, 8, axis=axis_at + 1).reshape(merged)
    widths = [(0, 0)] * gradient.ndim
    widths[axis_at + 1] = (0, 2)
    trailing = jnp.pad(lax.slice_in_dim(gradient, 8, 14, axis=axis_at + 1), widths).reshape(merged)
    front_pad = [(0, 0)] * len(merged)
    front_pad[axis_at] = (0, 8)
    back_pad = [(0, 0)] * len(merged)
    back_pad[axis_at] = (8, 0)
    summed = jnp.pad(leading, front_pad) + jnp.pad(trailing, back_pad)
    return lax.slice_in_dim(summed, 0, length + 6, axis=axis_at)


def key_tiles(extended):
    both_win = windows(windows(extended, 0), 2)
    return both_win.transpose(0, 2, 1, 3, 4).reshape(-1, 196, extended.shape[-1])


def untile_keys(tiled, row_blocks, col_blocks):
    stacked = tiled.reshape(row_blocks, col_blocks, 14, 14, tiled.shape[-1]).transpose(
        0, 2, 1, 3, 4
    )
    return unwindows(unwindows(stacked, 2), 0)


def query_tiles(values):
    tile_rows, tile_cols, feats = values.shape
    shaped = values.reshape(tile_rows // 8, 8, tile_cols // 8, 8, feats)
    return shaped.transpose(0, 2, 1, 3, 4).reshape(-1, 64, feats)


def untile_queries(tiled, row_blocks, col_blocks):
    feats = tiled.shape[-1]
    shaped = tiled.reshape(row_blocks, col_blocks, 8, 8, feats).transpose(0, 2, 1, 3, 4)
    return shaped.reshape(row_blocks * 8, col_blocks * 8, feats)


def local_mask():
    query_ids = jnp.arange(64, dtype=jnp.int32)
    key_ids = jnp.arange(196, dtype=jnp.int32)
    row_gap = key_ids[None, :] // 14 - 3 - query_ids[:, None] // 8
    col_gap = key_ids[None, :] % 14 - 3 - query_ids[:, None] % 8
    return (jnp.abs(row_gap) <= 3) & (jnp.abs(col_gap) <= 3)


def tile_attention(queries, grad_attn, kv_ext, valid_ext, head_count):
    width = queries.shape[-1]
    head_dim = width // head_count
    q_tiles = query_tiles(queries)
    tiles = q_tiles.shape[0]
    q_heads = q_tiles.reshape(tiles, 64, head_count, head_dim)
    g_heads = query_tiles(grad_attn).reshape(tiles, 64, head_count, head_dim)
    keyed = key_tiles(kv_ext)
    k_heads = keyed[..., :width].reshape(tiles, 196, head_count, head_dim)
    v_heads = keyed[..., width:].reshape(tiles, 196, head_count, head_dim)
    allowed = local_mask()[None] & (key_tiles(valid_ext)[:, None, :, 0] > 0.5)
    scores = jnp.einsum("bqhd,bkhd->bhqk", q_heads, k_heads, preferred_element_type=jnp.float32)
    raw_weights = jnp.where(allowed[:, None], jnp.exp(scores), 0.0)
    probs = raw_weights / jnp.sum(raw_weights, -1, keepdims=True)
    probs_round = probs.astype(jnp.bfloat16)
    attended = jnp.einsum(
        "bhqk,bkhd->bqhd", probs_round, v_heads, preferred_element_type=jnp.float32
    ).astype(jnp.bfloat16)
    grad_probs = jnp.einsum("bqhd,bkhd->bhqk", g_heads, v_heads, preferred_element_type=jnp.float32)
    grad_v = jnp.einsum("bhqk,bqhd->bkhd", probs_round, g_heads, preferred_element_type=jnp.float32)
    centred = jnp.sum(probs * grad_probs, -1, keepdims=True)
    grad_scores = (probs * (grad_probs - centred)).astype(jnp.bfloat16)
    grad_q = jnp.einsum("bhqk,bkhd->bqhd", grad_scores, k_heads, preferred_element_type=jnp.float32)
    grad_k = jnp.einsum("bhqk,bqhd->bkhd", grad_scores, q_heads, preferred_element_type=jnp.float32)
    grad_kv = jnp.concatenate(
        [grad_k.reshape(tiles, 196, width), grad_v.reshape(tiles, 196, width)], -1
    )
    return (attended.reshape(tiles, 64, width), grad_q.reshape(tiles, 64, width), grad_kv)


def prepare(flat_x, norm_gain, w_qkv, head_scale):
    tokens_here, width = flat_x.shape
    head_count = head_scale.shape[0]
    head_dim = width // head_count
    x_float = flat_x.astype(jnp.float32)
    inv_rms = lax.rsqrt(jnp.mean(x_float * x_float, -1, keepdims=True) + 1e-06)
    normed = (x_float * inv_rms * norm_gain).astype(jnp.bfloat16)
    qkv = jnp.dot(normed, w_qkv, preferred_element_type=jnp.float32)
    q_raw = qkv[:, :width].reshape(tokens_here, head_count, head_dim)
    k_raw = qkv[:, width : 2 * width].reshape(tokens_here, head_count, head_dim)
    v_raw = qkv[:, 2 * width :]
    q_norm = lax.rsqrt(jnp.sum(q_raw * q_raw, -1, keepdims=True) + 1e-06)
    k_norm = lax.rsqrt(jnp.sum(k_raw * k_raw, -1, keepdims=True) + 1e-06)
    q_scaled = (
        (q_raw * q_norm * head_scale[:, None]).astype(jnp.bfloat16).reshape(tokens_here, width)
    )
    k_unit = (k_raw * k_norm).astype(jnp.bfloat16).reshape(tokens_here, width)
    kv_pair = jnp.concatenate([k_unit, v_raw.astype(jnp.bfloat16)], 1)
    return (x_float, inv_rms, normed, q_raw, k_raw, q_norm, k_norm, q_scaled, kv_pair)


def finish(flat_x, flat_dy, saved, attended, grad_qs, grad_kv, norm_gain, w_qkv, w_out, head_scale):
    x_float, inv_rms, normed, q_raw, k_raw, q_norm, k_norm = saved
    tokens_here, width = flat_x.shape
    head_count = head_scale.shape[0]
    head_dim = width // head_count
    grad_qs3 = grad_qs.reshape(tokens_here, head_count, head_dim)
    grad_ku3 = grad_kv[:, :width].reshape(tokens_here, head_count, head_dim)
    grad_q = head_scale[:, None] * (
        q_norm * grad_qs3
        - q_raw * q_norm * q_norm * q_norm * jnp.sum(q_raw * grad_qs3, -1, keepdims=True)
    )
    grad_k = k_norm * grad_ku3 - k_raw * k_norm * k_norm * k_norm * jnp.sum(
        k_raw * grad_ku3, -1, keepdims=True
    )
    grad_act = jnp.concatenate(
        [
            grad_q.reshape(tokens_here, width),
            grad_k.reshape(tokens_here, width),
            grad_kv[:, width:],
        ],
        1,
    ).astype(jnp.bfloat16)
    grad_normed = jnp.dot(grad_act, w_qkv.T, preferred_element_type=jnp.float32)
    part_qkv = jnp.dot(normed.T, grad_act, preferred_element_type=jnp.float32)
    scaled_grad = grad_normed * norm_gain
    grad_input = (
        flat_dy.astype(jnp.float32)
        + inv_rms * scaled_grad
        - x_float * inv_rms * inv_rms * inv_rms * jnp.mean(x_float * scaled_grad, -1, keepdims=True)
    ).astype(jnp.bfloat16)
    mixed = (x_float + jnp.dot(attended, w_out, preferred_element_type=jnp.float32)).astype(
        jnp.bfloat16
    )
    part_out = jnp.dot(attended.T, flat_dy, preferred_element_type=jnp.float32)
    return (mixed, grad_input, part_qkv, part_out)


def per_device(inputs, cotangent, norm_gain, w_qkv, w_out, head_scale):
    tile_rows, tile_cols, width = (inputs.shape[1], inputs.shape[2], inputs.shape[3])
    head_count = head_scale.shape[0]
    tokens_here = tile_rows * tile_cols
    row_blocks = tile_rows // 8
    col_blocks = tile_cols // 8
    flat_x = inputs.reshape(tokens_here, width)
    flat_dy = cotangent.reshape(tokens_here, width)
    prepared = prepare(flat_x, norm_gain, w_qkv, head_scale)
    q_scaled, kv_pair = (prepared[7], prepared[8])
    kv_grid = kv_pair.reshape(tile_rows, tile_cols, 2 * width)
    kv_ext = padded_2(kv_grid, (("gy", 0), ("gx", 1)), 3)
    grad_attn = jnp.dot(flat_dy, w_out.T, preferred_element_type=jnp.float32).astype(jnp.bfloat16)
    row_ids = lax.axis_index("gy") * tile_rows + jnp.arange(tile_rows + 6, dtype=jnp.int32) - 3
    col_ids = lax.axis_index("gx") * tile_cols + jnp.arange(tile_cols + 6, dtype=jnp.int32) - 3
    row_inside = (row_ids >= 0) & (row_ids < tile_rows * lax.axis_size("gy"))
    col_inside = (col_ids >= 0) & (col_ids < tile_cols * lax.axis_size("gx"))
    valid_ext = (row_inside[:, None] & col_inside[None, :]).astype(jnp.float32)[:, :, None]
    out_tiles, dq_tiles, dkv_tiles = tile_attention(
        q_scaled.reshape(tile_rows, tile_cols, width),
        grad_attn.reshape(tile_rows, tile_cols, width),
        kv_ext,
        valid_ext,
        head_count,
    )
    attended = untile_queries(out_tiles, row_blocks, col_blocks).reshape(tokens_here, width)
    grad_qs = untile_queries(dq_tiles, row_blocks, col_blocks).reshape(tokens_here, width)
    grad_ext = untile_keys(dkv_tiles, row_blocks, col_blocks)
    col_sides = jnp.concatenate([grad_ext[:, :3], grad_ext[:, tile_cols + 3 :]], axis=1)
    from_cols = padded_2(col_sides.astype(jnp.bfloat16), (("gx", 1),), 3).astype(col_sides.dtype)
    inner = grad_ext[:, 3 : tile_cols + 3]
    inner = inner.at[:, :3].add(from_cols[:, :3]).at[:, tile_cols - 3 :].add(from_cols[:, 9:])
    row_sides = jnp.concatenate([inner[:3], inner[tile_rows + 3 :]], axis=0)
    from_rows = padded_2(row_sides.astype(jnp.bfloat16), (("gy", 0),), 3).astype(row_sides.dtype)
    middle = inner[3 : tile_rows + 3]
    middle = middle.at[:3].add(from_rows[:3]).at[tile_rows - 3 :].add(from_rows[9:])
    grad_kv = middle.reshape(tokens_here, 2 * width)
    mixed, grad_input, part_qkv, part_out = finish(
        flat_x,
        flat_dy,
        prepared[:7],
        attended,
        grad_qs,
        grad_kv,
        norm_gain,
        w_qkv,
        w_out,
        head_scale,
    )
    factor = 1.0 / math.sqrt(
        lax.axis_size("img") * lax.axis_size("gy") * tile_rows * lax.axis_size("gx") * tile_cols
    )
    mine_qkv, mine_out = reduce_call(*fold_parts(part_qkv, part_out), factor)
    shape_out = (1, tile_rows, tile_cols, width)
    return (
        mixed.reshape(shape_out),
        grad_input.reshape(shape_out),
        mine_qkv,
        mine_out,
    )


def solution(mesh):
    in_specs = (P("img", "gy", "gx", None), P("img", "gy", "gx", None), P(), P(), P(), P())
    out_specs = (
        P("img", "gy", "gx", None),
        P("img", "gy", "gx", None),
        P(("gy", "gx"), None),
        P(("gy", "gx"), None),
    )
    return jax.shard_map(
        per_device, mesh=mesh, in_specs=in_specs, out_specs=out_specs, check_vma=False
    )
```

```python
import math

import jax
import jax.numpy as jnp
from jax import lax
from jax.experimental import pallas as pl
from jax.experimental.pallas import tpu as pltpu
from jax.sharding import PartitionSpec as P

F32, BF16 = jnp.float32, jnp.bfloat16


class Links:
    def __init__(self, send, recv):
        self.send, self.recv, self.used, self.all = send, recv, 0, []

    def start(self, src, dst, device):
        copy = pltpu.make_async_remote_copy(
            src_ref=src,
            dst_ref=dst,
            send_sem=self.send.at[self.used],
            recv_sem=self.recv.at[self.used],
            device_id=device,
            device_id_type=pl.DeviceIdType.MESH,
        )
        copy.start()
        self.used += 1
        self.all.append(copy)
        return copy

    def drain(self):
        for copy in self.all:
            copy.wait_send()


class Place:
    def __init__(self):
        gy, gx, self.z = lax.axis_index("gy"), lax.axis_index("gx"), lax.axis_index("img")
        self.gy, self.gx = gy, gx
        self.ngy, self.ngx, self.nz = (lax.axis_size(a) for a in ("gy", "gx", "img"))
        self.nx = self.ngx // 2
        self.ny = self.ngy
        self.core, self.x = gy % 2, gx % self.nx
        self.y = (gy // 2) * 2 + gx // self.nx

    def other_core(self):
        return (self.gy + 1 - 2 * self.core, self.gx, self.z)

    def x_peer(self, k):
        to = (self.x + k) % self.nx
        return to, (self.gy, self.gx - self.x + to, self.z)

    def y_peer(self, k):
        to = (self.y + k) % self.ny
        return to, ((to // 2) * 2 + self.core, (to % 2) * self.nx + self.x, self.z)

    def z_peer(self, k):
        to = (self.z + k) % self.nz
        return to, (self.gy, self.gx, to)

    def reduce_peers(self):
        return (
            [self.other_core()]
            + [self.x_peer(k)[1] for k in range(1, self.nx)]
            + [self.y_peer(k)[1] for k in range(1, self.ny)]
            + [self.z_peer(k)[1] for k in range(1, self.nz)]
        )


def enter(devices):
    barrier = pltpu.get_barrier_semaphore()
    for device in devices:
        pl.semaphore_signal(barrier, inc=1, device_id=device, device_id_type=pl.DeviceIdType.MESH)
    return lambda: pl.semaphore_wait(barrier, len(devices))


def reduce_scratch(nx, ny, nz):
    v = pltpu.VMEM
    return dict(
        r0a=v((ny, nx, 4, 16, 128), BF16),
        r0b=v((ny, 2, 8, 16, 128), BF16),
        s1a=v((ny, nx, 4, 16, 128), BF16),
        s1b=v((ny, 2, 8, 16, 128), BF16),
        rxa=v((nx - 1, ny, 4, 16, 128), BF16),
        s2a=v((ny, 4, 16, 128), BF16),
        rya=v((ny - 1, 4, 16, 128), BF16),
        ta=v((nz, 8, 128), F32),
        rza=v((nz - 1, 8, 128), F32),
        ga=v((nz, 8, 128), F32),
        ryb=v((ny - 1, 8, 16, 128), BF16),
        rzb=v((nz - 1, ny, 16, 128), BF16),
        syb=v((nz, 16, 128), BF16),
        szb=v((ny, 16, 128), BF16),
        r2z=v((nz - 1, 16, 128), BF16),
        r2y=v((ny - 1, 16, 128), BF16),
        ub=v((nx, 8, 128), F32),
        r3x=v((nx - 1, 8, 128), F32),
        gb=v((nz, 8, 128), F32),
    )


def reduce_count(nx, ny, nz):
    return 2 + 2 * (nx - 1) + 3 * (ny - 1) + 5 * (nz - 1)


def core_add(s1, own, got):
    def add(i, _):
        s1[i] = (own[i].astype(F32) + got[i].astype(F32)).astype(BF16)
        return 0

    lax.fori_loop(0, s1.shape[0], add, 0)


def start_a(p, links, b, first_a):
    first_a.wait_recv()
    core_add(b["s1a"], b["own_a"], b["r0a"])
    xs = []
    for k in range(1, p.nx):
        to, device = p.x_peer(k)
        xs.append(links.start(b["s1a"].at[:, to], b["rxa"].at[k - 1], device))
    return xs


def reduce_tail(p, links, b, first_b, xs, finish, factor):
    nx, ny, nz = p.nx, p.ny, p.nz
    first_b.wait_recv()
    core_add(b["s1b"], b["own_b"], b["r0b"])
    ys, zs = [], []
    for k in range(1, max(ny, nz)):
        if k < ny:
            to, device = p.y_peer(k)
            ys.append(links.start(b["s1b"].at[to, 0], b["ryb"].at[k - 1], device))
        if k < nz:
            to, device = p.z_peer(k)
            zs.append(links.start(b["s1b"].at[:, 1, to], b["rzb"].at[k - 1], device))
    finish()

    for c in xs:
        c.wait_recv()

    def add_x(i, _):
        total = b["s1a"][i, p.x].astype(F32)
        for k in range(nx - 1):
            total += b["rxa"][k, i].astype(F32)
        b["s2a"][i] = total.astype(BF16)
        return 0

    lax.fori_loop(0, ny, add_x, 0)
    y2 = []
    for k in range(1, ny):
        to, device = p.y_peer(k)
        y2.append(links.start(b["s2a"].at[to], b["rya"].at[k - 1], device))

    for c in ys:
        c.wait_recv()

    def add_y(i, _):
        total = b["s1b"][p.y, 0, i].astype(F32)
        for k in range(ny - 1):
            total += b["ryb"][k, i].astype(F32)
        b["syb"][i] = total.astype(BF16)
        return 0

    lax.fori_loop(0, nz, add_y, 0)
    z3 = []
    for k in range(1, nz):
        to, device = p.z_peer(k)
        z3.append(links.start(b["syb"].at[to], b["r2z"].at[k - 1], device))

    for c in zs:
        c.wait_recv()

    def add_z(i, _):
        total = b["s1b"][i, 1, p.z].astype(F32)
        for k in range(nz - 1):
            total += b["rzb"][k, i].astype(F32)
        b["szb"][i] = total.astype(BF16)
        return 0

    lax.fori_loop(0, ny, add_z, 0)
    y3 = []
    for k in range(1, ny):
        to, device = p.y_peer(k)
        y3.append(links.start(b["szb"].at[to], b["r2y"].at[k - 1], device))

    for c in y2:
        c.wait_recv()
    total = b["s2a"][p.y].astype(F32)
    for k in range(ny - 1):
        total += b["rya"][k].astype(F32)
    b["ta"][0:4] = total[:, 0:8]
    b["ta"][4:8] = total[:, 8:16]
    z2 = []
    for k in range(1, nz):
        to, device = p.z_peer(k)
        z2.append(links.start(b["ta"].at[to], b["rza"].at[k - 1], device))

    for c in z3:
        c.wait_recv()
    low = b["syb"][p.z].astype(F32)
    for k in range(nz - 1):
        low += b["r2z"][k].astype(F32)
    for c in y3:
        c.wait_recv()
    high = b["szb"][p.y].astype(F32)
    for k in range(ny - 1):
        high += b["r2y"][k].astype(F32)
    b["ub"][0] = low[0:8]
    b["ub"][1] = low[8:16]
    b["ub"][2] = high[0:8]
    b["ub"][3] = high[8:16]
    x3 = []
    for k in range(1, nx):
        to, device = p.x_peer(k)
        x3.append(links.start(b["ub"].at[to], b["r3x"].at[k - 1], device))

    for c in z2:
        c.wait_recv()
    total = b["ta"][p.z]
    for k in range(nz - 1):
        total += b["rza"][k]
    b["ga"][p.z] = total * factor
    last = []
    for k in range(1, nz):
        to, device = p.z_peer(k)
        last.append(links.start(b["ga"].at[p.z], b["ga"].at[p.z], device))

    for c in x3:
        c.wait_recv()
    total = b["ub"][p.x]
    for k in range(nx - 1):
        total += b["r3x"][k]
    b["gb"][p.z] = total * factor
    for k in range(1, nz):
        to, device = p.z_peer(k)
        last.append(links.start(b["gb"].at[p.z], b["gb"].at[p.z], device))
    for c in last:
        c.wait_recv()


def write_rows(b, qkv_ref, out_ref):
    for t in range(4):
        lanes = slice(t * 128, t * 128 + 128)
        qkv_ref[:, lanes] = b["ga"][t]
        out_ref[:, lanes] = b["ga"][4 + t]
    for t in range(8):
        qkv_ref[:, 512 + t * 128 : 640 + t * 128] = b["gb"][t]


def dot(a, b, dims=((1,), (0,))):
    return lax.dot_general(a, b, (dims, ((), ())), preferred_element_type=F32)


TURN = ((1,), (1,))
FIRST = ((0,), (0,))


def iota(shape, dim):
    return lax.broadcasted_iota(jnp.int32, shape, dim)


def edge_tokens(j):
    side = j & 31
    side_token = jnp.where((side >> 3) < 3, (side & 7) * 16 + (side >> 3) + 13 * ((j >> 5) & 1), -1)
    corner = (j - 64) >> 4
    down, across = (j >> 2) & 3, j & 3
    token = (down + 5 * (corner >> 1)) * 16 + across + 13 * (corner & 1)
    corner_token = jnp.where((down < 3) & (across < 3), token, -1)
    return jnp.where(j < 64, side_token, corner_token)


def halo_place(j):
    row = jnp.where(j < 48, (j >> 4) - 3, (j >> 4) + 5)
    col = j & 15
    side = j & 31
    is_side = (j >= 96) & (j < 160)
    row = jnp.where(is_side, side & 7, row)
    col = jnp.where(is_side, (side >> 3) + jnp.where(j < 128, -3, 16), col)
    corner = (j - 160) >> 4
    down, across = (j >> 2) & 3, j & 3
    is_corner = j >= 160
    row = jnp.where(is_corner, down + jnp.where(corner < 2, -3, 8), row)
    col = jnp.where(is_corner, across + jnp.where((corner & 1) == 0, -3, 16), col)
    filled = jnp.where(is_side, side >> 3, jnp.where(is_corner, jnp.maximum(down, across), 0))
    return row, col, filled < 3


def near(row, col, shape):
    query = iota(shape, 1)
    return (jnp.abs(row - (query >> 4)) <= 3) & (jnp.abs(col - (query & 15)) <= 3)


def twice(a):
    return jnp.concatenate([a, a], axis=1)


def head_sum(a, ones):
    top = a.astype(BF16)
    rest = (a - top.astype(F32)).astype(BF16)
    return dot(top, ones) + dot(rest, ones)


def pick(a):
    return jnp.concatenate([a[0:64, 0:128], a[64:128, 128:256]], axis=0)


BLOCKS = (
    (0, 48, 48, -1, 0),
    (48, 48, 0, 1, 0),
    (96, 32, 128, 0, -1),
    (128, 32, 96, 0, 1),
    (160, 16, 208, -1, -1),
    (176, 16, 192, -1, 1),
    (192, 16, 176, 1, -1),
    (208, 16, 160, 1, 1),
)


def block_call(x, dy, gain, w_qkv, w_out, head_scale, factor):
    nx, ny, nz = lax.axis_size("gx") // 2, lax.axis_size("gy"), lax.axis_size("img")
    v = pltpu.VMEM
    scratch = reduce_scratch(nx, ny, nz)
    scratch.update(
        own_a=v((ny, nx, 4, 16, 128), F32),
        own_b=v((ny, 2, 8, 16, 128), F32),
        s0a=v((ny, nx, 4, 16, 128), BF16),
        s0b=v((ny, 2, 8, 16, 128), BF16),
        normed=v((128, 512), BF16),
        normed_t=v((ny // 2, 2, 64, 128), BF16),
        uq=v((128, 512), F32),
        uk=v((128, 512), F32),
        nq=v((128, 512), F32),
        nk=v((128, 512), F32),
        kv=v((128, 1024), BF16),
        packed=v((128, 1024), BF16),
        halo=v((224, 1024), BF16),
        qm=v((4, 256, 128), BF16),
        gm=v((4, 256, 128), BF16),
        mask=v((128, 128), F32),
        mask_h=v((224, 128), F32),
        e_l=v((4, 128, 256), F32),
        d_l=v((4, 128, 256), F32),
        p_h=v((4, 224, 256), BF16),
        ds_h=v((4, 224, 256), BF16),
        gsend=v((224, 1024), BF16),
        grecv=v((224, 1024), BF16),
        gkv=v((128, 1024), F32),
        att=v((128, 512), BF16),
        att_t=v((ny // 2, 2, 64, 128), BF16),
        act=v((128, 1536), BF16),
        gn=v((128, 512), F32),
        inv=v((128, 128), F32),
    )
    names = list(scratch)
    count = reduce_count(nx, ny, nz) + 16

    def kernel(x_ref, dy_ref, gain_ref, wqkv_ref, wout_ref, scale_ref, mixed_ref, gin_ref, gqkv_ref, gout_ref, *rest):
        b = dict(zip(names, rest))
        links = Links(*rest[len(names) :])
        p = Place()

        def neighbour(dy_step, dx_step):
            return ((p.gy + dy_step) % p.ngy, (p.gx + dx_step) % p.ngx, p.z)

        arrive = enter(p.reduce_peers() + [neighbour(*block[3:]) for block in BLOCKS])

        def exchange(source, target):
            return [
                links.start(source(start, size), target.at[land : land + size], neighbour(*step))
                for start, size, land, *step in BLOCKS
            ]

        low = iota((128, 128), 1) < 64
        ones = jnp.where((iota((128, 128), 0) < 64) == low, 1.0, 0.0).astype(BF16)

        def masked(a):
            zero = jnp.zeros_like(a)
            return jnp.concatenate([jnp.where(low, a, zero), jnp.where(low, zero, a)], axis=0).astype(BF16)

        xf = x_ref[...].astype(F32)
        inv_rms = lax.rsqrt(jnp.sum(xf * xf, -1, keepdims=True) * (1.0 / 512) + 1e-6)
        b["inv"][...] = jnp.broadcast_to(inv_rms, (128, 128))
        normed_f = xf * inv_rms * gain_ref[...]
        normed = normed_f.astype(BF16)
        b["normed"][...] = normed
        for i in range(4):
            lanes = slice(i * 128, i * 128 + 128)
            k_raw = dot(normed, wqkv_ref[:, 512 + i * 128 : 640 + i * 128])
            nk = lax.rsqrt(head_sum(k_raw * k_raw, ones) + 1e-6)
            uk = k_raw * nk
            b["nk"][:, lanes] = nk
            b["uk"][:, lanes] = uk
            b["kv"][:, lanes] = uk.astype(BF16)
        b["kv"][:, 512:1024] = dot(normed, wqkv_ref[:, 1024:1536]).astype(BF16)
        choose = jnp.where(edge_tokens(iota((128, 128), 0)) == iota((128, 128), 1), 1.0, 0.0)
        b["packed"][...] = dot(choose.astype(BF16), b["kv"][...]).astype(BF16)
        arrive()

        def key_block(start, size):
            if start == 0:
                return b["kv"].at[0:48]
            if start == 48:
                return b["kv"].at[80:128]
            return b["packed"].at[start - 96 : start - 96 + size]

        keys = exchange(key_block, b["halo"])

        for i in range(4):
            lanes = slice(i * 128, i * 128 + 128)
            q_raw = dot(normed, wqkv_ref[:, lanes])
            nq = lax.rsqrt(head_sum(q_raw * q_raw, ones) + 1e-6)
            uq = q_raw * nq
            scale = jnp.where(low, scale_ref[2 * i], scale_ref[2 * i + 1])
            b["nq"][:, lanes] = nq * scale
            b["uq"][:, lanes] = uq
            b["qm"][i] = masked(uq * scale)
            b["gm"][i] = masked(dot(dy_ref[...], wout_ref[lanes, :], TURN))

        token = iota((128, 128), 0)
        b["mask"][...] = jnp.where(near(token >> 4, token & 15, (128, 128)), 1.0, 0.0)
        row, col, there = halo_place(iota((224, 128), 0))
        all_row, all_col = row + p.gy * 8, col + p.gx * 16
        there = there & (all_row >= 0) & (all_row < 8 * p.ngy) & (all_col >= 0) & (all_col < 16 * p.ngx)
        b["mask_h"][...] = jnp.where(there & near(row, col, (224, 128)), 1.0, 0.0)
        sums, mids = [], []
        for i in range(4):
            lanes, more = slice(i * 128, i * 128 + 128), slice(512 + i * 128, 640 + i * 128)
            e = jnp.exp(dot(b["kv"][:, lanes], b["qm"][i], TURN)) * twice(b["mask"][...])
            d = dot(b["kv"][:, more], b["gm"][i], TURN)
            b["e_l"][i] = e
            b["d_l"][i] = d
            sums.append(jnp.sum(e, 0, keepdims=True))
            mids.append(jnp.sum(e * d, 0, keepdims=True))
        for i in range(4):
            lanes = slice(i * 128, i * 128 + 128)
            b["normed_t"][i] = b["normed"][:, lanes].astype(F32).T.astype(BF16).reshape(2, 64, 128)
        for c in keys:
            c.wait_recv()

        for i in range(4):
            lanes, more = slice(i * 128, i * 128 + 128), slice(512 + i * 128, 640 + i * 128)
            e = jnp.exp(dot(b["halo"][:, lanes], b["qm"][i], TURN)) * twice(b["mask_h"][...])
            d = dot(b["halo"][:, more], b["gm"][i], TURN)
            inverse = 1.0 / (sums[i] + jnp.sum(e, 0, keepdims=True))
            mids[i] = (mids[i] + jnp.sum(e * d, 0, keepdims=True)) * inverse
            sums[i] = inverse
            probs = e * inverse
            ds = (probs * (d - mids[i])).astype(BF16)
            probs = probs.astype(BF16)
            b["p_h"][i] = probs
            b["ds_h"][i] = ds
            b["gsend"][:, lanes] = dot(ds, b["qm"][i]).astype(BF16)
            b["gsend"][:, more] = dot(probs, b["gm"][i]).astype(BF16)
        grads = exchange(lambda start, size: b["gsend"].at[start : start + size], b["grecv"])

        for i in range(4):
            lanes, more = slice(i * 128, i * 128 + 128), slice(512 + i * 128, 640 + i * 128)
            probs = b["e_l"][i] * sums[i]
            ds = (probs * (b["d_l"][i] - mids[i])).astype(BF16)
            probs = probs.astype(BF16)
            att_t = pick(dot(b["kv"][:, more], probs, FIRST) + dot(b["halo"][:, more], b["p_h"][i], FIRST))
            gqs_t = pick(dot(b["kv"][:, lanes], ds, FIRST) + dot(b["halo"][:, lanes], b["ds_h"][i], FIRST))
            half = att_t.astype(BF16)
            b["att_t"][i] = half.reshape(2, 64, 128)
            att = att_t.T.astype(BF16)
            b["att"][:, lanes] = att
            gqs = gqs_t.T
            uq = b["uq"][:, lanes]
            grad_q = b["nq"][:, lanes] * (gqs - uq * head_sum(uq * gqs, ones))
            b["act"][:, lanes] = grad_q.astype(BF16)
            b["gkv"][:, lanes] = dot(ds, b["qm"][i])
            b["gkv"][:, more] = dot(probs, b["gm"][i])

        rows = 32 * ny

        def part_a(core):
            left = b["normed_t"][:, core].reshape(rows, 128)
            right = b["att_t"][:, core].reshape(rows, 128)
            q_part = dot(left, b["act"][:, 0:512])
            out_part = dot(right, dy_ref[...])
            return [
                jnp.concatenate(
                    [a[:, t * 128 : t * 128 + 128].reshape(ny, nx, 8, 128) for a in (q_part, out_part)], axis=2
                )
                for t in range(4)
            ]

        for t, tile in enumerate(part_a(1 - p.core)):
            b["s0a"][:, :, t] = tile.astype(BF16)
        first_a = links.start(b["s0a"], b["r0a"], p.other_core())
        for t, tile in enumerate(part_a(p.core)):
            b["own_a"][:, :, t] = tile
        mixed_ref[...] = (x_ref[...].astype(F32) + dot(b["att"][...], wout_ref[...])).astype(BF16)
        b["gn"][...] = dot(b["act"][:, 0:512], wqkv_ref[:, 0:512], TURN)
        xs = start_a(p, links, b, first_a)

        for c in grads:
            c.wait_recv()
        back = jnp.where(edge_tokens(iota((128, 128), 1)) == iota((128, 128), 0), 1.0, 0.0)
        total = b["gkv"][...] + dot(back.astype(BF16), b["grecv"][96:224, :])
        total = jnp.concatenate(
            [
                total[0:48] + b["grecv"][0:48, :].astype(F32),
                total[48:80],
                total[80:128] + b["grecv"][48:96, :].astype(F32),
            ],
            axis=0,
        )
        for i in range(4):
            lanes, more = slice(i * 128, i * 128 + 128), slice(512 + i * 128, 640 + i * 128)
            uk = b["uk"][:, lanes]
            gku = total[:, lanes]
            b["act"][:, more] = (b["nk"][:, lanes] * (gku - uk * head_sum(uk * gku, ones))).astype(BF16)
        b["act"][:, 1024:1536] = total[:, 512:1024].astype(BF16)

        def part_b(core):
            left = b["normed_t"][:, core].reshape(rows, 128)
            a = dot(left, b["act"][:, 512:1536])
            return [a[:, t * 128 : t * 128 + 128].reshape(ny, 2, 16, 128) for t in range(8)]

        for t, tile in enumerate(part_b(1 - p.core)):
            b["s0b"][:, :, t] = tile.astype(BF16)
        first_b = links.start(b["s0b"], b["r0b"], p.other_core())
        for t, tile in enumerate(part_b(p.core)):
            b["own_b"][:, :, t] = tile

        def finish():
            grad_n = b["gn"][...] + dot(b["act"][:, 512:1536], wqkv_ref[:, 512:1536], TURN)
            g = grad_n * gain_ref[...]
            xf = x_ref[...].astype(F32)
            inv = b["inv"][:, 0:1]
            mean = jnp.sum(xf * g, -1, keepdims=True) * (1.0 / 512)
            gin_ref[...] = (dy_ref[...].astype(F32) + inv * g - xf * (inv * inv * inv * mean)).astype(BF16)

        reduce_tail(p, links, b, first_b, xs, finish, factor)
        write_rows(b, gqkv_ref, gout_ref)
        links.drain()

    vm = pl.BlockSpec(memory_space=pltpu.VMEM)
    return pl.pallas_call(
        kernel,
        out_shape=(
            jax.ShapeDtypeStruct((128, 512), BF16),
            jax.ShapeDtypeStruct((128, 512), BF16),
            jax.ShapeDtypeStruct((8, 1536), F32),
            jax.ShapeDtypeStruct((8, 512), F32),
        ),
        in_specs=[vm] * 5 + [pl.BlockSpec(memory_space=pltpu.SMEM)],
        out_specs=(vm, vm, vm, vm),
        scratch_shapes=[scratch[n] for n in names]
        + [pltpu.SemaphoreType.DMA((count,)), pltpu.SemaphoreType.DMA((count,))],
        compiler_params=pltpu.CompilerParams(
            collective_id=1, has_side_effects=True, vmem_limit_bytes=56 * 1024 * 1024
        ),
        cost_estimate=pl.CostEstimate(flops=10**9, bytes_accessed=4 * 10**6, transcendentals=10**6),
        name="block",
    )(x, dy, gain, w_qkv, w_out, head_scale)


def per_device(inputs, cotangent, norm_gain, w_qkv, w_out, head_scale):
    shape, width = inputs.shape, inputs.shape[-1]
    tokens = shape[1] * shape[2]
    factor = 1.0 / math.sqrt(
        lax.axis_size("img") * lax.axis_size("gy") * lax.axis_size("gx") * tokens
    )
    mixed, grad_input, grad_qkv, grad_out = block_call(
        inputs.reshape(tokens, width),
        cotangent.reshape(tokens, width),
        norm_gain.reshape(1, width),
        w_qkv,
        w_out,
        head_scale,
        factor,
    )
    return (mixed.reshape(shape), grad_input.reshape(shape), grad_qkv, grad_out)


def solution(mesh):
    tokens, rows = P("img", "gy", "gx", None), P(("gy", "gx"), None)
    return jax.shard_map(
        per_device,
        mesh=mesh,
        in_specs=(tokens, tokens, P(), P(), P(), P()),
        out_specs=(tokens, tokens, rows, rows),
        check_vma=False,
    )
```

```python
import math

import jax
import jax.numpy as jnp
from jax import lax
from jax.experimental import pallas as pl
from jax.experimental.pallas import tpu as pltpu
from jax.sharding import PartitionSpec as P

F32, BF16 = jnp.float32, jnp.bfloat16


class Links:
    def __init__(self, send, recv):
        self.send, self.recv, self.used, self.all = send, recv, 0, []

    def start(self, src, dst, device):
        copy = pltpu.make_async_remote_copy(
            src_ref=src,
            dst_ref=dst,
            send_sem=self.send.at[self.used],
            recv_sem=self.recv.at[self.used],
            device_id=device,
            device_id_type=pl.DeviceIdType.MESH,
        )
        copy.start()
        self.used += 1
        self.all.append(copy)
        return copy

    def drain(self):
        for copy in self.all:
            copy.wait_send()


class Place:
    def __init__(self):
        gy, gx, self.z = lax.axis_index("gy"), lax.axis_index("gx"), lax.axis_index("img")
        self.gy, self.gx = gy, gx
        self.ngy, self.ngx, self.nz = (lax.axis_size(a) for a in ("gy", "gx", "img"))
        self.nx = self.ngx // 2
        self.ny = self.ngy
        self.core, self.x = gy % 2, gx % self.nx
        self.y = (gy // 2) * 2 + gx // self.nx

    def other_core(self):
        return (self.gy + 1 - 2 * self.core, self.gx, self.z)

    def x_peer(self, k):
        to = (self.x + k) % self.nx
        return to, (self.gy, self.gx - self.x + to, self.z)

    def y_peer(self, k):
        to = (self.y + k) % self.ny
        return to, ((to // 2) * 2 + self.core, (to % 2) * self.nx + self.x, self.z)

    def z_peer(self, k):
        to = (self.z + k) % self.nz
        return to, (self.gy, self.gx, to)

    def reduce_peers(self):
        return (
            [self.other_core()]
            + [self.x_peer(k)[1] for k in range(1, self.nx)]
            + [self.y_peer(k)[1] for k in range(1, self.ny)]
            + [self.z_peer(k)[1] for k in range(1, self.nz)]
        )


def enter(devices):
    barrier = pltpu.get_barrier_semaphore()
    for device in devices:
        pl.semaphore_signal(barrier, inc=1, device_id=device, device_id_type=pl.DeviceIdType.MESH)
    return lambda: pl.semaphore_wait(barrier, len(devices))


def reduce_scratch(nx, ny, nz):
    v = pltpu.VMEM
    return dict(
        r0a=v((ny, nx, 4, 16, 128), BF16),
        r0b=v((ny, 2, 8, 16, 128), BF16),
        s1a=v((ny, nx, 4, 16, 128), BF16),
        s1b=v((ny, 2, 8, 16, 128), BF16),
        rxa=v((nx - 1, ny, 4, 16, 128), BF16),
        s2a=v((ny, 4, 16, 128), BF16),
        rya=v((ny - 1, 4, 16, 128), BF16),
        za=v((nz, 4, 16, 128), BF16),
        ryb=v((ny - 1, 8, 16, 128), BF16),
        rzb=v((nz - 1, ny, 16, 128), BF16),
        syb=v((nz, 16, 128), BF16),
        szb=v((ny, 16, 128), BF16),
        r2z=v((nz - 1, 16, 128), BF16),
        r2y=v((ny - 1, 16, 128), BF16),
        ub=v((nx, 8, 128), F32),
        r3x=v((nx - 1, 8, 128), F32),
        gb=v((nz, 8, 128), F32),
    )


def reduce_count(nx, ny, nz):
    return 2 + 2 * (nx - 1) + 3 * (ny - 1) + 4 * (nz - 1)


def core_add(s1, own, got):
    def add(i, _):
        s1[i] = (own[i].astype(F32) + got[i].astype(F32)).astype(BF16)
        return 0

    lax.fori_loop(0, s1.shape[0], add, 0)


def start_a(p, links, b, first_a):
    first_a.wait_recv()
    core_add(b["s1a"], b["own_a"], b["r0a"])
    xs = []
    for k in range(1, p.nx):
        to, device = p.x_peer(k)
        xs.append(links.start(b["s1a"].at[:, to], b["rxa"].at[k - 1], device))
    return xs


def reduce_tail(p, links, b, first_b, xs, send_grads, finish, factor, qkv_ref, out_ref):
    nx, ny, nz = p.nx, p.ny, p.nz
    first_b.wait_recv()
    core_add(b["s1b"], b["own_b"], b["r0b"])
    ys, zs = [], []
    for k in range(1, max(ny, nz)):
        if k < ny:
            to, device = p.y_peer(k)
            ys.append(links.start(b["s1b"].at[to, 0], b["ryb"].at[k - 1], device))
        if k < nz:
            to, device = p.z_peer(k)
            zs.append(links.start(b["s1b"].at[:, 1, to], b["rzb"].at[k - 1], device))
    send_grads()

    for c in xs:
        c.wait_recv()

    def add_x(i, _):
        total = b["s1a"][i, p.x].astype(F32)
        for k in range(nx - 1):
            total += b["rxa"][k, i].astype(F32)
        b["s2a"][i] = total.astype(BF16)
        return 0

    lax.fori_loop(0, ny, add_x, 0)
    y2 = []
    for k in range(1, ny):
        to, device = p.y_peer(k)
        y2.append(links.start(b["s2a"].at[to], b["rya"].at[k - 1], device))

    for c in ys:
        c.wait_recv()

    def add_y(i, _):
        total = b["s1b"][p.y, 0, i].astype(F32)
        for k in range(ny - 1):
            total += b["ryb"][k, i].astype(F32)
        b["syb"][i] = total.astype(BF16)
        return 0

    lax.fori_loop(0, nz, add_y, 0)
    z3 = []
    for k in range(1, nz):
        to, device = p.z_peer(k)
        z3.append(links.start(b["syb"].at[to], b["r2z"].at[k - 1], device))

    for c in zs:
        c.wait_recv()

    def add_z(i, _):
        total = b["s1b"][i, 1, p.z].astype(F32)
        for k in range(nz - 1):
            total += b["rzb"][k, i].astype(F32)
        b["szb"][i] = total.astype(BF16)
        return 0

    lax.fori_loop(0, ny, add_z, 0)
    y3 = []
    for k in range(1, ny):
        to, device = p.y_peer(k)
        y3.append(links.start(b["szb"].at[to], b["r2y"].at[k - 1], device))

    for c in y2:
        c.wait_recv()
    total = b["s2a"][p.y].astype(F32)
    for k in range(ny - 1):
        total += b["rya"][k].astype(F32)
    b["za"][p.z] = total.astype(BF16)
    last_a = []
    for k in range(1, nz):
        to, device = p.z_peer(k)
        last_a.append(links.start(b["za"].at[p.z], b["za"].at[p.z], device))

    for c in z3:
        c.wait_recv()
    low = b["syb"][p.z].astype(F32)
    for k in range(nz - 1):
        low += b["r2z"][k].astype(F32)
    for c in y3:
        c.wait_recv()
    high = b["szb"][p.y].astype(F32)
    for k in range(ny - 1):
        high += b["r2y"][k].astype(F32)
    b["ub"][0] = low[0:8]
    b["ub"][1] = low[8:16]
    b["ub"][2] = high[0:8]
    b["ub"][3] = high[8:16]
    x3 = []
    for k in range(1, nx):
        to, device = p.x_peer(k)
        x3.append(links.start(b["ub"].at[to], b["r3x"].at[k - 1], device))

    finish()
    for c in x3:
        c.wait_recv()
    total = b["ub"][p.x]
    for k in range(nx - 1):
        total += b["r3x"][k]
    b["gb"][p.z] = total * factor
    last = []
    for k in range(1, nz):
        to, device = p.z_peer(k)
        last.append(links.start(b["gb"].at[p.z], b["gb"].at[p.z], device))
    for c in last_a:
        c.wait_recv()
    total = b["za"][0].astype(F32)
    for z in range(1, nz):
        total += b["za"][z].astype(F32)
    total = total * factor
    for t in range(4):
        qkv_ref[:, t * 128 : t * 128 + 128] = total[t, 0:8]
        out_ref[:, t * 128 : t * 128 + 128] = total[t, 8:16]
    for c in last:
        c.wait_recv()
    for t in range(8):
        qkv_ref[:, 512 + t * 128 : 640 + t * 128] = b["gb"][t]


def dot(a, b, dims=((1,), (0,))):
    return lax.dot_general(a, b, (dims, ((), ())), preferred_element_type=F32)


TURN = ((1,), (1,))
FIRST = ((0,), (0,))


def iota(shape, dim):
    return lax.broadcasted_iota(jnp.int32, shape, dim)


def edge_tokens(j):
    side = j & 31
    side_token = jnp.where((side >> 3) < 3, (side & 7) * 16 + (side >> 3) + 13 * ((j >> 5) & 1), -1)
    corner = (j - 64) >> 4
    down, across = (j >> 2) & 3, j & 3
    token = (down + 5 * (corner >> 1)) * 16 + across + 13 * (corner & 1)
    corner_token = jnp.where((down < 3) & (across < 3), token, -1)
    return jnp.where(j < 64, side_token, corner_token)


def halo_place(j):
    row = jnp.where(j < 48, (j >> 4) - 3, (j >> 4) + 5)
    col = j & 15
    side = j & 31
    is_side = (j >= 96) & (j < 160)
    row = jnp.where(is_side, side & 7, row)
    col = jnp.where(is_side, (side >> 3) + jnp.where(j < 128, -3, 16), col)
    corner = (j - 160) >> 4
    down, across = (j >> 2) & 3, j & 3
    is_corner = j >= 160
    row = jnp.where(is_corner, down + jnp.where(corner < 2, -3, 8), row)
    col = jnp.where(is_corner, across + jnp.where((corner & 1) == 0, -3, 16), col)
    filled = jnp.where(is_side, side >> 3, jnp.where(is_corner, jnp.maximum(down, across), 0))
    return row, col, filled < 3


def near(row, col, shape):
    query = iota(shape, 1)
    return (jnp.abs(row - (query >> 4)) <= 3) & (jnp.abs(col - (query & 15)) <= 3)


def twice(a):
    return jnp.concatenate([a, a], axis=1)


def head_sum(a, ones):
    top = a.astype(BF16)
    rest = (a - top.astype(F32)).astype(BF16)
    return dot(top, ones) + dot(rest, ones)


def pick(a):
    return jnp.concatenate([a[0:64, 0:128], a[64:128, 128:256]], axis=0)


BLOCKS = (
    (0, 48, 48, -1, 0),
    (48, 48, 0, 1, 0),
    (96, 32, 128, 0, -1),
    (128, 32, 96, 0, 1),
    (160, 16, 208, -1, -1),
    (176, 16, 192, -1, 1),
    (192, 16, 176, 1, -1),
    (208, 16, 160, 1, 1),
)


def block_call(x, dy, gain, w_qkv, w_out, head_scale, factor):
    nx, ny, nz = lax.axis_size("gx") // 2, lax.axis_size("gy"), lax.axis_size("img")
    v = pltpu.VMEM
    scratch = reduce_scratch(nx, ny, nz)
    scratch.update(
        own_a=v((ny, nx, 4, 16, 128), F32),
        own_b=v((ny, 2, 8, 16, 128), F32),
        s0a=v((ny, nx, 4, 16, 128), BF16),
        s0b=v((ny, 2, 8, 16, 128), BF16),
        normed=v((128, 512), BF16),
        normed_h=v((224, 512), BF16),
        normed_t=v((ny // 2, 2, 64, 128), BF16),
        uq=v((128, 512), F32),
        uk=v((128, 512), F32),
        nq=v((128, 512), F32),
        nk=v((128, 512), F32),
        x=v((128, 512), BF16),
        dy=v((128, 512), BF16),
        wqkv=v((512, 1536), BF16),
        wout=v((512, 512), BF16),
        kv=v((128, 1024), BF16),
        packed=v((128, 512), BF16),
        halo_x=v((224, 512), BF16),
        halo=v((224, 1024), BF16),
        uk_h=v((224, 512), F32),
        nk_h=v((224, 512), F32),
        normed_th=v((ny // 2, 2, 64, 224), BF16),
        act_h=v((224, 1024), BF16),
        qm=v((4, 256, 128), BF16),
        gm=v((4, 256, 128), BF16),
        mask=v((128, 128), F32),
        mask_h=v((224, 128), F32),
        e_l=v((4, 128, 256), F32),
        d_l=v((4, 128, 256), F32),
        p_h=v((4, 224, 256), BF16),
        p_l=v((4, 128, 256), BF16),
        ds_l=v((4, 128, 256), BF16),
        ds_h=v((4, 224, 256), BF16),
        gsend=v((224, 512), BF16),
        grecv=v((224, 512), BF16),
        att=v((128, 512), BF16),
        att_t=v((ny // 2, 2, 64, 128), BF16),
        act=v((128, 1536), BF16),
        inv=v((128, 128), F32),
    )
    names = list(scratch)
    count = reduce_count(nx, ny, nz) + 16

    def kernel(x_hbm, dy_hbm, gain_ref, wqkv_hbm, wout_hbm, scale_ref, mixed_ref, gin_ref, gqkv_ref, gout_ref, *rest):
        b = dict(zip(names, rest))
        links = Links(*rest[len(names) : len(names) + 2])
        load_sem = rest[-1]
        x_ref, dy_ref, wqkv_ref, wout_ref = b["x"], b["dy"], b["wqkv"], b["wout"]
        loads = [
            pltpu.make_async_copy(source, target, load_sem.at[i])
            for i, (source, target) in enumerate(
                ((x_hbm, x_ref), (wqkv_hbm, wqkv_ref), (dy_hbm, dy_ref), (wout_hbm, wout_ref))
            )
        ]
        for c in loads:
            c.start()
        p = Place()

        def neighbour(dy_step, dx_step):
            return ((p.gy + dy_step) % p.ngy, (p.gx + dx_step) % p.ngx, p.z)

        arrive = enter(p.reduce_peers() + [neighbour(*block[3:]) for block in BLOCKS])

        def exchange(source, target):
            return [
                links.start(source(start, size), target.at[land : land + size], neighbour(*step))
                for start, size, land, *step in BLOCKS
            ]

        low = iota((128, 128), 1) < 64
        ones = jnp.where((iota((128, 128), 0) < 64) == low, 1.0, 0.0).astype(BF16)

        def masked(a):
            zero = jnp.zeros_like(a)
            return jnp.concatenate([jnp.where(low, a, zero), jnp.where(low, zero, a)], axis=0).astype(BF16)

        choose = jnp.where(edge_tokens(iota((128, 128), 0)) == iota((128, 128), 1), 1.0, 0.0)
        loads[0].wait()
        b["packed"][...] = dot(choose.astype(BF16), x_ref[...]).astype(BF16)
        arrive()

        def edge_block(start, size):
            if start == 0:
                return x_ref.at[0:48]
            if start == 48:
                return x_ref.at[80:128]
            return b["packed"].at[start - 96 : start - 96 + size]

        edges = exchange(edge_block, b["halo_x"])

        def norm(source, normed_ref, turned_ref):
            xf = source[...].astype(F32)
            inv_rms = lax.rsqrt(jnp.sum(xf * xf, -1, keepdims=True) * (1.0 / 512) + 1e-6)
            normed = xf * inv_rms * gain_ref[...]
            normed_ref[...] = normed.astype(BF16)
            for i in range(4):
                turned = normed[:, i * 128 : i * 128 + 128].T.astype(BF16)
                turned_ref[i] = turned.reshape(2, 64, turned.shape[1])
            return inv_rms

        def keys_values(normed_ref, uk_ref, nk_ref, kv_ref):
            normed = normed_ref[...]
            for i in range(4):
                lanes = slice(i * 128, i * 128 + 128)
                k_raw = dot(normed, wqkv_ref[:, 512 + i * 128 : 640 + i * 128])
                nk = lax.rsqrt(head_sum(k_raw * k_raw, ones) + 1e-6)
                uk = k_raw * nk
                nk_ref[:, lanes] = nk
                uk_ref[:, lanes] = uk
                kv_ref[:, lanes] = uk.astype(BF16)
            kv_ref[:, 512:1024] = dot(normed, wqkv_ref[:, 1024:1536]).astype(BF16)

        inv_rms = norm(x_ref, b["normed"], b["normed_t"])
        b["inv"][...] = jnp.broadcast_to(inv_rms, (128, 128))
        token = iota((128, 128), 0)
        b["mask"][...] = jnp.where(near(token >> 4, token & 15, (128, 128)), 1.0, 0.0)
        row, col, there = halo_place(iota((224, 128), 0))
        all_row, all_col = row + p.gy * 8, col + p.gx * 16
        there = there & (all_row >= 0) & (all_row < 8 * p.ngy) & (all_col >= 0) & (all_col < 16 * p.ngx)
        b["mask_h"][...] = jnp.where(there & near(row, col, (224, 128)), 1.0, 0.0)
        loads[1].wait()
        keys_values(b["normed"], b["uk"], b["nk"], b["kv"])
        loads[2].wait()
        loads[3].wait()
        for i in range(4):
            lanes = slice(i * 128, i * 128 + 128)
            q_raw = dot(b["normed"][...], wqkv_ref[:, lanes])
            nq = lax.rsqrt(head_sum(q_raw * q_raw, ones) + 1e-6)
            uq = q_raw * nq
            scale = jnp.where(low, scale_ref[2 * i], scale_ref[2 * i + 1])
            b["nq"][:, lanes] = nq * scale
            b["uq"][:, lanes] = uq
            b["qm"][i] = masked(uq * scale)
            b["gm"][i] = masked(dot(dy_ref[...], wout_ref[lanes, :], TURN))

        sums, mids = [], []
        for i in range(4):
            lanes, more = slice(i * 128, i * 128 + 128), slice(512 + i * 128, 640 + i * 128)
            e = jnp.exp(dot(b["kv"][:, lanes], b["qm"][i], TURN)) * twice(b["mask"][...])
            d = dot(b["kv"][:, more], b["gm"][i], TURN)
            b["e_l"][i] = e
            b["d_l"][i] = d
            sums.append(jnp.sum(e, 0, keepdims=True))
            mids.append(jnp.sum(e * d, 0, keepdims=True))
        for c in edges:
            c.wait_recv()

        norm(b["halo_x"], b["normed_h"], b["normed_th"])
        keys_values(b["normed_h"], b["uk_h"], b["nk_h"], b["halo"])

        def key_gradient(uk, nk, gku):
            return (nk * (gku - uk * head_sum(uk * gku, ones))).astype(BF16)

        for i in range(4):
            lanes, more = slice(i * 128, i * 128 + 128), slice(512 + i * 128, 640 + i * 128)
            e = jnp.exp(dot(b["halo"][:, lanes], b["qm"][i], TURN)) * twice(b["mask_h"][...])
            d = dot(b["halo"][:, more], b["gm"][i], TURN)
            inverse = 1.0 / (sums[i] + jnp.sum(e, 0, keepdims=True))
            mid = (mids[i] + jnp.sum(e * d, 0, keepdims=True)) * inverse
            probs_h = e * inverse
            ds_h = (probs_h * (d - mid)).astype(BF16)
            probs_h = probs_h.astype(BF16)
            probs = b["e_l"][i] * inverse
            ds = (probs * (b["d_l"][i] - mid)).astype(BF16)
            probs = probs.astype(BF16)
            b["p_h"][i] = probs_h
            b["ds_h"][i] = ds_h
            b["p_l"][i] = probs
            b["ds_l"][i] = ds
            att_t = pick(dot(b["kv"][:, more], probs, FIRST) + dot(b["halo"][:, more], probs_h, FIRST))
            gqs_t = pick(dot(b["kv"][:, lanes], ds, FIRST) + dot(b["halo"][:, lanes], ds_h, FIRST))
            b["att_t"][i] = att_t.astype(BF16).reshape(2, 64, 128)
            b["att"][:, lanes] = att_t.T.astype(BF16)
            gqs = gqs_t.T
            uq = b["uq"][:, lanes]
            b["act"][:, lanes] = (b["nq"][:, lanes] * (gqs - uq * head_sum(uq * gqs, ones))).astype(BF16)

        rows = 32 * ny

        def part_a(core):
            q_part = dot(b["normed_t"][:, core].reshape(rows, 128), b["act"][:, 0:512])
            out_part = dot(b["att_t"][:, core].reshape(rows, 128), dy_ref[...])
            return [
                jnp.concatenate(
                    [a[:, t * 128 : t * 128 + 128].reshape(ny, nx, 8, 128) for a in (q_part, out_part)], axis=2
                )
                for t in range(4)
            ]

        for t, tile in enumerate(part_a(1 - p.core)):
            b["s0a"][:, :, t] = tile.astype(BF16)
        first_a = links.start(b["s0a"], b["r0a"], p.other_core())
        for t, tile in enumerate(part_a(p.core)):
            b["own_a"][:, :, t] = tile

        for i in range(4):
            lanes, more = slice(i * 128, i * 128 + 128), slice(512 + i * 128, 640 + i * 128)
            b["act_h"][:, lanes] = key_gradient(b["uk_h"][:, lanes], b["nk_h"][:, lanes], dot(b["ds_h"][i], b["qm"][i]))
            b["act_h"][:, more] = dot(b["p_h"][i], b["gm"][i]).astype(BF16)
            b["act"][:, more] = key_gradient(b["uk"][:, lanes], b["nk"][:, lanes], dot(b["ds_l"][i], b["qm"][i]))
            b["act"][:, 1024 + i * 128 : 1152 + i * 128] = dot(b["p_l"][i], b["gm"][i]).astype(BF16)

        def part_b(core):
            a = dot(b["normed_t"][:, core].reshape(rows, 128), b["act"][:, 512:1536])
            a += dot(b["normed_th"][:, core].reshape(rows, 224), b["act_h"][...])
            return [a[:, t * 128 : t * 128 + 128].reshape(ny, 2, 16, 128) for t in range(8)]

        xs = start_a(p, links, b, first_a)
        for t, tile in enumerate(part_b(1 - p.core)):
            b["s0b"][:, :, t] = tile.astype(BF16)
        first_b = links.start(b["s0b"], b["r0b"], p.other_core())
        for t, tile in enumerate(part_b(p.core)):
            b["own_b"][:, :, t] = tile
        b["gsend"][...] = dot(b["act_h"][...], wqkv_ref[:, 512:1536], TURN).astype(BF16)
        grads = []

        def send_grads():
            grads.extend(exchange(lambda start, size: b["gsend"].at[start : start + size], b["grecv"]))
            mixed_ref[...] = (x_ref[...].astype(F32) + dot(b["att"][...], wout_ref[...])).astype(BF16)

        def finish():
            grad_n = dot(b["act"][...], wqkv_ref[...], TURN)
            back = jnp.where(edge_tokens(iota((128, 128), 1)) == iota((128, 128), 0), 1.0, 0.0)
            for c in grads:
                c.wait_recv()
            grad_n += dot(back.astype(BF16), b["grecv"][96:224, :])
            grad_n = jnp.concatenate(
                [
                    grad_n[0:48] + b["grecv"][0:48, :].astype(F32),
                    grad_n[48:80],
                    grad_n[80:128] + b["grecv"][48:96, :].astype(F32),
                ],
                axis=0,
            )
            g = grad_n * gain_ref[...]
            xf = x_ref[...].astype(F32)
            inv = b["inv"][:, 0:1]
            mean = jnp.sum(xf * g, -1, keepdims=True) * (1.0 / 512)
            gin_ref[...] = (dy_ref[...].astype(F32) + inv * g - xf * (inv * inv * inv * mean)).astype(BF16)

        reduce_tail(p, links, b, first_b, xs, send_grads, finish, factor, gqkv_ref, gout_ref)
        links.drain()

    vm, anywhere = pl.BlockSpec(memory_space=pltpu.VMEM), pl.BlockSpec(memory_space=pl.ANY)
    return pl.pallas_call(
        kernel,
        out_shape=(
            jax.ShapeDtypeStruct((128, 512), BF16),
            jax.ShapeDtypeStruct((128, 512), BF16),
            jax.ShapeDtypeStruct((8, 1536), F32),
            jax.ShapeDtypeStruct((8, 512), F32),
        ),
        in_specs=[anywhere, anywhere, vm, anywhere, anywhere, pl.BlockSpec(memory_space=pltpu.SMEM)],
        out_specs=(vm, vm, vm, vm),
        scratch_shapes=[scratch[n] for n in names]
        + [pltpu.SemaphoreType.DMA((count,)), pltpu.SemaphoreType.DMA((count,)), pltpu.SemaphoreType.DMA((4,))],
        compiler_params=pltpu.CompilerParams(
            collective_id=1, has_side_effects=True, vmem_limit_bytes=56 * 1024 * 1024
        ),
        cost_estimate=pl.CostEstimate(flops=10**9, bytes_accessed=4 * 10**6, transcendentals=10**6),
        name="block",
    )(x, dy, gain, w_qkv, w_out, head_scale)


def hand_over(*arrays):
    count = len(arrays)

    def kernel(*refs):
        for i in range(count):
            refs[count + i][...] = refs[i][...]

    vm = pl.BlockSpec(memory_space=pltpu.VMEM)
    return pl.pallas_call(
        kernel,
        out_shape=tuple(jax.ShapeDtypeStruct(a.shape, a.dtype) for a in arrays),
        in_specs=[vm] * count,
        out_specs=(vm,) * count,
        name="hand_over",
    )(*arrays)


def per_device(inputs, cotangent, norm_gain, w_qkv, w_out, head_scale):
    shape, width = inputs.shape, inputs.shape[-1]
    tokens = shape[1] * shape[2]
    factor = 1.0 / math.sqrt(
        lax.axis_size("img") * lax.axis_size("gy") * lax.axis_size("gx") * tokens
    )
    results = block_call(
        inputs.reshape(tokens, width),
        cotangent.reshape(tokens, width),
        norm_gain.reshape(1, width),
        w_qkv,
        w_out,
        head_scale,
        factor,
    )
    mixed, grad_input, grad_qkv, grad_out = hand_over(*results)
    return (mixed.reshape(shape), grad_input.reshape(shape), grad_qkv, grad_out)


def solution(mesh):
    tokens, rows = P("img", "gy", "gx", None), P(("gy", "gx"), None)
    return jax.shard_map(
        per_device,
        mesh=mesh,
        in_specs=(tokens, tokens, P(), P(), P(), P()),
        out_specs=(tokens, tokens, rows, rows),
        check_vma=False,
    )
```

```python
import math

import jax
import jax.numpy as jnp
from jax import lax
from jax.experimental import pallas as pl
from jax.experimental.pallas import tpu as pltpu
from jax.sharding import PartitionSpec as P

F32, BF16 = jnp.float32, jnp.bfloat16


class Links:
    def __init__(self, send, recv):
        self.send, self.recv, self.used, self.all = send, recv, 0, []

    def start(self, src, dst, device):
        copy = pltpu.make_async_remote_copy(
            src_ref=src,
            dst_ref=dst,
            send_sem=self.send.at[self.used],
            recv_sem=self.recv.at[self.used],
            device_id=device,
            device_id_type=pl.DeviceIdType.MESH,
        )
        copy.start()
        self.used += 1
        self.all.append(copy)
        return copy

    def drain(self):
        for copy in self.all:
            copy.wait_send()


class Place:
    def __init__(self):
        gy, gx, self.z = lax.axis_index("gy"), lax.axis_index("gx"), lax.axis_index("img")
        self.gy, self.gx = gy, gx
        self.ngy, self.ngx, self.nz = (lax.axis_size(a) for a in ("gy", "gx", "img"))
        self.nx = self.ngx // 2
        self.ny = self.ngy
        self.core, self.x = gy % 2, gx % self.nx
        self.y = (gy // 2) * 2 + gx // self.nx

    def other_core(self):
        return (self.gy + 1 - 2 * self.core, self.gx, self.z)

    def x_peer(self, k):
        to = (self.x + k) % self.nx
        return to, (self.gy, self.gx - self.x + to, self.z)

    def y_peer(self, k):
        to = (self.y + k) % self.ny
        return to, ((to // 2) * 2 + self.core, (to % 2) * self.nx + self.x, self.z)

    def z_peer(self, k):
        to = (self.z + k) % self.nz
        return to, (self.gy, self.gx, to)

    def reduce_peers(self):
        return (
            [self.other_core()]
            + [self.x_peer(k)[1] for k in range(1, self.nx)]
            + [self.y_peer(k)[1] for k in range(1, self.ny)]
            + [self.z_peer(k)[1] for k in range(1, self.nz)]
        )


def enter(devices):
    barrier = pltpu.get_barrier_semaphore()
    for device in devices:
        pl.semaphore_signal(barrier, inc=1, device_id=device, device_id_type=pl.DeviceIdType.MESH)
    return lambda: pl.semaphore_wait(barrier, len(devices))


def reduce_scratch(nx, ny, nz):
    v = pltpu.VMEM
    return dict(
        r0a=v((ny, nx, 4, 16, 128), BF16),
        r0b=v((ny, 2, 8, 16, 128), BF16),
        s1a=v((ny, nx, 4, 16, 128), BF16),
        s1b=v((ny, 2, 8, 16, 128), BF16),
        rxa=v((nx - 1, ny, 4, 16, 128), BF16),
        s2a=v((ny, 4, 16, 128), BF16),
        rya=v((ny - 1, 4, 16, 128), BF16),
        za=v((nz, 4, 16, 128), BF16),
        ryb=v((ny - 1, 8, 16, 128), BF16),
        rzb=v((nz - 1, ny, 16, 128), BF16),
        syb=v((nz, 16, 128), BF16),
        szb=v((ny, 16, 128), BF16),
        r2z=v((nz - 1, 16, 128), BF16),
        r2y=v((ny - 1, 16, 128), BF16),
        ub=v((nx, 8, 128), F32),
        r3x=v((nx - 1, 8, 128), F32),
        gb=v((nz, 8, 128), F32),
    )


def reduce_count(nx, ny, nz):
    return 2 + 2 * (nx - 1) + 3 * (ny - 1) + 4 * (nz - 1)


def core_add(s1, own, got):
    def add(i, _):
        s1[i] = (own[i].astype(F32) + got[i].astype(F32)).astype(BF16)
        return 0

    lax.fori_loop(0, s1.shape[0], add, 0)


def start_a(p, links, b, first_a):
    first_a.wait_recv()
    core_add(b["s1a"], b["own_a"], b["r0a"])
    xs = []
    for k in range(1, p.nx):
        to, device = p.x_peer(k)
        xs.append(links.start(b["s1a"].at[:, to], b["rxa"].at[k - 1], device))
    return xs


def reduce_tail(p, links, b, first_b, xs, meanwhile, send_grads, finish, factor, qkv_ref, out_ref):
    nx, ny, nz = p.nx, p.ny, p.nz
    first_b.wait_recv()
    core_add(b["s1b"], b["own_b"], b["r0b"])
    ys, zs = [], []
    for k in range(1, max(ny, nz)):
        if k < ny:
            to, device = p.y_peer(k)
            ys.append(links.start(b["s1b"].at[to, 0], b["ryb"].at[k - 1], device))
        if k < nz:
            to, device = p.z_peer(k)
            zs.append(links.start(b["s1b"].at[:, 1, to], b["rzb"].at[k - 1], device))
    meanwhile()

    for c in xs:
        c.wait_recv()

    def add_x(i, _):
        total = b["s1a"][i, p.x].astype(F32)
        for k in range(nx - 1):
            total += b["rxa"][k, i].astype(F32)
        b["s2a"][i] = total.astype(BF16)
        return 0

    lax.fori_loop(0, ny, add_x, 0)
    y2 = []
    for k in range(1, ny):
        to, device = p.y_peer(k)
        y2.append(links.start(b["s2a"].at[to], b["rya"].at[k - 1], device))

    for c in ys:
        c.wait_recv()

    def add_y(i, _):
        total = b["s1b"][p.y, 0, i].astype(F32)
        for k in range(ny - 1):
            total += b["ryb"][k, i].astype(F32)
        b["syb"][i] = total.astype(BF16)
        return 0

    lax.fori_loop(0, nz, add_y, 0)
    z3 = []
    for k in range(1, nz):
        to, device = p.z_peer(k)
        z3.append(links.start(b["syb"].at[to], b["r2z"].at[k - 1], device))

    for c in zs:
        c.wait_recv()

    def add_z(i, _):
        total = b["s1b"][i, 1, p.z].astype(F32)
        for k in range(nz - 1):
            total += b["rzb"][k, i].astype(F32)
        b["szb"][i] = total.astype(BF16)
        return 0

    lax.fori_loop(0, ny, add_z, 0)
    y3 = []
    for k in range(1, ny):
        to, device = p.y_peer(k)
        y3.append(links.start(b["szb"].at[to], b["r2y"].at[k - 1], device))
    send_grads()

    for c in y2:
        c.wait_recv()
    total = b["s2a"][p.y].astype(F32)
    for k in range(ny - 1):
        total += b["rya"][k].astype(F32)
    b["za"][p.z] = total.astype(BF16)
    last_a = []
    for k in range(1, nz):
        to, device = p.z_peer(k)
        last_a.append(links.start(b["za"].at[p.z], b["za"].at[p.z], device))

    for c in z3:
        c.wait_recv()
    low = b["syb"][p.z].astype(F32)
    for k in range(nz - 1):
        low += b["r2z"][k].astype(F32)
    for c in y3:
        c.wait_recv()
    high = b["szb"][p.y].astype(F32)
    for k in range(ny - 1):
        high += b["r2y"][k].astype(F32)
    b["ub"][0] = low[0:8]
    b["ub"][1] = low[8:16]
    b["ub"][2] = high[0:8]
    b["ub"][3] = high[8:16]
    x3 = []
    for k in range(1, nx):
        to, device = p.x_peer(k)
        x3.append(links.start(b["ub"].at[to], b["r3x"].at[k - 1], device))

    for c in x3:
        c.wait_recv()
    total = b["ub"][p.x]
    for k in range(nx - 1):
        total += b["r3x"][k]
    b["gb"][p.z] = total * factor
    last = []
    for k in range(1, nz):
        to, device = p.z_peer(k)
        last.append(links.start(b["gb"].at[p.z], b["gb"].at[p.z], device))
    finish()
    for c in last_a:
        c.wait_recv()
    total = b["za"][0].astype(F32)
    for z in range(1, nz):
        total += b["za"][z].astype(F32)
    total = total * factor
    for t in range(4):
        qkv_ref[:, t * 128 : t * 128 + 128] = total[t, 0:8]
        out_ref[:, t * 128 : t * 128 + 128] = total[t, 8:16]
    for c in last:
        c.wait_recv()
    for t in range(8):
        qkv_ref[:, 512 + t * 128 : 640 + t * 128] = b["gb"][t]


def dot(a, b, dims=((1,), (0,))):
    return lax.dot_general(a, b, (dims, ((), ())), preferred_element_type=F32)


TURN = ((1,), (1,))
FIRST = ((0,), (0,))


def iota(shape, dim):
    return lax.broadcasted_iota(jnp.int32, shape, dim)


def edge_tokens(j):
    side = j & 31
    side_token = jnp.where((side >> 3) < 3, (side & 7) * 16 + (side >> 3) + 13 * ((j >> 5) & 1), -1)
    corner = (j - 64) >> 4
    down, across = (j >> 2) & 3, j & 3
    token = (down + 5 * (corner >> 1)) * 16 + across + 13 * (corner & 1)
    corner_token = jnp.where((down < 3) & (across < 3), token, -1)
    return jnp.where(j < 64, side_token, corner_token)


def halo_place(j):
    row = jnp.where(j < 48, (j >> 4) - 3, (j >> 4) + 5)
    col = j & 15
    side = j & 31
    is_side = (j >= 96) & (j < 160)
    row = jnp.where(is_side, side & 7, row)
    col = jnp.where(is_side, (side >> 3) + jnp.where(j < 128, -3, 16), col)
    corner = (j - 160) >> 4
    down, across = (j >> 2) & 3, j & 3
    is_corner = j >= 160
    row = jnp.where(is_corner, down + jnp.where(corner < 2, -3, 8), row)
    col = jnp.where(is_corner, across + jnp.where((corner & 1) == 0, -3, 16), col)
    filled = jnp.where(is_side, side >> 3, jnp.where(is_corner, jnp.maximum(down, across), 0))
    return row, col, filled < 3


def near(row, col, shape):
    query = iota(shape, 1)
    return (jnp.abs(row - (query >> 4)) <= 3) & (jnp.abs(col - (query & 15)) <= 3)


def twice(a):
    return jnp.concatenate([a, a], axis=1)


def head_sum(a, ones):
    top = a.astype(BF16)
    rest = (a - top.astype(F32)).astype(BF16)
    return dot(top, ones) + dot(rest, ones)


def pick(a):
    return jnp.concatenate([a[0:64, 0:128], a[64:128, 128:256]], axis=0)


BLOCKS = (
    (0, 48, 48, -1, 0),
    (48, 48, 0, 1, 0),
    (96, 32, 128, 0, -1),
    (128, 32, 96, 0, 1),
    (160, 16, 208, -1, -1),
    (176, 16, 192, -1, 1),
    (192, 16, 176, 1, -1),
    (208, 16, 160, 1, 1),
)


def block_call(x, dy, gain, w_qkv, w_out, head_scale, factor):
    nx, ny, nz = lax.axis_size("gx") // 2, lax.axis_size("gy"), lax.axis_size("img")
    v = pltpu.VMEM
    scratch = reduce_scratch(nx, ny, nz)
    scratch.update(
        own_a=v((ny, nx, 4, 16, 128), F32),
        own_b=v((ny, 2, 8, 16, 128), F32),
        s0a=v((ny, nx, 4, 16, 128), BF16),
        s0b=v((ny, 2, 8, 16, 128), BF16),
        normed=v((128, 512), BF16),
        normed_h=v((224, 512), BF16),
        normed_t=v((ny // 2, 2, 64, 128), BF16),
        uq=v((128, 512), F32),
        uk=v((128, 512), F32),
        nq=v((128, 512), F32),
        nk=v((128, 512), F32),
        x=v((128, 512), BF16),
        dy=v((128, 512), BF16),
        wqkv=v((512, 1536), BF16),
        wout=v((512, 512), BF16),
        kv=v((128, 1024), BF16),
        packed=v((128, 512), BF16),
        halo_x=v((224, 512), BF16),
        halo=v((224, 1024), BF16),
        uk_h=v((224, 512), F32),
        nk_h=v((224, 512), F32),
        normed_th=v((ny // 2, 2, 64, 224), BF16),
        act_h=v((224, 1024), BF16),
        qm=v((4, 256, 128), BF16),
        gm=v((4, 256, 128), BF16),
        mask=v((128, 128), F32),
        mask_h=v((224, 128), F32),
        e_l=v((4, 128, 256), F32),
        d_l=v((4, 128, 256), F32),
        p_h=v((4, 224, 256), BF16),
        p_l=v((4, 128, 256), BF16),
        ds_l=v((4, 128, 256), BF16),
        ds_h=v((4, 224, 256), BF16),
        gsend=v((224, 512), BF16),
        gn=v((128, 512), F32),
        grecv=v((224, 512), BF16),
        att=v((128, 512), BF16),
        att_t=v((ny // 2, 2, 64, 128), BF16),
        act=v((128, 1536), BF16),
        inv=v((128, 128), F32),
    )
    names = list(scratch)
    count = reduce_count(nx, ny, nz) + 16

    def kernel(x_hbm, dy_hbm, gain_ref, wqkv_hbm, wout_hbm, scale_ref, mixed_ref, gin_ref, gqkv_ref, gout_ref, *rest):
        b = dict(zip(names, rest))
        links = Links(*rest[len(names) : len(names) + 2])
        load_sem = rest[-1]
        x_ref, dy_ref, wqkv_ref, wout_ref = b["x"], b["dy"], b["wqkv"], b["wout"]
        loads = [
            pltpu.make_async_copy(source, target, load_sem.at[i])
            for i, (source, target) in enumerate(
                ((x_hbm, x_ref), (wqkv_hbm, wqkv_ref), (dy_hbm, dy_ref), (wout_hbm, wout_ref))
            )
        ]
        for c in loads:
            c.start()
        p = Place()

        def neighbour(dy_step, dx_step):
            return ((p.gy + dy_step) % p.ngy, (p.gx + dx_step) % p.ngx, p.z)

        arrive = enter(p.reduce_peers() + [neighbour(*block[3:]) for block in BLOCKS])

        def exchange(source, target):
            return [
                links.start(source(start, size), target.at[land : land + size], neighbour(*step))
                for start, size, land, *step in BLOCKS
            ]

        low = iota((128, 128), 1) < 64
        ones = jnp.where((iota((128, 128), 0) < 64) == low, 1.0, 0.0).astype(BF16)

        def masked(a):
            zero = jnp.zeros_like(a)
            return jnp.concatenate([jnp.where(low, a, zero), jnp.where(low, zero, a)], axis=0).astype(BF16)

        choose = jnp.where(edge_tokens(iota((128, 128), 0)) == iota((128, 128), 1), 1.0, 0.0)
        loads[0].wait()
        b["packed"][...] = dot(choose.astype(BF16), x_ref[...]).astype(BF16)
        arrive()

        def edge_block(start, size):
            if start == 0:
                return x_ref.at[0:48]
            if start == 48:
                return x_ref.at[80:128]
            return b["packed"].at[start - 96 : start - 96 + size]

        edges = exchange(edge_block, b["halo_x"])

        def norm(source, normed_ref, turned_ref):
            xf = source[...].astype(F32)
            inv_rms = lax.rsqrt(jnp.sum(xf * xf, -1, keepdims=True) * (1.0 / 512) + 1e-6)
            normed = xf * inv_rms * gain_ref[...]
            normed_ref[...] = normed.astype(BF16)
            for i in range(4):
                turned = normed[:, i * 128 : i * 128 + 128].T.astype(BF16)
                turned_ref[i] = turned.reshape(2, 64, turned.shape[1])
            return inv_rms

        def keys_values(normed_ref, uk_ref, nk_ref, kv_ref):
            normed = normed_ref[...]
            for i in range(4):
                lanes = slice(i * 128, i * 128 + 128)
                k_raw = dot(normed, wqkv_ref[:, 512 + i * 128 : 640 + i * 128])
                nk = lax.rsqrt(head_sum(k_raw * k_raw, ones) + 1e-6)
                uk = k_raw * nk
                nk_ref[:, lanes] = nk
                uk_ref[:, lanes] = uk
                kv_ref[:, lanes] = uk.astype(BF16)
            kv_ref[:, 512:1024] = dot(normed, wqkv_ref[:, 1024:1536]).astype(BF16)

        inv_rms = norm(x_ref, b["normed"], b["normed_t"])
        b["inv"][...] = jnp.broadcast_to(inv_rms, (128, 128))
        token = iota((128, 128), 0)
        b["mask"][...] = jnp.where(near(token >> 4, token & 15, (128, 128)), 1.0, 0.0)
        row, col, there = halo_place(iota((224, 128), 0))
        all_row, all_col = row + p.gy * 8, col + p.gx * 16
        there = there & (all_row >= 0) & (all_row < 8 * p.ngy) & (all_col >= 0) & (all_col < 16 * p.ngx)
        b["mask_h"][...] = jnp.where(there & near(row, col, (224, 128)), 1.0, 0.0)
        loads[1].wait()
        keys_values(b["normed"], b["uk"], b["nk"], b["kv"])
        loads[2].wait()
        loads[3].wait()
        for i in range(4):
            lanes = slice(i * 128, i * 128 + 128)
            q_raw = dot(b["normed"][...], wqkv_ref[:, lanes])
            nq = lax.rsqrt(head_sum(q_raw * q_raw, ones) + 1e-6)
            uq = q_raw * nq
            scale = jnp.where(low, scale_ref[2 * i], scale_ref[2 * i + 1])
            b["nq"][:, lanes] = nq * scale
            b["uq"][:, lanes] = uq
            b["qm"][i] = masked(uq * scale)
            b["gm"][i] = masked(dot(dy_ref[...], wout_ref[lanes, :], TURN))

        sums, mids = [], []
        for i in range(4):
            lanes, more = slice(i * 128, i * 128 + 128), slice(512 + i * 128, 640 + i * 128)
            e = jnp.exp(dot(b["kv"][:, lanes], b["qm"][i], TURN)) * twice(b["mask"][...])
            d = dot(b["kv"][:, more], b["gm"][i], TURN)
            b["e_l"][i] = e
            b["d_l"][i] = d
            sums.append(jnp.sum(e, 0, keepdims=True))
            mids.append(jnp.sum(e * d, 0, keepdims=True))
        for c in edges:
            c.wait_recv()

        norm(b["halo_x"], b["normed_h"], b["normed_th"])
        keys_values(b["normed_h"], b["uk_h"], b["nk_h"], b["halo"])

        def key_gradient(uk, nk, gku):
            return (nk * (gku - uk * head_sum(uk * gku, ones))).astype(BF16)

        for i in range(4):
            lanes, more = slice(i * 128, i * 128 + 128), slice(512 + i * 128, 640 + i * 128)
            e = jnp.exp(dot(b["halo"][:, lanes], b["qm"][i], TURN)) * twice(b["mask_h"][...])
            d = dot(b["halo"][:, more], b["gm"][i], TURN)
            inverse = 1.0 / (sums[i] + jnp.sum(e, 0, keepdims=True))
            mid = (mids[i] + jnp.sum(e * d, 0, keepdims=True)) * inverse
            probs_h = e * inverse
            ds_h = (probs_h * (d - mid)).astype(BF16)
            probs_h = probs_h.astype(BF16)
            probs = b["e_l"][i] * inverse
            ds = (probs * (b["d_l"][i] - mid)).astype(BF16)
            probs = probs.astype(BF16)
            b["p_h"][i] = probs_h
            b["ds_h"][i] = ds_h
            b["p_l"][i] = probs
            b["ds_l"][i] = ds
            att_t = pick(dot(b["kv"][:, more], probs, FIRST) + dot(b["halo"][:, more], probs_h, FIRST))
            gqs_t = pick(dot(b["kv"][:, lanes], ds, FIRST) + dot(b["halo"][:, lanes], ds_h, FIRST))
            b["att_t"][i] = att_t.astype(BF16).reshape(2, 64, 128)
            b["att"][:, lanes] = att_t.T.astype(BF16)
            gqs = gqs_t.T
            uq = b["uq"][:, lanes]
            b["act"][:, lanes] = (b["nq"][:, lanes] * (gqs - uq * head_sum(uq * gqs, ones))).astype(BF16)

        rows = 32 * ny

        def part_a(core):
            q_part = dot(b["normed_t"][:, core].reshape(rows, 128), b["act"][:, 0:512])
            out_part = dot(b["att_t"][:, core].reshape(rows, 128), dy_ref[...])
            return [
                jnp.concatenate(
                    [a[:, t * 128 : t * 128 + 128].reshape(ny, nx, 8, 128) for a in (q_part, out_part)], axis=2
                )
                for t in range(4)
            ]

        for t, tile in enumerate(part_a(1 - p.core)):
            b["s0a"][:, :, t] = tile.astype(BF16)
        first_a = links.start(b["s0a"], b["r0a"], p.other_core())
        for t, tile in enumerate(part_a(p.core)):
            b["own_a"][:, :, t] = tile

        for i in range(4):
            lanes, more = slice(i * 128, i * 128 + 128), slice(512 + i * 128, 640 + i * 128)
            b["act_h"][:, lanes] = key_gradient(b["uk_h"][:, lanes], b["nk_h"][:, lanes], dot(b["ds_h"][i], b["qm"][i]))
            b["act_h"][:, more] = dot(b["p_h"][i], b["gm"][i]).astype(BF16)
            b["act"][:, more] = key_gradient(b["uk"][:, lanes], b["nk"][:, lanes], dot(b["ds_l"][i], b["qm"][i]))
            b["act"][:, 1024 + i * 128 : 1152 + i * 128] = dot(b["p_l"][i], b["gm"][i]).astype(BF16)

        def part_b(core):
            a = dot(b["normed_t"][:, core].reshape(rows, 128), b["act"][:, 512:1536])
            a += dot(b["normed_th"][:, core].reshape(rows, 224), b["act_h"][...])
            return [a[:, t * 128 : t * 128 + 128].reshape(ny, 2, 16, 128) for t in range(8)]

        xs = start_a(p, links, b, first_a)
        for t, tile in enumerate(part_b(1 - p.core)):
            b["s0b"][:, :, t] = tile.astype(BF16)
        first_b = links.start(b["s0b"], b["r0b"], p.other_core())
        for t, tile in enumerate(part_b(p.core)):
            b["own_b"][:, :, t] = tile
        grads = []

        def send_grads():
            grads.extend(exchange(lambda start, size: b["gsend"].at[start : start + size], b["grecv"]))

        def meanwhile():
            b["gsend"][...] = dot(b["act_h"][...], wqkv_ref[:, 512:1536], TURN).astype(BF16)
            b["gn"][...] = dot(b["act"][...], wqkv_ref[...], TURN)
            mixed_ref[...] = (x_ref[...].astype(F32) + dot(b["att"][...], wout_ref[...])).astype(BF16)

        def finish():
            back = jnp.where(edge_tokens(iota((128, 128), 1)) == iota((128, 128), 0), 1.0, 0.0)
            for c in grads:
                c.wait_recv()
            grad_n = b["gn"][...] + dot(back.astype(BF16), b["grecv"][96:224, :])
            grad_n = jnp.concatenate(
                [
                    grad_n[0:48] + b["grecv"][0:48, :].astype(F32),
                    grad_n[48:80],
                    grad_n[80:128] + b["grecv"][48:96, :].astype(F32),
                ],
                axis=0,
            )
            g = grad_n * gain_ref[...]
            xf = x_ref[...].astype(F32)
            inv = b["inv"][:, 0:1]
            mean = jnp.sum(xf * g, -1, keepdims=True) * (1.0 / 512)
            gin_ref[...] = (dy_ref[...].astype(F32) + inv * g - xf * (inv * inv * inv * mean)).astype(BF16)

        reduce_tail(p, links, b, first_b, xs, meanwhile, send_grads, finish, factor, gqkv_ref, gout_ref)
        links.drain()

    vm, anywhere = pl.BlockSpec(memory_space=pltpu.VMEM), pl.BlockSpec(memory_space=pl.ANY)
    return pl.pallas_call(
        kernel,
        out_shape=(
            jax.ShapeDtypeStruct((128, 512), BF16),
            jax.ShapeDtypeStruct((128, 512), BF16),
            jax.ShapeDtypeStruct((8, 1536), F32),
            jax.ShapeDtypeStruct((8, 512), F32),
        ),
        in_specs=[anywhere, anywhere, vm, anywhere, anywhere, pl.BlockSpec(memory_space=pltpu.SMEM)],
        out_specs=(vm, vm, vm, vm),
        scratch_shapes=[scratch[n] for n in names]
        + [pltpu.SemaphoreType.DMA((count,)), pltpu.SemaphoreType.DMA((count,)), pltpu.SemaphoreType.DMA((4,))],
        compiler_params=pltpu.CompilerParams(
            collective_id=1, has_side_effects=True, vmem_limit_bytes=56 * 1024 * 1024
        ),
        cost_estimate=pl.CostEstimate(flops=10**9, bytes_accessed=4 * 10**6, transcendentals=10**6),
        name="block",
    )(x, dy, gain, w_qkv, w_out, head_scale)


def hand_over(*arrays):
    count = len(arrays)

    def kernel(*refs):
        for i in range(count):
            refs[count + i][...] = refs[i][...]

    vm = pl.BlockSpec(memory_space=pltpu.VMEM)
    return pl.pallas_call(
        kernel,
        out_shape=tuple(jax.ShapeDtypeStruct(a.shape, a.dtype) for a in arrays),
        in_specs=[vm] * count,
        out_specs=(vm,) * count,
        name="hand_over",
    )(*arrays)


def per_device(inputs, cotangent, norm_gain, w_qkv, w_out, head_scale):
    shape, width = inputs.shape, inputs.shape[-1]
    tokens = shape[1] * shape[2]
    factor = 1.0 / math.sqrt(
        lax.axis_size("img") * lax.axis_size("gy") * lax.axis_size("gx") * tokens
    )
    results = block_call(
        inputs.reshape(tokens, width),
        cotangent.reshape(tokens, width),
        norm_gain.reshape(1, width),
        w_qkv,
        w_out,
        head_scale,
        factor,
    )
    mixed, grad_input, grad_qkv, grad_out = hand_over(*results)
    return (mixed.reshape(shape), grad_input.reshape(shape), grad_qkv, grad_out)


def solution(mesh):
    tokens, rows = P("img", "gy", "gx", None), P(("gy", "gx"), None)
    return jax.shard_map(
        per_device,
        mesh=mesh,
        in_specs=(tokens, tokens, P(), P(), P(), P()),
        out_specs=(tokens, tokens, rows, rows),
        check_vma=False,
    )
```

```python
import math

import jax
import jax.numpy as jnp
from jax import lax
from jax.experimental import pallas as pl
from jax.experimental.pallas import tpu as pltpu
from jax.sharding import PartitionSpec as P

F32, BF16 = jnp.float32, jnp.bfloat16


class Links:
    def __init__(self, send, recv):
        self.send, self.recv, self.used, self.all = send, recv, 0, []

    def start(self, src, dst, device):
        copy = pltpu.make_async_remote_copy(
            src_ref=src,
            dst_ref=dst,
            send_sem=self.send.at[self.used],
            recv_sem=self.recv.at[self.used],
            device_id=device,
            device_id_type=pl.DeviceIdType.MESH,
        )
        copy.start()
        self.used += 1
        self.all.append(copy)
        return copy

    def drain(self):
        for copy in self.all:
            copy.wait_send()


class Place:
    def __init__(self):
        gy, gx, self.z = lax.axis_index("gy"), lax.axis_index("gx"), lax.axis_index("img")
        self.gy, self.gx = gy, gx
        self.ngy, self.ngx, self.nz = (lax.axis_size(a) for a in ("gy", "gx", "img"))
        self.nx = self.ngx // 2
        self.ny = self.ngy
        self.core, self.x = gy % 2, gx % self.nx
        self.y = (gy // 2) * 2 + gx // self.nx

    def other_core(self):
        return (self.gy + 1 - 2 * self.core, self.gx, self.z)

    def x_peer(self, k):
        to = (self.x + k) % self.nx
        return to, (self.gy, self.gx - self.x + to, self.z)

    def y_peer(self, k):
        to = (self.y + k) % self.ny
        return to, ((to // 2) * 2 + self.core, (to % 2) * self.nx + self.x, self.z)

    def z_peer(self, k):
        to = (self.z + k) % self.nz
        return to, (self.gy, self.gx, to)

    def reduce_peers(self):
        return (
            [self.other_core()]
            + [self.x_peer(k)[1] for k in range(1, self.nx)]
            + [self.y_peer(k)[1] for k in range(1, self.ny)]
            + [self.z_peer(k)[1] for k in range(1, self.nz)]
        )


def enter(devices):
    barrier = pltpu.get_barrier_semaphore()
    for device in devices:
        pl.semaphore_signal(barrier, inc=1, device_id=device, device_id_type=pl.DeviceIdType.MESH)
    return lambda: pl.semaphore_wait(barrier, len(devices))


def reduce_scratch(nx, ny, nz):
    v = pltpu.VMEM
    return dict(
        r0a=v((ny, nx, 4, 16, 128), BF16),
        r0b=v((ny, 2, 8, 16, 128), BF16),
        s1a=v((ny, nx, 4, 16, 128), BF16),
        s1b=v((ny, 2, 8, 16, 128), BF16),
        rxa=v((nx - 1, ny, 4, 16, 128), BF16),
        s2a=v((ny, 4, 16, 128), BF16),
        rya=v((ny - 1, 4, 16, 128), BF16),
        za=v((nz, 4, 16, 128), BF16),
        ryb=v((ny - 1, 8, 16, 128), BF16),
        rzb=v((nz - 1, ny, 16, 128), BF16),
        syb=v((2, nz, 8, 128), F32),
        szb=v((2, ny, 8, 128), F32),
        mb=v((nx * nz, 8, 128), F32),
        gb=v((nz, 8, 128), F32),
    )


def reduce_count(nx, ny, nz):
    return 2 + (nx - 1) + 2 * (ny - 1) + 3 * (nz - 1)


def core_add(s1, own, got):
    def add(i, _):
        s1[i] = (own[i].astype(F32) + got[i].astype(F32)).astype(BF16)
        return 0

    lax.fori_loop(0, s1.shape[0], add, 0)


def start_a(p, links, b, first_a):
    first_a.wait_recv()
    core_add(b["s1a"], b["own_a"], b["r0a"])
    xs = []
    for k in range(1, p.nx):
        to, device = p.x_peer(k)
        xs.append(links.start(b["s1a"].at[:, to], b["rxa"].at[k - 1], device))
    return xs


def reduce_tail(p, links, b, first_b, xs, owner_sems, meanwhile, send_grads, finish, factor, qkv_ref, out_ref):
    nx, ny, nz = p.nx, p.ny, p.nz
    first_b.wait_recv()
    core_add(b["s1b"], b["own_b"], b["r0b"])
    ys, zs = [], []
    for k in range(1, max(ny, nz)):
        if k < ny:
            to, device = p.y_peer(k)
            ys.append(links.start(b["s1b"].at[to, 0], b["ryb"].at[k - 1], device))
        if k < nz:
            to, device = p.z_peer(k)
            zs.append(links.start(b["s1b"].at[:, 1, to], b["rzb"].at[k - 1], device))
    meanwhile()

    for c in xs:
        c.wait_recv()

    def add_x(i, _):
        total = b["s1a"][i, p.x].astype(F32)
        for k in range(nx - 1):
            total += b["rxa"][k, i].astype(F32)
        b["s2a"][i] = total.astype(BF16)
        return 0

    lax.fori_loop(0, ny, add_x, 0)
    y2 = []
    for k in range(1, ny):
        to, device = p.y_peer(k)
        y2.append(links.start(b["s2a"].at[to], b["rya"].at[k - 1], device))

    for c in ys:
        c.wait_recv()

    def add_y(i, _):
        total = b["s1b"][p.y, 0, i].astype(F32)
        for k in range(ny - 1):
            total += b["ryb"][k, i].astype(F32)
        b["syb"][0, i] = total[0:8]
        b["syb"][1, i] = total[8:16]
        return 0

    lax.fori_loop(0, nz, add_y, 0)

    def to_owner(tile, slot, device):
        return pltpu.make_async_remote_copy(
            src_ref=tile,
            dst_ref=b["mb"].at[slot],
            send_sem=owner_sems.at[0],
            recv_sem=owner_sems.at[1],
            device_id=device,
            device_id_type=pl.DeviceIdType.MESH,
        )

    def spread(tiles, first, peers, mine):
        for j in range(2):
            column = p.gx - p.x + first + j
            for k in range(peers):
                if first == 0:
                    to, device = p.z_peer(k)
                    device = (p.gy, column, device[2])
                else:
                    to, device = p.y_peer(k)
                    device = (device[0], device[1] - p.x + first + j, p.z)
                copy = to_owner(tiles.at[j, to], p.x * peers + mine, device)
                if k > 0:
                    copy.start()
                else:
                    pl.when(p.x != first + j)(copy.start)

    spread(b["syb"], 0, nz, p.z)

    for c in zs:
        c.wait_recv()

    def add_z(i, _):
        total = b["s1b"][i, 1, p.z].astype(F32)
        for k in range(nz - 1):
            total += b["rzb"][k, i].astype(F32)
        b["szb"][0, i] = total[0:8]
        b["szb"][1, i] = total[8:16]
        return 0

    lax.fori_loop(0, ny, add_z, 0)
    spread(b["szb"], 2, ny, p.y)

    @pl.when(p.x < 2)
    def _():
        b["mb"][p.x * nz + p.z] = b["syb"][p.x % 2, p.z]

    @pl.when(p.x >= 2)
    def _():
        b["mb"][p.x * ny + p.y] = b["szb"][p.x % 2, p.y]

    send_grads()

    for c in y2:
        c.wait_recv()
    total = b["s2a"][p.y].astype(F32)
    for k in range(ny - 1):
        total += b["rya"][k].astype(F32)
    b["za"][p.z] = total.astype(BF16)
    last_a = []
    for k in range(1, nz):
        to, device = p.z_peer(k)
        last_a.append(links.start(b["za"].at[p.z], b["za"].at[p.z], device))

    others = b["mb"].at[0 : nx * nz - 1]
    pltpu.make_async_copy(others, others, owner_sems.at[1]).wait()
    total = jnp.sum(b["mb"][...], axis=0)
    b["gb"][p.z] = total * factor
    last = []
    for k in range(1, nz):
        to, device = p.z_peer(k)
        last.append(links.start(b["gb"].at[p.z], b["gb"].at[p.z], device))
    finish()
    for c in last_a:
        c.wait_recv()
    total = b["za"][0].astype(F32)
    for z in range(1, nz):
        total += b["za"][z].astype(F32)
    total = total * factor
    for t in range(4):
        qkv_ref[:, t * 128 : t * 128 + 128] = total[t, 0:8]
        out_ref[:, t * 128 : t * 128 + 128] = total[t, 8:16]
    for c in last:
        c.wait_recv()
    pltpu.make_async_copy(others, others, owner_sems.at[0]).wait()
    for t in range(8):
        qkv_ref[:, 512 + t * 128 : 640 + t * 128] = b["gb"][t]


def dot(a, b, dims=((1,), (0,))):
    return lax.dot_general(a, b, (dims, ((), ())), preferred_element_type=F32)


TURN = ((1,), (1,))
FIRST = ((0,), (0,))


def iota(shape, dim):
    return lax.broadcasted_iota(jnp.int32, shape, dim)


def edge_tokens(j):
    side = j & 31
    side_token = jnp.where((side >> 3) < 3, (side & 7) * 16 + (side >> 3) + 13 * ((j >> 5) & 1), -1)
    corner = (j - 64) >> 4
    down, across = (j >> 2) & 3, j & 3
    token = (down + 5 * (corner >> 1)) * 16 + across + 13 * (corner & 1)
    corner_token = jnp.where((down < 3) & (across < 3), token, -1)
    return jnp.where(j < 64, side_token, corner_token)


def halo_place(j):
    row = jnp.where(j < 48, (j >> 4) - 3, (j >> 4) + 5)
    col = j & 15
    side = j & 31
    is_side = (j >= 96) & (j < 160)
    row = jnp.where(is_side, side & 7, row)
    col = jnp.where(is_side, (side >> 3) + jnp.where(j < 128, -3, 16), col)
    corner = (j - 160) >> 4
    down, across = (j >> 2) & 3, j & 3
    is_corner = j >= 160
    row = jnp.where(is_corner, down + jnp.where(corner < 2, -3, 8), row)
    col = jnp.where(is_corner, across + jnp.where((corner & 1) == 0, -3, 16), col)
    filled = jnp.where(is_side, side >> 3, jnp.where(is_corner, jnp.maximum(down, across), 0))
    return row, col, filled < 3


def near(row, col, shape):
    query = iota(shape, 1)
    return (jnp.abs(row - (query >> 4)) <= 3) & (jnp.abs(col - (query & 15)) <= 3)


def twice(a):
    return jnp.concatenate([a, a], axis=1)


def head_sum(a, ones):
    top = a.astype(BF16)
    rest = (a - top.astype(F32)).astype(BF16)
    return dot(top, ones) + dot(rest, ones)


def pick(a):
    return jnp.concatenate([a[0:64, 0:128], a[64:128, 128:256]], axis=0)


BLOCKS = (
    (0, 48, 48, -1, 0),
    (48, 48, 0, 1, 0),
    (96, 32, 128, 0, -1),
    (128, 32, 96, 0, 1),
    (160, 16, 208, -1, -1),
    (176, 16, 192, -1, 1),
    (192, 16, 176, 1, -1),
    (208, 16, 160, 1, 1),
)


def block_call(x, dy, gain, w_qkv, w_out, head_scale, factor):
    nx, ny, nz = lax.axis_size("gx") // 2, lax.axis_size("gy"), lax.axis_size("img")
    v = pltpu.VMEM
    scratch = reduce_scratch(nx, ny, nz)
    scratch.update(
        own_a=v((ny, nx, 4, 16, 128), F32),
        own_b=v((ny, 2, 8, 16, 128), F32),
        s0a=v((ny, nx, 4, 16, 128), BF16),
        s0b=v((ny, 2, 8, 16, 128), BF16),
        normed=v((128, 512), BF16),
        normed_h=v((224, 512), BF16),
        normed_t=v((ny // 2, 2, 64, 128), BF16),
        uq=v((128, 512), F32),
        uk=v((128, 512), F32),
        nq=v((128, 512), F32),
        nk=v((128, 512), F32),
        x=v((128, 512), BF16),
        dy=v((128, 512), BF16),
        wqkv=v((512, 1536), BF16),
        wout=v((512, 512), BF16),
        kv=v((128, 1024), BF16),
        packed=v((128, 512), BF16),
        halo_x=v((224, 512), BF16),
        halo=v((224, 1024), BF16),
        uk_h=v((224, 512), F32),
        nk_h=v((224, 512), F32),
        normed_th=v((ny // 2, 2, 64, 224), BF16),
        act_h=v((224, 1024), BF16),
        qm=v((4, 256, 128), BF16),
        gm=v((4, 256, 128), BF16),
        mask=v((128, 128), F32),
        mask_h=v((224, 128), F32),
        e_l=v((4, 128, 256), F32),
        d_l=v((4, 128, 256), F32),
        p_h=v((4, 224, 256), BF16),
        p_l=v((4, 128, 256), BF16),
        ds_l=v((4, 128, 256), BF16),
        ds_h=v((4, 224, 256), BF16),
        gsend=v((224, 512), BF16),
        gn=v((128, 512), F32),
        grecv=v((224, 512), BF16),
        att=v((128, 512), BF16),
        att_t=v((ny // 2, 2, 64, 128), BF16),
        act=v((128, 1536), BF16),
        inv=v((128, 128), F32),
    )
    names = list(scratch)
    count = reduce_count(nx, ny, nz) + 16

    def kernel(x_hbm, dy_hbm, gain_ref, wqkv_hbm, wout_hbm, scale_ref, mixed_ref, gin_ref, gqkv_ref, gout_ref, *rest):
        b = dict(zip(names, rest))
        links = Links(*rest[len(names) : len(names) + 2])
        load_sem, owner_sems = rest[len(names) + 2 :]
        x_ref, dy_ref, wqkv_ref, wout_ref = b["x"], b["dy"], b["wqkv"], b["wout"]
        loads = [
            pltpu.make_async_copy(source, target, load_sem.at[i])
            for i, (source, target) in enumerate(
                ((x_hbm, x_ref), (wqkv_hbm, wqkv_ref), (dy_hbm, dy_ref), (wout_hbm, wout_ref))
            )
        ]
        for c in loads:
            c.start()
        p = Place()

        def neighbour(dy_step, dx_step):
            return ((p.gy + dy_step) % p.ngy, (p.gx + dx_step) % p.ngx, p.z)

        arrive = enter([neighbour(*block[3:]) for block in BLOCKS] + p.reduce_peers())

        def exchange(source, target):
            return [
                links.start(source(start, size), target.at[land : land + size], neighbour(*step))
                for start, size, land, *step in BLOCKS
            ]

        low = iota((128, 128), 1) < 64
        ones = jnp.where((iota((128, 128), 0) < 64) == low, 1.0, 0.0).astype(BF16)

        def masked(a):
            zero = jnp.zeros_like(a)
            return jnp.concatenate([jnp.where(low, a, zero), jnp.where(low, zero, a)], axis=0).astype(BF16)

        choose = jnp.where(edge_tokens(iota((128, 128), 0)) == iota((128, 128), 1), 1.0, 0.0)
        loads[0].wait()
        b["packed"][...] = dot(choose.astype(BF16), x_ref[...]).astype(BF16)
        arrive()

        def edge_block(start, size):
            if start == 0:
                return x_ref.at[0:48]
            if start == 48:
                return x_ref.at[80:128]
            return b["packed"].at[start - 96 : start - 96 + size]

        edges = exchange(edge_block, b["halo_x"])

        def norm(source, normed_ref, turned_ref):
            xf = source[...].astype(F32)
            inv_rms = lax.rsqrt(jnp.sum(xf * xf, -1, keepdims=True) * (1.0 / 512) + 1e-6)
            normed = xf * inv_rms * gain_ref[...]
            normed_ref[...] = normed.astype(BF16)
            for i in range(4):
                turned = normed[:, i * 128 : i * 128 + 128].T.astype(BF16)
                turned_ref[i] = turned.reshape(2, 64, turned.shape[1])
            return inv_rms

        def keys_values(normed_ref, uk_ref, nk_ref, kv_ref):
            normed = normed_ref[...]
            for i in range(4):
                lanes = slice(i * 128, i * 128 + 128)
                k_raw = dot(normed, wqkv_ref[:, 512 + i * 128 : 640 + i * 128])
                nk = lax.rsqrt(head_sum(k_raw * k_raw, ones) + 1e-6)
                uk = k_raw * nk
                nk_ref[:, lanes] = nk
                uk_ref[:, lanes] = uk
                kv_ref[:, lanes] = uk.astype(BF16)
            kv_ref[:, 512:1024] = dot(normed, wqkv_ref[:, 1024:1536]).astype(BF16)

        inv_rms = norm(x_ref, b["normed"], b["normed_t"])
        b["inv"][...] = jnp.broadcast_to(inv_rms, (128, 128))
        token = iota((128, 128), 0)
        b["mask"][...] = jnp.where(near(token >> 4, token & 15, (128, 128)), 1.0, 0.0)
        row, col, there = halo_place(iota((224, 128), 0))
        all_row, all_col = row + p.gy * 8, col + p.gx * 16
        there = there & (all_row >= 0) & (all_row < 8 * p.ngy) & (all_col >= 0) & (all_col < 16 * p.ngx)
        b["mask_h"][...] = jnp.where(there & near(row, col, (224, 128)), 1.0, 0.0)
        loads[1].wait()
        keys_values(b["normed"], b["uk"], b["nk"], b["kv"])
        loads[2].wait()
        loads[3].wait()
        for i in range(4):
            lanes = slice(i * 128, i * 128 + 128)
            q_raw = dot(b["normed"][...], wqkv_ref[:, lanes])
            nq = lax.rsqrt(head_sum(q_raw * q_raw, ones) + 1e-6)
            uq = q_raw * nq
            scale = jnp.where(low, scale_ref[2 * i], scale_ref[2 * i + 1])
            b["nq"][:, lanes] = nq * scale
            b["uq"][:, lanes] = uq
            b["qm"][i] = masked(uq * scale)
            b["gm"][i] = masked(dot(dy_ref[...], wout_ref[lanes, :], TURN))

        sums, mids = [], []
        for i in range(4):
            lanes, more = slice(i * 128, i * 128 + 128), slice(512 + i * 128, 640 + i * 128)
            e = jnp.exp(dot(b["kv"][:, lanes], b["qm"][i], TURN)) * twice(b["mask"][...])
            d = dot(b["kv"][:, more], b["gm"][i], TURN)
            b["e_l"][i] = e
            b["d_l"][i] = d
            sums.append(jnp.sum(e, 0, keepdims=True))
            mids.append(jnp.sum(e * d, 0, keepdims=True))
        for c in edges:
            c.wait_recv()

        norm(b["halo_x"], b["normed_h"], b["normed_th"])
        keys_values(b["normed_h"], b["uk_h"], b["nk_h"], b["halo"])

        def key_gradient(uk, nk, gku):
            return (nk * (gku - uk * head_sum(uk * gku, ones))).astype(BF16)

        for i in range(4):
            lanes, more = slice(i * 128, i * 128 + 128), slice(512 + i * 128, 640 + i * 128)
            e = jnp.exp(dot(b["halo"][:, lanes], b["qm"][i], TURN)) * twice(b["mask_h"][...])
            d = dot(b["halo"][:, more], b["gm"][i], TURN)
            inverse = 1.0 / (sums[i] + jnp.sum(e, 0, keepdims=True))
            mid = (mids[i] + jnp.sum(e * d, 0, keepdims=True)) * inverse
            probs_h = e * inverse
            ds_h = (probs_h * (d - mid)).astype(BF16)
            probs_h = probs_h.astype(BF16)
            probs = b["e_l"][i] * inverse
            ds = (probs * (b["d_l"][i] - mid)).astype(BF16)
            probs = probs.astype(BF16)
            b["p_h"][i] = probs_h
            b["ds_h"][i] = ds_h
            b["p_l"][i] = probs
            b["ds_l"][i] = ds
            att_t = pick(dot(b["kv"][:, more], probs, FIRST) + dot(b["halo"][:, more], probs_h, FIRST))
            gqs_t = pick(dot(b["kv"][:, lanes], ds, FIRST) + dot(b["halo"][:, lanes], ds_h, FIRST))
            b["att_t"][i] = att_t.astype(BF16).reshape(2, 64, 128)
            b["att"][:, lanes] = att_t.T.astype(BF16)
            gqs = gqs_t.T
            uq = b["uq"][:, lanes]
            b["act"][:, lanes] = (b["nq"][:, lanes] * (gqs - uq * head_sum(uq * gqs, ones))).astype(BF16)

        rows = 32 * ny

        def part_a(core):
            q_part = dot(b["normed_t"][:, core].reshape(rows, 128), b["act"][:, 0:512])
            out_part = dot(b["att_t"][:, core].reshape(rows, 128), dy_ref[...])
            return [
                jnp.concatenate(
                    [a[:, t * 128 : t * 128 + 128].reshape(ny, nx, 8, 128) for a in (q_part, out_part)], axis=2
                )
                for t in range(4)
            ]

        for t, tile in enumerate(part_a(1 - p.core)):
            b["s0a"][:, :, t] = tile.astype(BF16)
        first_a = links.start(b["s0a"], b["r0a"], p.other_core())
        for t, tile in enumerate(part_a(p.core)):
            b["own_a"][:, :, t] = tile

        for i in range(4):
            lanes, more = slice(i * 128, i * 128 + 128), slice(512 + i * 128, 640 + i * 128)
            b["act_h"][:, lanes] = key_gradient(b["uk_h"][:, lanes], b["nk_h"][:, lanes], dot(b["ds_h"][i], b["qm"][i]))
            b["act_h"][:, more] = dot(b["p_h"][i], b["gm"][i]).astype(BF16)
            b["act"][:, more] = key_gradient(b["uk"][:, lanes], b["nk"][:, lanes], dot(b["ds_l"][i], b["qm"][i]))
            b["act"][:, 1024 + i * 128 : 1152 + i * 128] = dot(b["p_l"][i], b["gm"][i]).astype(BF16)

        def part_b(core):
            a = dot(b["normed_t"][:, core].reshape(rows, 128), b["act"][:, 512:1536])
            a += dot(b["normed_th"][:, core].reshape(rows, 224), b["act_h"][...])
            return [a[:, t * 128 : t * 128 + 128].reshape(ny, 2, 16, 128) for t in range(8)]

        xs = start_a(p, links, b, first_a)
        for t, tile in enumerate(part_b(1 - p.core)):
            b["s0b"][:, :, t] = tile.astype(BF16)
        first_b = links.start(b["s0b"], b["r0b"], p.other_core())
        for t, tile in enumerate(part_b(p.core)):
            b["own_b"][:, :, t] = tile
        grads = []

        def send_grads():
            grads.extend(exchange(lambda start, size: b["gsend"].at[start : start + size], b["grecv"]))

        def meanwhile():
            b["gsend"][...] = dot(b["act_h"][...], wqkv_ref[:, 512:1536], TURN).astype(BF16)
            b["gn"][...] = dot(b["act"][...], wqkv_ref[...], TURN)
            mixed_ref[...] = (x_ref[...].astype(F32) + dot(b["att"][...], wout_ref[...])).astype(BF16)

        def finish():
            back = jnp.where(edge_tokens(iota((128, 128), 1)) == iota((128, 128), 0), 1.0, 0.0)
            for c in grads:
                c.wait_recv()
            grad_n = b["gn"][...] + dot(back.astype(BF16), b["grecv"][96:224, :])
            grad_n = jnp.concatenate(
                [
                    grad_n[0:48] + b["grecv"][0:48, :].astype(F32),
                    grad_n[48:80],
                    grad_n[80:128] + b["grecv"][48:96, :].astype(F32),
                ],
                axis=0,
            )
            g = grad_n * gain_ref[...]
            xf = x_ref[...].astype(F32)
            inv = b["inv"][:, 0:1]
            mean = jnp.sum(xf * g, -1, keepdims=True) * (1.0 / 512)
            gin_ref[...] = (dy_ref[...].astype(F32) + inv * g - xf * (inv * inv * inv * mean)).astype(BF16)

        reduce_tail(p, links, b, first_b, xs, owner_sems, meanwhile, send_grads, finish, factor, gqkv_ref, gout_ref)
        links.drain()

    vm, anywhere = pl.BlockSpec(memory_space=pltpu.VMEM), pl.BlockSpec(memory_space=pl.ANY)
    return pl.pallas_call(
        kernel,
        out_shape=(
            jax.ShapeDtypeStruct((128, 512), BF16),
            jax.ShapeDtypeStruct((128, 512), BF16),
            jax.ShapeDtypeStruct((8, 1536), F32),
            jax.ShapeDtypeStruct((8, 512), F32),
        ),
        in_specs=[anywhere, anywhere, vm, anywhere, anywhere, pl.BlockSpec(memory_space=pltpu.SMEM)],
        out_specs=(vm, vm, vm, vm),
        scratch_shapes=[scratch[n] for n in names]
        + [pltpu.SemaphoreType.DMA((count,)), pltpu.SemaphoreType.DMA((count,))]
        + [pltpu.SemaphoreType.DMA((4,)), pltpu.SemaphoreType.DMA((2,))],
        compiler_params=pltpu.CompilerParams(
            collective_id=1, has_side_effects=True, vmem_limit_bytes=56 * 1024 * 1024
        ),
        cost_estimate=pl.CostEstimate(flops=10**9, bytes_accessed=4 * 10**6, transcendentals=10**6),
        name="block",
    )(x, dy, gain, w_qkv, w_out, head_scale)


def hand_over(*arrays):
    count = len(arrays)

    def kernel(*refs):
        for i in range(count):
            refs[count + i][...] = refs[i][...]

    vm = pl.BlockSpec(memory_space=pltpu.VMEM)
    return pl.pallas_call(
        kernel,
        out_shape=tuple(jax.ShapeDtypeStruct(a.shape, a.dtype) for a in arrays),
        in_specs=[vm] * count,
        out_specs=(vm,) * count,
        name="hand_over",
    )(*arrays)


def per_device(inputs, cotangent, norm_gain, w_qkv, w_out, head_scale):
    shape, width = inputs.shape, inputs.shape[-1]
    tokens = shape[1] * shape[2]
    factor = 1.0 / math.sqrt(
        lax.axis_size("img") * lax.axis_size("gy") * lax.axis_size("gx") * tokens
    )
    results = block_call(
        inputs.reshape(tokens, width),
        cotangent.reshape(tokens, width),
        norm_gain.reshape(1, width),
        w_qkv,
        w_out,
        head_scale,
        factor,
    )
    mixed, grad_input, grad_qkv, grad_out = hand_over(*results)
    return (mixed.reshape(shape), grad_input.reshape(shape), grad_qkv, grad_out)


def solution(mesh):
    tokens, rows = P("img", "gy", "gx", None), P(("gy", "gx"), None)
    return jax.shard_map(
        per_device,
        mesh=mesh,
        in_specs=(tokens, tokens, P(), P(), P(), P()),
        out_specs=(tokens, tokens, rows, rows),
        check_vma=False,
    )
```

```python
import math

import jax
import jax.numpy as jnp
from jax import lax
from jax.experimental import pallas as pl
from jax.experimental.pallas import tpu as pltpu
from jax.sharding import PartitionSpec as P

F32, BF16 = jnp.float32, jnp.bfloat16


class Links:
    def __init__(self, send, recv):
        self.send, self.recv, self.used, self.all = send, recv, 0, []

    def start(self, src, dst, device):
        copy = pltpu.make_async_remote_copy(
            src_ref=src,
            dst_ref=dst,
            send_sem=self.send.at[self.used],
            recv_sem=self.recv.at[self.used],
            device_id=device,
            device_id_type=pl.DeviceIdType.MESH,
        )
        copy.start()
        self.used += 1
        self.all.append(copy)
        return copy

    def drain(self):
        for copy in self.all:
            copy.wait_send()


class Place:
    def __init__(self):
        gy, gx, self.z = lax.axis_index("gy"), lax.axis_index("gx"), lax.axis_index("img")
        self.gy, self.gx = gy, gx
        self.ngy, self.ngx, self.nz = (lax.axis_size(a) for a in ("gy", "gx", "img"))
        self.nx = self.ngx // 2
        self.ny = self.ngy
        self.core, self.x = gy % 2, gx % self.nx
        self.y = (gy // 2) * 2 + gx // self.nx

    def other_core(self):
        return (self.gy + 1 - 2 * self.core, self.gx, self.z)

    def x_peer(self, k):
        to = (self.x + k) % self.nx
        return to, (self.gy, self.gx - self.x + to, self.z)

    def y_peer(self, k):
        to = (self.y + k) % self.ny
        return to, ((to // 2) * 2 + self.core, (to % 2) * self.nx + self.x, self.z)

    def z_peer(self, k):
        to = (self.z + k) % self.nz
        return to, (self.gy, self.gx, to)

    def reduce_peers(self):
        return (
            [self.other_core()]
            + [self.x_peer(k)[1] for k in range(1, self.nx)]
            + [self.y_peer(k)[1] for k in range(1, self.ny)]
            + [self.z_peer(k)[1] for k in range(1, self.nz)]
        )


def enter(devices):
    barrier = pltpu.get_barrier_semaphore()
    for device in devices:
        pl.semaphore_signal(barrier, inc=1, device_id=device, device_id_type=pl.DeviceIdType.MESH)
    return lambda: pl.semaphore_wait(barrier, len(devices))


def reduce_scratch(nx, ny, nz):
    v = pltpu.VMEM
    return dict(
        r0a=v((ny, nx, 4, 16, 128), BF16),
        r0b=v((ny, 2, 8, 16, 128), BF16),
        s1a=v((ny, nx, 4, 16, 128), BF16),
        s1b=v((ny, 2, 8, 16, 128), BF16),
        rxa=v((nx - 1, ny, 4, 16, 128), BF16),
        s2a=v((ny, 4, 16, 128), BF16),
        rya=v((ny - 1, 4, 16, 128), BF16),
        za=v((nz, 4, 16, 128), BF16),
        ryb=v((ny - 1, 8, 16, 128), BF16),
        rzb=v((nz - 1, ny, 16, 128), BF16),
        syb=v((2, nz, 8, 128), F32),
        szb=v((2, ny, 8, 128), F32),
        mb=v((nx * nz, 8, 128), F32),
        gb=v((nz, 8, 128), F32),
    )


def reduce_count(nx, ny, nz):
    return 3 + 2 * (nx - 1) + 3 * (ny - 1) + 4 * (nz - 1)


def core_add(s1, own, got, tiles):
    def add(i, _):
        s1[i, :, tiles] = (own[i, :, tiles].astype(F32) + got[i, :, tiles].astype(F32)).astype(BF16)
        return 0

    lax.fori_loop(0, s1.shape[0], add, 0)


CHUNKS = (slice(0, 2), slice(2, 4))


def start_a(p, links, b, firsts):
    xs = []
    for first, tiles in zip(firsts, CHUNKS):
        first.wait_recv()
        core_add(b["s1a"], b["own_a"], b["r0a"], tiles)
        sent = []
        for k in range(1, p.nx):
            to, device = p.x_peer(k)
            sent.append(links.start(b["s1a"].at[:, to, tiles], b["rxa"].at[k - 1, :, tiles], device))
        xs.append(sent)
    return xs


def reduce_tail(p, links, b, first_b, first_a, owner_sems, meanwhile, send_grads, finish, factor, qkv_ref, out_ref):
    nx, ny, nz = p.nx, p.ny, p.nz
    first_b.wait_recv()
    core_add(b["s1b"], b["own_b"], b["r0b"], slice(0, 8))
    ys, zs = [], []
    for k in range(1, max(ny, nz)):
        if k < ny:
            to, device = p.y_peer(k)
            ys.append(links.start(b["s1b"].at[to, 0], b["ryb"].at[k - 1], device))
        if k < nz:
            to, device = p.z_peer(k)
            zs.append(links.start(b["s1b"].at[:, 1, to], b["rzb"].at[k - 1], device))
    xs = start_a(p, links, b, first_a)
    meanwhile()

    y2 = []
    for arriving, tiles in zip(xs, CHUNKS):
        for c in arriving:
            c.wait_recv()

        def add_x(i, _):
            total = b["s1a"][i, p.x, tiles].astype(F32)
            for k in range(nx - 1):
                total += b["rxa"][k, i, tiles].astype(F32)
            b["s2a"][i, tiles] = total.astype(BF16)
            return 0

        lax.fori_loop(0, ny, add_x, 0)
        sent = []
        for k in range(1, ny):
            to, device = p.y_peer(k)
            sent.append(links.start(b["s2a"].at[to, tiles], b["rya"].at[k - 1, tiles], device))
        y2.append(sent)

    for c in ys:
        c.wait_recv()

    def add_y(i, _):
        total = b["s1b"][p.y, 0, i].astype(F32)
        for k in range(ny - 1):
            total += b["ryb"][k, i].astype(F32)
        b["syb"][0, i] = total[0:8]
        b["syb"][1, i] = total[8:16]
        return 0

    lax.fori_loop(0, nz, add_y, 0)

    def to_owner(tile, slot, device):
        return pltpu.make_async_remote_copy(
            src_ref=tile,
            dst_ref=b["mb"].at[slot],
            send_sem=owner_sems.at[0],
            recv_sem=owner_sems.at[1],
            device_id=device,
            device_id_type=pl.DeviceIdType.MESH,
        )

    def spread(tiles, first, peers, mine):
        for j in range(2):
            column = p.gx - p.x + first + j
            for k in range(peers):
                if first == 0:
                    to, device = p.z_peer(k)
                    device = (p.gy, column, device[2])
                else:
                    to, device = p.y_peer(k)
                    device = (device[0], device[1] - p.x + first + j, p.z)
                copy = to_owner(tiles.at[j, to], p.x * peers + mine, device)
                if k > 0:
                    copy.start()
                else:
                    pl.when(p.x != first + j)(copy.start)

    spread(b["syb"], 0, nz, p.z)

    for c in zs:
        c.wait_recv()

    def add_z(i, _):
        total = b["s1b"][i, 1, p.z].astype(F32)
        for k in range(nz - 1):
            total += b["rzb"][k, i].astype(F32)
        b["szb"][0, i] = total[0:8]
        b["szb"][1, i] = total[8:16]
        return 0

    lax.fori_loop(0, ny, add_z, 0)
    spread(b["szb"], 2, ny, p.y)

    @pl.when(p.x < 2)
    def _():
        b["mb"][p.x * nz + p.z] = b["syb"][p.x % 2, p.z]

    @pl.when(p.x >= 2)
    def _():
        b["mb"][p.x * ny + p.y] = b["szb"][p.x % 2, p.y]

    send_grads()

    last_a = []
    for arriving, tiles in zip(y2, CHUNKS):
        for c in arriving:
            c.wait_recv()
        total = b["s2a"][p.y, tiles].astype(F32)
        for k in range(ny - 1):
            total += b["rya"][k, tiles].astype(F32)
        b["za"][p.z, tiles] = total.astype(BF16)
        for k in range(1, nz):
            to, device = p.z_peer(k)
            last_a.append(links.start(b["za"].at[p.z, tiles], b["za"].at[p.z, tiles], device))

    others = b["mb"].at[0 : nx * nz - 1]
    pltpu.make_async_copy(others, others, owner_sems.at[1]).wait()
    total = jnp.sum(b["mb"][...], axis=0)
    b["gb"][p.z] = total * factor
    last = []
    for k in range(1, nz):
        to, device = p.z_peer(k)
        last.append(links.start(b["gb"].at[p.z], b["gb"].at[p.z], device))
    finish()
    for c in last_a:
        c.wait_recv()
    total = b["za"][0].astype(F32)
    for z in range(1, nz):
        total += b["za"][z].astype(F32)
    total = total * factor
    for t in range(4):
        qkv_ref[:, t * 128 : t * 128 + 128] = total[t, 0:8]
        out_ref[:, t * 128 : t * 128 + 128] = total[t, 8:16]
    for c in last:
        c.wait_recv()
    pltpu.make_async_copy(others, others, owner_sems.at[0]).wait()
    for t in range(8):
        qkv_ref[:, 512 + t * 128 : 640 + t * 128] = b["gb"][t]


def dot(a, b, dims=((1,), (0,))):
    return lax.dot_general(a, b, (dims, ((), ())), preferred_element_type=F32)


TURN = ((1,), (1,))
FIRST = ((0,), (0,))


def iota(shape, dim):
    return lax.broadcasted_iota(jnp.int32, shape, dim)


def edge_tokens(j):
    side = j & 31
    side_token = jnp.where((side >> 3) < 3, (side & 7) * 16 + (side >> 3) + 13 * ((j >> 5) & 1), -1)
    corner = (j - 64) >> 4
    down, across = (j >> 2) & 3, j & 3
    token = (down + 5 * (corner >> 1)) * 16 + across + 13 * (corner & 1)
    corner_token = jnp.where((down < 3) & (across < 3), token, -1)
    return jnp.where(j < 64, side_token, corner_token)


def halo_place(j):
    row = jnp.where(j < 48, (j >> 4) - 3, (j >> 4) + 5)
    col = j & 15
    side = j & 31
    is_side = (j >= 96) & (j < 160)
    row = jnp.where(is_side, side & 7, row)
    col = jnp.where(is_side, (side >> 3) + jnp.where(j < 128, -3, 16), col)
    corner = (j - 160) >> 4
    down, across = (j >> 2) & 3, j & 3
    is_corner = j >= 160
    row = jnp.where(is_corner, down + jnp.where(corner < 2, -3, 8), row)
    col = jnp.where(is_corner, across + jnp.where((corner & 1) == 0, -3, 16), col)
    filled = jnp.where(is_side, side >> 3, jnp.where(is_corner, jnp.maximum(down, across), 0))
    return row, col, filled < 3


def near(row, col, shape):
    query = iota(shape, 1)
    return (jnp.abs(row - (query >> 4)) <= 3) & (jnp.abs(col - (query & 15)) <= 3)


def twice(a):
    return jnp.concatenate([a, a], axis=1)


def head_sum(a, ones):
    top = a.astype(BF16)
    rest = (a - top.astype(F32)).astype(BF16)
    return dot(top, ones) + dot(rest, ones)


def pick(a):
    return jnp.concatenate([a[0:64, 0:128], a[64:128, 128:256]], axis=0)


BLOCKS = (
    (0, 48, 48, -1, 0),
    (48, 48, 0, 1, 0),
    (96, 32, 128, 0, -1),
    (128, 32, 96, 0, 1),
    (160, 16, 208, -1, -1),
    (176, 16, 192, -1, 1),
    (192, 16, 176, 1, -1),
    (208, 16, 160, 1, 1),
)


def block_call(x, dy, gain, w_qkv, w_out, head_scale, factor):
    nx, ny, nz = lax.axis_size("gx") // 2, lax.axis_size("gy"), lax.axis_size("img")
    v = pltpu.VMEM
    scratch = reduce_scratch(nx, ny, nz)
    scratch.update(
        own_a=v((ny, nx, 4, 16, 128), F32),
        own_b=v((ny, 2, 8, 16, 128), F32),
        s0a=v((ny, nx, 4, 16, 128), BF16),
        s0b=v((ny, 2, 8, 16, 128), BF16),
        normed=v((128, 512), BF16),
        normed_h=v((224, 512), BF16),
        normed_t=v((ny // 2, 2, 64, 128), BF16),
        uq=v((128, 512), F32),
        uk=v((128, 512), F32),
        nq=v((128, 512), F32),
        nk=v((128, 512), F32),
        x=v((128, 512), BF16),
        dy=v((128, 512), BF16),
        wqkv=v((512, 1536), BF16),
        wout=v((512, 512), BF16),
        kv=v((128, 1024), BF16),
        packed=v((128, 512), BF16),
        halo_x=v((224, 512), BF16),
        halo=v((224, 1024), BF16),
        uk_h=v((224, 512), F32),
        nk_h=v((224, 512), F32),
        normed_th=v((ny // 2, 2, 64, 224), BF16),
        act_h=v((224, 1024), BF16),
        qm=v((4, 256, 128), BF16),
        gm=v((4, 256, 128), BF16),
        mask=v((128, 128), F32),
        mask_h=v((224, 128), F32),
        e_l=v((4, 128, 256), F32),
        d_l=v((4, 128, 256), F32),
        p_h=v((4, 224, 256), BF16),
        p_l=v((4, 128, 256), BF16),
        ds_l=v((4, 128, 256), BF16),
        ds_h=v((4, 224, 256), BF16),
        gsend=v((224, 512), BF16),
        gn=v((128, 512), F32),
        grecv=v((224, 512), BF16),
        att=v((128, 512), BF16),
        att_t=v((ny // 2, 2, 64, 128), BF16),
        act=v((128, 1536), BF16),
        inv=v((128, 128), F32),
    )
    names = list(scratch)
    count = reduce_count(nx, ny, nz) + 16

    def kernel(x_hbm, dy_hbm, gain_ref, wqkv_hbm, wout_hbm, scale_ref, mixed_ref, gin_ref, gqkv_ref, gout_ref, *rest):
        b = dict(zip(names, rest))
        links = Links(*rest[len(names) : len(names) + 2])
        load_sem, owner_sems = rest[len(names) + 2 :]
        x_ref, dy_ref, wqkv_ref, wout_ref = b["x"], b["dy"], b["wqkv"], b["wout"]
        loads = [
            pltpu.make_async_copy(source, target, load_sem.at[i])
            for i, (source, target) in enumerate(
                ((x_hbm, x_ref), (wqkv_hbm, wqkv_ref), (dy_hbm, dy_ref), (wout_hbm, wout_ref))
            )
        ]
        for c in loads:
            c.start()
        p = Place()

        def neighbour(dy_step, dx_step):
            return ((p.gy + dy_step) % p.ngy, (p.gx + dx_step) % p.ngx, p.z)

        arrive = enter([neighbour(*block[3:]) for block in BLOCKS] + p.reduce_peers())

        def exchange(source, target):
            return [
                links.start(source(start, size), target.at[land : land + size], neighbour(*step))
                for start, size, land, *step in BLOCKS
            ]

        low = iota((128, 128), 1) < 64
        ones = jnp.where((iota((128, 128), 0) < 64) == low, 1.0, 0.0).astype(BF16)

        def masked(a):
            zero = jnp.zeros_like(a)
            return jnp.concatenate([jnp.where(low, a, zero), jnp.where(low, zero, a)], axis=0).astype(BF16)

        choose = jnp.where(edge_tokens(iota((128, 128), 0)) == iota((128, 128), 1), 1.0, 0.0)
        loads[0].wait()
        b["packed"][...] = dot(choose.astype(BF16), x_ref[...]).astype(BF16)
        arrive()

        def edge_block(start, size):
            if start == 0:
                return x_ref.at[0:48]
            if start == 48:
                return x_ref.at[80:128]
            return b["packed"].at[start - 96 : start - 96 + size]

        edges = exchange(edge_block, b["halo_x"])

        def norm(source, normed_ref, turned_ref):
            xf = source[...].astype(F32)
            inv_rms = lax.rsqrt(jnp.sum(xf * xf, -1, keepdims=True) * (1.0 / 512) + 1e-6)
            normed = xf * inv_rms * gain_ref[...]
            normed_ref[...] = normed.astype(BF16)
            for i in range(4):
                turned = normed[:, i * 128 : i * 128 + 128].T.astype(BF16)
                turned_ref[i] = turned.reshape(2, 64, turned.shape[1])
            return inv_rms

        def keys_values(normed_ref, uk_ref, nk_ref, kv_ref):
            normed = normed_ref[...]
            for i in range(4):
                lanes = slice(i * 128, i * 128 + 128)
                k_raw = dot(normed, wqkv_ref[:, 512 + i * 128 : 640 + i * 128])
                nk = lax.rsqrt(head_sum(k_raw * k_raw, ones) + 1e-6)
                uk = k_raw * nk
                nk_ref[:, lanes] = nk
                uk_ref[:, lanes] = uk
                kv_ref[:, lanes] = uk.astype(BF16)
            kv_ref[:, 512:1024] = dot(normed, wqkv_ref[:, 1024:1536]).astype(BF16)

        inv_rms = norm(x_ref, b["normed"], b["normed_t"])
        b["inv"][...] = jnp.broadcast_to(inv_rms, (128, 128))
        token = iota((128, 128), 0)
        b["mask"][...] = jnp.where(near(token >> 4, token & 15, (128, 128)), 1.0, 0.0)
        row, col, there = halo_place(iota((224, 128), 0))
        all_row, all_col = row + p.gy * 8, col + p.gx * 16
        there = there & (all_row >= 0) & (all_row < 8 * p.ngy) & (all_col >= 0) & (all_col < 16 * p.ngx)
        b["mask_h"][...] = jnp.where(there & near(row, col, (224, 128)), 1.0, 0.0)
        loads[1].wait()
        keys_values(b["normed"], b["uk"], b["nk"], b["kv"])
        loads[2].wait()
        loads[3].wait()
        for i in range(4):
            lanes = slice(i * 128, i * 128 + 128)
            q_raw = dot(b["normed"][...], wqkv_ref[:, lanes])
            nq = lax.rsqrt(head_sum(q_raw * q_raw, ones) + 1e-6)
            uq = q_raw * nq
            scale = jnp.where(low, scale_ref[2 * i], scale_ref[2 * i + 1])
            b["nq"][:, lanes] = nq * scale
            b["uq"][:, lanes] = uq
            b["qm"][i] = masked(uq * scale)
            b["gm"][i] = masked(dot(dy_ref[...], wout_ref[lanes, :], TURN))

        sums, mids = [], []
        for i in range(4):
            lanes, more = slice(i * 128, i * 128 + 128), slice(512 + i * 128, 640 + i * 128)
            e = jnp.exp(dot(b["kv"][:, lanes], b["qm"][i], TURN)) * twice(b["mask"][...])
            d = dot(b["kv"][:, more], b["gm"][i], TURN)
            b["e_l"][i] = e
            b["d_l"][i] = d
            sums.append(jnp.sum(e, 0, keepdims=True))
            mids.append(jnp.sum(e * d, 0, keepdims=True))
        for c in edges:
            c.wait_recv()

        norm(b["halo_x"], b["normed_h"], b["normed_th"])
        keys_values(b["normed_h"], b["uk_h"], b["nk_h"], b["halo"])

        def key_gradient(uk, nk, gku):
            return (nk * (gku - uk * head_sum(uk * gku, ones))).astype(BF16)

        for i in range(4):
            lanes, more = slice(i * 128, i * 128 + 128), slice(512 + i * 128, 640 + i * 128)
            e = jnp.exp(dot(b["halo"][:, lanes], b["qm"][i], TURN)) * twice(b["mask_h"][...])
            d = dot(b["halo"][:, more], b["gm"][i], TURN)
            inverse = 1.0 / (sums[i] + jnp.sum(e, 0, keepdims=True))
            mid = (mids[i] + jnp.sum(e * d, 0, keepdims=True)) * inverse
            probs_h = e * inverse
            ds_h = (probs_h * (d - mid)).astype(BF16)
            probs_h = probs_h.astype(BF16)
            probs = b["e_l"][i] * inverse
            ds = (probs * (b["d_l"][i] - mid)).astype(BF16)
            probs = probs.astype(BF16)
            b["p_h"][i] = probs_h
            b["ds_h"][i] = ds_h
            b["p_l"][i] = probs
            b["ds_l"][i] = ds

        rows = 32 * ny

        for i in range(4):
            lanes, more = slice(i * 128, i * 128 + 128), slice(512 + i * 128, 640 + i * 128)
            b["act_h"][:, lanes] = key_gradient(b["uk_h"][:, lanes], b["nk_h"][:, lanes], dot(b["ds_h"][i], b["qm"][i]))
            b["act_h"][:, more] = dot(b["p_h"][i], b["gm"][i]).astype(BF16)
            b["act"][:, more] = key_gradient(b["uk"][:, lanes], b["nk"][:, lanes], dot(b["ds_l"][i], b["qm"][i]))
            b["act"][:, 1024 + i * 128 : 1152 + i * 128] = dot(b["p_l"][i], b["gm"][i]).astype(BF16)

        def part_b(core):
            a = dot(b["normed_t"][:, core].reshape(rows, 128), b["act"][:, 512:1536])
            a += dot(b["normed_th"][:, core].reshape(rows, 224), b["act_h"][...])
            return [a[:, t * 128 : t * 128 + 128].reshape(ny, 2, 16, 128) for t in range(8)]

        for t, tile in enumerate(part_b(1 - p.core)):
            b["s0b"][:, :, t] = tile.astype(BF16)
        first_b = links.start(b["s0b"], b["r0b"], p.other_core())
        for t, tile in enumerate(part_b(p.core)):
            b["own_b"][:, :, t] = tile

        for i in range(4):
            lanes, more = slice(i * 128, i * 128 + 128), slice(512 + i * 128, 640 + i * 128)
            att_t = pick(dot(b["kv"][:, more], b["p_l"][i], FIRST) + dot(b["halo"][:, more], b["p_h"][i], FIRST))
            gqs_t = pick(dot(b["kv"][:, lanes], b["ds_l"][i], FIRST) + dot(b["halo"][:, lanes], b["ds_h"][i], FIRST))
            b["att_t"][i] = att_t.astype(BF16).reshape(2, 64, 128)
            b["att"][:, lanes] = att_t.T.astype(BF16)
            gqs = gqs_t.T
            uq = b["uq"][:, lanes]
            b["act"][:, lanes] = (b["nq"][:, lanes] * (gqs - uq * head_sum(uq * gqs, ones))).astype(BF16)

        def part_a(core, tiles):
            lanes = slice(tiles.start * 128, tiles.stop * 128)
            q_part = dot(b["normed_t"][:, core].reshape(rows, 128), b["act"][:, lanes])
            out_part = dot(b["att_t"][:, core].reshape(rows, 128), dy_ref[:, lanes])
            return [
                jnp.concatenate(
                    [a[:, t * 128 : t * 128 + 128].reshape(ny, nx, 8, 128) for a in (q_part, out_part)], axis=2
                )
                for t in range(tiles.stop - tiles.start)
            ]

        first_a = []
        for tiles in CHUNKS:
            for t, tile in enumerate(part_a(1 - p.core, tiles)):
                b["s0a"][:, :, tiles.start + t] = tile.astype(BF16)
            first_a.append(links.start(b["s0a"].at[:, :, tiles], b["r0a"].at[:, :, tiles], p.other_core()))
        for tiles in CHUNKS:
            for t, tile in enumerate(part_a(p.core, tiles)):
                b["own_a"][:, :, tiles.start + t] = tile

        grads = []

        def send_grads():
            grads.extend(exchange(lambda start, size: b["gsend"].at[start : start + size], b["grecv"]))

        def meanwhile():
            b["gsend"][...] = dot(b["act_h"][...], wqkv_ref[:, 512:1536], TURN).astype(BF16)
            b["gn"][...] = dot(b["act"][...], wqkv_ref[...], TURN)
            mixed_ref[...] = (x_ref[...].astype(F32) + dot(b["att"][...], wout_ref[...])).astype(BF16)

        def finish():
            back = jnp.where(edge_tokens(iota((128, 128), 1)) == iota((128, 128), 0), 1.0, 0.0)
            for c in grads:
                c.wait_recv()
            grad_n = b["gn"][...] + dot(back.astype(BF16), b["grecv"][96:224, :])
            grad_n = jnp.concatenate(
                [
                    grad_n[0:48] + b["grecv"][0:48, :].astype(F32),
                    grad_n[48:80],
                    grad_n[80:128] + b["grecv"][48:96, :].astype(F32),
                ],
                axis=0,
            )
            g = grad_n * gain_ref[...]
            xf = x_ref[...].astype(F32)
            inv = b["inv"][:, 0:1]
            mean = jnp.sum(xf * g, -1, keepdims=True) * (1.0 / 512)
            gin_ref[...] = (dy_ref[...].astype(F32) + inv * g - xf * (inv * inv * inv * mean)).astype(BF16)

        reduce_tail(p, links, b, first_b, first_a, owner_sems, meanwhile, send_grads, finish, factor, gqkv_ref, gout_ref)
        links.drain()

    vm, anywhere = pl.BlockSpec(memory_space=pltpu.VMEM), pl.BlockSpec(memory_space=pl.ANY)
    return pl.pallas_call(
        kernel,
        out_shape=(
            jax.ShapeDtypeStruct((128, 512), BF16),
            jax.ShapeDtypeStruct((128, 512), BF16),
            jax.ShapeDtypeStruct((8, 1536), F32),
            jax.ShapeDtypeStruct((8, 512), F32),
        ),
        in_specs=[anywhere, anywhere, vm, anywhere, anywhere, pl.BlockSpec(memory_space=pltpu.SMEM)],
        out_specs=(vm, vm, vm, vm),
        scratch_shapes=[scratch[n] for n in names]
        + [pltpu.SemaphoreType.DMA((count,)), pltpu.SemaphoreType.DMA((count,))]
        + [pltpu.SemaphoreType.DMA((4,)), pltpu.SemaphoreType.DMA((2,))],
        compiler_params=pltpu.CompilerParams(
            collective_id=1, has_side_effects=True, vmem_limit_bytes=56 * 1024 * 1024
        ),
        cost_estimate=pl.CostEstimate(flops=10**9, bytes_accessed=4 * 10**6, transcendentals=10**6),
        name="block",
    )(x, dy, gain, w_qkv, w_out, head_scale)


def hand_over(*arrays):
    count = len(arrays)

    def kernel(*refs):
        for i in range(count):
            refs[count + i][...] = refs[i][...]

    vm = pl.BlockSpec(memory_space=pltpu.VMEM)
    return pl.pallas_call(
        kernel,
        out_shape=tuple(jax.ShapeDtypeStruct(a.shape, a.dtype) for a in arrays),
        in_specs=[vm] * count,
        out_specs=(vm,) * count,
        name="hand_over",
    )(*arrays)


def per_device(inputs, cotangent, norm_gain, w_qkv, w_out, head_scale):
    shape, width = inputs.shape, inputs.shape[-1]
    tokens = shape[1] * shape[2]
    factor = 1.0 / math.sqrt(
        lax.axis_size("img") * lax.axis_size("gy") * lax.axis_size("gx") * tokens
    )
    results = block_call(
        inputs.reshape(tokens, width),
        cotangent.reshape(tokens, width),
        norm_gain.reshape(1, width),
        w_qkv,
        w_out,
        head_scale,
        factor,
    )
    mixed, grad_input, grad_qkv, grad_out = hand_over(*results)
    return (mixed.reshape(shape), grad_input.reshape(shape), grad_qkv, grad_out)


def solution(mesh):
    tokens, rows = P("img", "gy", "gx", None), P(("gy", "gx"), None)
    return jax.shard_map(
        per_device,
        mesh=mesh,
        in_specs=(tokens, tokens, P(), P(), P(), P()),
        out_specs=(tokens, tokens, rows, rows),
        check_vma=False,
    )
```

```python
import math

import jax
import jax.numpy as jnp
from jax import lax
from jax.experimental import pallas as pl
from jax.experimental.pallas import tpu as pltpu
from jax.sharding import PartitionSpec as P

F32, BF16 = jnp.float32, jnp.bfloat16


class Links:
    def __init__(self, send, recv):
        self.send, self.recv, self.used, self.all = send, recv, 0, []

    def start(self, src, dst, device):
        copy = pltpu.make_async_remote_copy(
            src_ref=src,
            dst_ref=dst,
            send_sem=self.send.at[self.used],
            recv_sem=self.recv.at[self.used],
            device_id=device,
            device_id_type=pl.DeviceIdType.MESH,
        )
        copy.start()
        self.used += 1
        self.all.append(copy)
        return copy

    def drain(self):
        for copy in self.all:
            copy.wait_send()


class Place:
    def __init__(self):
        gy, gx, self.z = lax.axis_index("gy"), lax.axis_index("gx"), lax.axis_index("img")
        self.gy, self.gx = gy, gx
        self.ngy, self.ngx, self.nz = (lax.axis_size(a) for a in ("gy", "gx", "img"))
        self.nx = self.ngx // 2
        self.ny = self.ngy
        self.core, self.x = gy % 2, gx % self.nx
        self.y = (gy // 2) * 2 + gx // self.nx

    def other_core(self):
        return (self.gy + 1 - 2 * self.core, self.gx, self.z)

    def x_peer(self, k):
        to = (self.x + k) % self.nx
        return to, (self.gy, self.gx - self.x + to, self.z)

    def y_peer(self, k):
        to = (self.y + k) % self.ny
        return to, ((to // 2) * 2 + self.core, (to % 2) * self.nx + self.x, self.z)

    def z_peer(self, k):
        to = (self.z + k) % self.nz
        return to, (self.gy, self.gx, to)

    def reduce_peers(self):
        return (
            [self.other_core()]
            + [self.x_peer(k)[1] for k in range(1, self.nx)]
            + [self.y_peer(k)[1] for k in range(1, self.ny)]
            + [self.z_peer(k)[1] for k in range(1, self.nz)]
        )


def enter(devices):
    barrier = pltpu.get_barrier_semaphore()
    for device in devices:
        pl.semaphore_signal(barrier, inc=1, device_id=device, device_id_type=pl.DeviceIdType.MESH)
    return lambda: pl.semaphore_wait(barrier, len(devices))


def reduce_scratch(nx, ny, nz):
    v = pltpu.VMEM
    return dict(
        r0a=v((ny, nx, 4, 16, 128), BF16),
        r0b=v((ny, 2, 8, 16, 128), BF16),
        s1a=v((ny, nx, 4, 16, 128), BF16),
        s1b=v((ny, 2, 8, 16, 128), BF16),
        rxa=v((nx - 1, ny, 4, 16, 128), BF16),
        s2a=v((ny, 4, 16, 128), BF16),
        rya=v((ny - 1, 4, 16, 128), BF16),
        za=v((nz, 4, 16, 128), BF16),
        ryb=v((ny - 1, 8, 16, 128), BF16),
        rzb=v((nz - 1, ny, 16, 128), BF16),
        syb=v((2, nz, 8, 128), F32),
        szb=v((2, ny, 8, 128), F32),
        mb=v((nx * nz, 8, 128), F32),
        gb=v((nz, 8, 128), F32),
    )


def reduce_count(nx, ny, nz):
    return 4 + 2 * (nx - 1) + 3 * (ny - 1) + 4 * (nz - 1)


def core_add(s1, own, got, tiles):
    def add(i, _):
        s1[i, :, tiles] = (own[i, :, tiles].astype(F32) + got[i, :, tiles].astype(F32)).astype(BF16)
        return 0

    lax.fori_loop(0, s1.shape[0], add, 0)


CHUNKS = (slice(0, 2), slice(2, 4))
HALVES = (slice(4, 8), slice(0, 4))


def start_a(p, links, b, firsts):
    xs = []
    for first, tiles in zip(firsts, CHUNKS):
        first.wait_recv()
        core_add(b["s1a"], b["own_a"], b["r0a"], tiles)
        sent = []
        for k in far_first(p.nx):
            to, device = p.x_peer(k)
            sent.append(links.start(b["s1a"].at[:, to, tiles], b["rxa"].at[k - 1, :, tiles], device))
        xs.append(sent)
    return xs


def far_first(n):
    return sorted(range(1, n), key=lambda k: -min(k, n - k))


def start_b(p, links, b, firsts):
    for first, tiles in zip(firsts, HALVES):
        first.wait_recv()
        core_add(b["s1b"], b["own_b"], b["r0b"], tiles)
    ys, zs = [], []
    for k in far_first(p.ny):
        to, device = p.y_peer(k)
        ys.append(links.start(b["s1b"].at[to, 0], b["ryb"].at[k - 1], device))
        to, device = p.z_peer(k)
        zs.append(links.start(b["s1b"].at[:, 1, to], b["rzb"].at[k - 1], device))
    return ys, zs


def reduce_tail(p, links, b, ys, zs, first_a, owner_sems, meanwhile, send_grads, finish, factor, qkv_ref, out_ref):
    nx, ny, nz = p.nx, p.ny, p.nz
    xs = start_a(p, links, b, first_a)
    meanwhile()

    y2 = []
    for arriving, tiles in zip(xs, CHUNKS):
        for c in arriving:
            c.wait_recv()

        def add_x(i, _):
            total = b["s1a"][i, p.x, tiles].astype(F32)
            for k in range(nx - 1):
                total += b["rxa"][k, i, tiles].astype(F32)
            b["s2a"][i, tiles] = total.astype(BF16)
            return 0

        lax.fori_loop(0, ny, add_x, 0)
        sent = []
        for k in far_first(ny):
            to, device = p.y_peer(k)
            sent.append(links.start(b["s2a"].at[to, tiles], b["rya"].at[k - 1, tiles], device))
        y2.append(sent)

    for c in ys:
        c.wait_recv()

    def add_y(i, _):
        total = b["s1b"][p.y, 0, i].astype(F32)
        for k in range(ny - 1):
            total += b["ryb"][k, i].astype(F32)
        b["syb"][0, i] = total[0:8]
        b["syb"][1, i] = total[8:16]
        return 0

    lax.fori_loop(0, nz, add_y, 0)

    def to_owner(tile, slot, device):
        return pltpu.make_async_remote_copy(
            src_ref=tile,
            dst_ref=b["mb"].at[slot],
            send_sem=owner_sems.at[0],
            recv_sem=owner_sems.at[1],
            device_id=device,
            device_id_type=pl.DeviceIdType.MESH,
        )

    def spread(tiles, first, peers, mine):
        for j in range(2):
            column = p.gx - p.x + first + j
            for k in far_first(peers) + [0]:
                if first == 0:
                    to, device = p.z_peer(k)
                    device = (p.gy, column, device[2])
                else:
                    to, device = p.y_peer(k)
                    device = (device[0], device[1] - p.x + first + j, p.z)
                copy = to_owner(tiles.at[j, to], p.x * peers + mine, device)
                if k > 0:
                    copy.start()
                else:
                    pl.when(p.x != first + j)(copy.start)

    spread(b["syb"], 0, nz, p.z)

    for c in zs:
        c.wait_recv()

    def add_z(i, _):
        total = b["s1b"][i, 1, p.z].astype(F32)
        for k in range(nz - 1):
            total += b["rzb"][k, i].astype(F32)
        b["szb"][0, i] = total[0:8]
        b["szb"][1, i] = total[8:16]
        return 0

    lax.fori_loop(0, ny, add_z, 0)
    spread(b["szb"], 2, ny, p.y)

    @pl.when(p.x < 2)
    def _():
        b["mb"][p.x * nz + p.z] = b["syb"][p.x % 2, p.z]

    @pl.when(p.x >= 2)
    def _():
        b["mb"][p.x * ny + p.y] = b["szb"][p.x % 2, p.y]

    send_grads()

    last_a = []
    for arriving, tiles in zip(y2, CHUNKS):
        for c in arriving:
            c.wait_recv()
        total = b["s2a"][p.y, tiles].astype(F32)
        for k in range(ny - 1):
            total += b["rya"][k, tiles].astype(F32)
        b["za"][p.z, tiles] = total.astype(BF16)
        for k in far_first(nz):
            to, device = p.z_peer(k)
            last_a.append(links.start(b["za"].at[p.z, tiles], b["za"].at[p.z, tiles], device))

    others = b["mb"].at[0 : nx * nz - 1]
    pltpu.make_async_copy(others, others, owner_sems.at[1]).wait()
    total = jnp.sum(b["mb"][...], axis=0)
    b["gb"][p.z] = total * factor
    last = []
    for k in far_first(nz):
        to, device = p.z_peer(k)
        last.append(links.start(b["gb"].at[p.z], b["gb"].at[p.z], device))
    finish()
    for c in last_a:
        c.wait_recv()
    total = b["za"][0].astype(F32)
    for z in range(1, nz):
        total += b["za"][z].astype(F32)
    total = total * factor
    for t in range(4):
        qkv_ref[:, t * 128 : t * 128 + 128] = total[t, 0:8]
        out_ref[:, t * 128 : t * 128 + 128] = total[t, 8:16]
    for c in last:
        c.wait_recv()
    pltpu.make_async_copy(others, others, owner_sems.at[0]).wait()
    for t in range(8):
        qkv_ref[:, 512 + t * 128 : 640 + t * 128] = b["gb"][t]


def dot(a, b, dims=((1,), (0,))):
    return lax.dot_general(a, b, (dims, ((), ())), preferred_element_type=F32)


TURN = ((1,), (1,))
FIRST = ((0,), (0,))


def iota(shape, dim):
    return lax.broadcasted_iota(jnp.int32, shape, dim)


def edge_tokens(j):
    side = j & 31
    side_token = jnp.where((side >> 3) < 3, (side & 7) * 16 + (side >> 3) + 13 * ((j >> 5) & 1), -1)
    corner = (j - 64) >> 4
    down, across = (j >> 2) & 3, j & 3
    token = (down + 5 * (corner >> 1)) * 16 + across + 13 * (corner & 1)
    corner_token = jnp.where((down < 3) & (across < 3), token, -1)
    return jnp.where(j < 64, side_token, corner_token)


def halo_place(j):
    row = jnp.where(j < 48, (j >> 4) - 3, (j >> 4) + 5)
    col = j & 15
    side = j & 31
    is_side = (j >= 96) & (j < 160)
    row = jnp.where(is_side, side & 7, row)
    col = jnp.where(is_side, (side >> 3) + jnp.where(j < 128, -3, 16), col)
    corner = (j - 160) >> 4
    down, across = (j >> 2) & 3, j & 3
    is_corner = j >= 160
    row = jnp.where(is_corner, down + jnp.where(corner < 2, -3, 8), row)
    col = jnp.where(is_corner, across + jnp.where((corner & 1) == 0, -3, 16), col)
    filled = jnp.where(is_side, side >> 3, jnp.where(is_corner, jnp.maximum(down, across), 0))
    return row, col, filled < 3


def near(row, col, shape):
    query = iota(shape, 1)
    return (jnp.abs(row - (query >> 4)) <= 3) & (jnp.abs(col - (query & 15)) <= 3)


def twice(a):
    return jnp.concatenate([a, a], axis=1)


def head_sum(a, ones):
    top = a.astype(BF16)
    rest = (a - top.astype(F32)).astype(BF16)
    return dot(top, ones) + dot(rest, ones)


def pick(a):
    return jnp.concatenate([a[0:64, 0:128], a[64:128, 128:256]], axis=0)


BLOCKS = (
    (0, 48, 48, -1, 0),
    (48, 48, 0, 1, 0),
    (96, 32, 128, 0, -1),
    (128, 32, 96, 0, 1),
    (160, 16, 208, -1, -1),
    (176, 16, 192, -1, 1),
    (192, 16, 176, 1, -1),
    (208, 16, 160, 1, 1),
)


def block_call(x, dy, gain, w_qkv, w_out, head_scale, factor):
    nx, ny, nz = lax.axis_size("gx") // 2, lax.axis_size("gy"), lax.axis_size("img")
    v = pltpu.VMEM
    scratch = reduce_scratch(nx, ny, nz)
    scratch.update(
        own_a=v((ny, nx, 4, 16, 128), F32),
        own_b=v((ny, 2, 8, 16, 128), F32),
        s0a=v((ny, nx, 4, 16, 128), BF16),
        s0b=v((ny, 2, 8, 16, 128), BF16),
        normed=v((128, 512), BF16),
        normed_h=v((224, 512), BF16),
        normed_t=v((ny // 2, 2, 64, 128), BF16),
        uq=v((128, 512), F32),
        uk=v((128, 512), F32),
        nq=v((128, 512), F32),
        nk=v((128, 512), F32),
        x=v((128, 512), BF16),
        dy=v((128, 512), BF16),
        wqkv=v((512, 1536), BF16),
        wout=v((512, 512), BF16),
        kv=v((128, 1024), BF16),
        packed=v((128, 512), BF16),
        halo_x=v((224, 512), BF16),
        halo=v((224, 1024), BF16),
        uk_h=v((224, 512), F32),
        nk_h=v((224, 512), F32),
        normed_th=v((ny // 2, 2, 64, 224), BF16),
        act_h=v((224, 1024), BF16),
        qm=v((4, 256, 128), BF16),
        gm=v((4, 256, 128), BF16),
        mask=v((128, 128), F32),
        mask_h=v((224, 128), F32),
        e_l=v((4, 128, 256), F32),
        d_l=v((4, 128, 256), F32),
        p_h=v((4, 224, 256), BF16),
        p_l=v((4, 128, 256), BF16),
        ds_l=v((4, 128, 256), BF16),
        ds_h=v((4, 224, 256), BF16),
        gsend=v((224, 512), BF16),
        gn=v((128, 512), F32),
        grecv=v((224, 512), BF16),
        att=v((128, 512), BF16),
        att_t=v((ny // 2, 2, 64, 128), BF16),
        act=v((128, 1536), BF16),
        inv=v((128, 128), F32),
    )
    names = list(scratch)
    count = reduce_count(nx, ny, nz) + 16

    def kernel(x_hbm, dy_hbm, gain_ref, wqkv_hbm, wout_hbm, scale_ref, mixed_ref, gin_ref, gqkv_ref, gout_ref, *rest):
        b = dict(zip(names, rest))
        links = Links(*rest[len(names) : len(names) + 2])
        load_sem, owner_sems = rest[len(names) + 2 :]
        x_ref, dy_ref, wqkv_ref, wout_ref = b["x"], b["dy"], b["wqkv"], b["wout"]
        loads = [
            pltpu.make_async_copy(source, target, load_sem.at[i])
            for i, (source, target) in enumerate(
                ((x_hbm, x_ref), (wqkv_hbm, wqkv_ref), (dy_hbm, dy_ref), (wout_hbm, wout_ref))
            )
        ]
        for c in loads:
            c.start()
        p = Place()

        def neighbour(dy_step, dx_step):
            return ((p.gy + dy_step) % p.ngy, (p.gx + dx_step) % p.ngx, p.z)

        arrive = enter([neighbour(*block[3:]) for block in BLOCKS] + p.reduce_peers())

        def exchange(source, target):
            return [
                links.start(source(start, size), target.at[land : land + size], neighbour(*step))
                for start, size, land, *step in BLOCKS
            ]

        low = iota((128, 128), 1) < 64
        ones = jnp.where((iota((128, 128), 0) < 64) == low, 1.0, 0.0).astype(BF16)

        def masked(a):
            zero = jnp.zeros_like(a)
            return jnp.concatenate([jnp.where(low, a, zero), jnp.where(low, zero, a)], axis=0).astype(BF16)

        choose = jnp.where(edge_tokens(iota((128, 128), 0)) == iota((128, 128), 1), 1.0, 0.0)
        loads[0].wait()
        b["packed"][...] = dot(choose.astype(BF16), x_ref[...]).astype(BF16)
        arrive()

        def edge_block(start, size):
            if start == 0:
                return x_ref.at[0:48]
            if start == 48:
                return x_ref.at[80:128]
            return b["packed"].at[start - 96 : start - 96 + size]

        edges = exchange(edge_block, b["halo_x"])

        def norm(source, normed_ref, turned_ref):
            xf = source[...].astype(F32)
            inv_rms = lax.rsqrt(jnp.sum(xf * xf, -1, keepdims=True) * (1.0 / 512) + 1e-6)
            normed = xf * inv_rms * gain_ref[...]
            normed_ref[...] = normed.astype(BF16)
            for i in range(4):
                turned = normed[:, i * 128 : i * 128 + 128].T.astype(BF16)
                turned_ref[i] = turned.reshape(2, 64, turned.shape[1])
            return inv_rms

        def keys_values(normed_ref, uk_ref, nk_ref, kv_ref):
            normed = normed_ref[...]
            for i in range(4):
                lanes = slice(i * 128, i * 128 + 128)
                k_raw = dot(normed, wqkv_ref[:, 512 + i * 128 : 640 + i * 128])
                nk = lax.rsqrt(head_sum(k_raw * k_raw, ones) + 1e-6)
                uk = k_raw * nk
                nk_ref[:, lanes] = nk
                uk_ref[:, lanes] = uk
                kv_ref[:, lanes] = uk.astype(BF16)
            kv_ref[:, 512:1024] = dot(normed, wqkv_ref[:, 1024:1536]).astype(BF16)

        inv_rms = norm(x_ref, b["normed"], b["normed_t"])
        b["inv"][...] = jnp.broadcast_to(inv_rms, (128, 128))
        token = iota((128, 128), 0)
        b["mask"][...] = jnp.where(near(token >> 4, token & 15, (128, 128)), 1.0, 0.0)
        row, col, there = halo_place(iota((224, 128), 0))
        all_row, all_col = row + p.gy * 8, col + p.gx * 16
        there = there & (all_row >= 0) & (all_row < 8 * p.ngy) & (all_col >= 0) & (all_col < 16 * p.ngx)
        b["mask_h"][...] = jnp.where(there & near(row, col, (224, 128)), 1.0, 0.0)
        loads[1].wait()
        keys_values(b["normed"], b["uk"], b["nk"], b["kv"])
        loads[2].wait()
        loads[3].wait()
        for i in range(4):
            lanes = slice(i * 128, i * 128 + 128)
            q_raw = dot(b["normed"][...], wqkv_ref[:, lanes])
            nq = lax.rsqrt(head_sum(q_raw * q_raw, ones) + 1e-6)
            uq = q_raw * nq
            scale = jnp.where(low, scale_ref[2 * i], scale_ref[2 * i + 1])
            b["nq"][:, lanes] = nq * scale
            b["uq"][:, lanes] = uq
            b["qm"][i] = masked(uq * scale)
            b["gm"][i] = masked(dot(dy_ref[...], wout_ref[lanes, :], TURN))

        sums, mids = [], []
        for i in range(4):
            lanes, more = slice(i * 128, i * 128 + 128), slice(512 + i * 128, 640 + i * 128)
            e = jnp.exp(dot(b["kv"][:, lanes], b["qm"][i], TURN)) * twice(b["mask"][...])
            d = dot(b["kv"][:, more], b["gm"][i], TURN)
            b["e_l"][i] = e
            b["d_l"][i] = d
            sums.append(jnp.sum(e, 0, keepdims=True))
            mids.append(jnp.sum(e * d, 0, keepdims=True))
        for c in edges:
            c.wait_recv()

        norm(b["halo_x"], b["normed_h"], b["normed_th"])
        keys_values(b["normed_h"], b["uk_h"], b["nk_h"], b["halo"])

        def key_gradient(uk, nk, gku):
            return (nk * (gku - uk * head_sum(uk * gku, ones))).astype(BF16)

        for i in range(4):
            lanes, more = slice(i * 128, i * 128 + 128), slice(512 + i * 128, 640 + i * 128)
            e = jnp.exp(dot(b["halo"][:, lanes], b["qm"][i], TURN)) * twice(b["mask_h"][...])
            d = dot(b["halo"][:, more], b["gm"][i], TURN)
            inverse = 1.0 / (sums[i] + jnp.sum(e, 0, keepdims=True))
            mid = (mids[i] + jnp.sum(e * d, 0, keepdims=True)) * inverse
            probs_h = e * inverse
            ds_h = (probs_h * (d - mid)).astype(BF16)
            probs_h = probs_h.astype(BF16)
            probs = b["e_l"][i] * inverse
            ds = (probs * (b["d_l"][i] - mid)).astype(BF16)
            probs = probs.astype(BF16)
            b["p_h"][i] = probs_h
            b["ds_h"][i] = ds_h
            b["p_l"][i] = probs
            b["ds_l"][i] = ds

        rows = 32 * ny

        def part_b(core, tiles):
            lanes = slice(tiles.start * 128, tiles.stop * 128)
            a = dot(b["normed_t"][:, core].reshape(rows, 128), b["act"][:, 512 + lanes.start : 512 + lanes.stop])
            a += dot(b["normed_th"][:, core].reshape(rows, 224), b["act_h"][:, lanes])
            return [(tiles.start + t, a[:, t * 128 : t * 128 + 128].reshape(ny, 2, 16, 128)) for t in range(4)]

        def send_b(tiles):
            for t, tile in part_b(1 - p.core, tiles):
                b["s0b"][:, :, t] = tile.astype(BF16)
            return links.start(b["s0b"].at[:, :, tiles], b["r0b"].at[:, :, tiles], p.other_core())

        for i in range(4):
            more = slice(512 + i * 128, 640 + i * 128)
            b["act_h"][:, more] = dot(b["p_h"][i], b["gm"][i]).astype(BF16)
            b["act"][:, 1024 + i * 128 : 1152 + i * 128] = dot(b["p_l"][i], b["gm"][i]).astype(BF16)
        first_b = [send_b(HALVES[0])]
        for i in range(4):
            lanes, more = slice(i * 128, i * 128 + 128), slice(512 + i * 128, 640 + i * 128)
            b["act_h"][:, lanes] = key_gradient(b["uk_h"][:, lanes], b["nk_h"][:, lanes], dot(b["ds_h"][i], b["qm"][i]))
            b["act"][:, more] = key_gradient(b["uk"][:, lanes], b["nk"][:, lanes], dot(b["ds_l"][i], b["qm"][i]))
        first_b.append(send_b(HALVES[1]))
        for tiles in HALVES:
            for t, tile in part_b(p.core, tiles):
                b["own_b"][:, :, t] = tile

        for i in range(4):
            lanes, more = slice(i * 128, i * 128 + 128), slice(512 + i * 128, 640 + i * 128)
            att_t = pick(dot(b["kv"][:, more], b["p_l"][i], FIRST) + dot(b["halo"][:, more], b["p_h"][i], FIRST))
            gqs_t = pick(dot(b["kv"][:, lanes], b["ds_l"][i], FIRST) + dot(b["halo"][:, lanes], b["ds_h"][i], FIRST))
            b["att_t"][i] = att_t.astype(BF16).reshape(2, 64, 128)
            b["att"][:, lanes] = att_t.T.astype(BF16)
            gqs = gqs_t.T
            uq = b["uq"][:, lanes]
            b["act"][:, lanes] = (b["nq"][:, lanes] * (gqs - uq * head_sum(uq * gqs, ones))).astype(BF16)

        def part_a(core, tiles):
            lanes = slice(tiles.start * 128, tiles.stop * 128)
            q_part = dot(b["normed_t"][:, core].reshape(rows, 128), b["act"][:, lanes])
            out_part = dot(b["att_t"][:, core].reshape(rows, 128), dy_ref[:, lanes])
            return [
                jnp.concatenate(
                    [a[:, t * 128 : t * 128 + 128].reshape(ny, nx, 8, 128) for a in (q_part, out_part)], axis=2
                )
                for t in range(tiles.stop - tiles.start)
            ]

        first_a = []
        for tiles in CHUNKS:
            for t, tile in enumerate(part_a(1 - p.core, tiles)):
                b["s0a"][:, :, tiles.start + t] = tile.astype(BF16)
            first_a.append(links.start(b["s0a"].at[:, :, tiles], b["r0a"].at[:, :, tiles], p.other_core()))
        ys, zs = start_b(p, links, b, first_b)
        for tiles in CHUNKS:
            for t, tile in enumerate(part_a(p.core, tiles)):
                b["own_a"][:, :, tiles.start + t] = tile

        grads = []

        def send_grads():
            grads.extend(exchange(lambda start, size: b["gsend"].at[start : start + size], b["grecv"]))

        def meanwhile():
            b["gsend"][...] = dot(b["act_h"][...], wqkv_ref[:, 512:1536], TURN).astype(BF16)
            b["gn"][...] = dot(b["act"][...], wqkv_ref[...], TURN)
            mixed_ref[...] = (x_ref[...].astype(F32) + dot(b["att"][...], wout_ref[...])).astype(BF16)

        def finish():
            back = jnp.where(edge_tokens(iota((128, 128), 1)) == iota((128, 128), 0), 1.0, 0.0)
            for c in grads:
                c.wait_recv()
            grad_n = b["gn"][...] + dot(back.astype(BF16), b["grecv"][96:224, :])
            grad_n = jnp.concatenate(
                [
                    grad_n[0:48] + b["grecv"][0:48, :].astype(F32),
                    grad_n[48:80],
                    grad_n[80:128] + b["grecv"][48:96, :].astype(F32),
                ],
                axis=0,
            )
            g = grad_n * gain_ref[...]
            xf = x_ref[...].astype(F32)
            inv = b["inv"][:, 0:1]
            mean = jnp.sum(xf * g, -1, keepdims=True) * (1.0 / 512)
            gin_ref[...] = (dy_ref[...].astype(F32) + inv * g - xf * (inv * inv * inv * mean)).astype(BF16)

        reduce_tail(p, links, b, ys, zs, first_a, owner_sems, meanwhile, send_grads, finish, factor, gqkv_ref, gout_ref)
        links.drain()

    vm, anywhere = pl.BlockSpec(memory_space=pltpu.VMEM), pl.BlockSpec(memory_space=pl.ANY)
    return pl.pallas_call(
        kernel,
        out_shape=(
            jax.ShapeDtypeStruct((128, 512), BF16),
            jax.ShapeDtypeStruct((128, 512), BF16),
            jax.ShapeDtypeStruct((8, 1536), F32),
            jax.ShapeDtypeStruct((8, 512), F32),
        ),
        in_specs=[anywhere, anywhere, vm, anywhere, anywhere, pl.BlockSpec(memory_space=pltpu.SMEM)],
        out_specs=(vm, vm, vm, vm),
        scratch_shapes=[scratch[n] for n in names]
        + [pltpu.SemaphoreType.DMA((count,)), pltpu.SemaphoreType.DMA((count,))]
        + [pltpu.SemaphoreType.DMA((4,)), pltpu.SemaphoreType.DMA((2,))],
        compiler_params=pltpu.CompilerParams(
            collective_id=1, has_side_effects=True, vmem_limit_bytes=56 * 1024 * 1024
        ),
        cost_estimate=pl.CostEstimate(flops=10**9, bytes_accessed=4 * 10**6, transcendentals=10**6),
        name="block",
    )(x, dy, gain, w_qkv, w_out, head_scale)


def hand_over(*arrays):
    count = len(arrays)

    def kernel(*refs):
        for i in range(count):
            refs[count + i][...] = refs[i][...]

    vm = pl.BlockSpec(memory_space=pltpu.VMEM)
    return pl.pallas_call(
        kernel,
        out_shape=tuple(jax.ShapeDtypeStruct(a.shape, a.dtype) for a in arrays),
        in_specs=[vm] * count,
        out_specs=(vm,) * count,
        name="hand_over",
    )(*arrays)


def per_device(inputs, cotangent, norm_gain, w_qkv, w_out, head_scale):
    shape, width = inputs.shape, inputs.shape[-1]
    tokens = shape[1] * shape[2]
    factor = 1.0 / math.sqrt(
        lax.axis_size("img") * lax.axis_size("gy") * lax.axis_size("gx") * tokens
    )
    results = block_call(
        inputs.reshape(tokens, width),
        cotangent.reshape(tokens, width),
        norm_gain.reshape(1, width),
        w_qkv,
        w_out,
        head_scale,
        factor,
    )
    mixed, grad_input, grad_qkv, grad_out = hand_over(*results)
    return (mixed.reshape(shape), grad_input.reshape(shape), grad_qkv, grad_out)


def solution(mesh):
    tokens, rows = P("img", "gy", "gx", None), P(("gy", "gx"), None)
    return jax.shard_map(
        per_device,
        mesh=mesh,
        in_specs=(tokens, tokens, P(), P(), P(), P()),
        out_specs=(tokens, tokens, rows, rows),
        check_vma=False,
    )
```

```python
import math

import jax
import jax.numpy as jnp
from jax import lax
from jax.experimental import pallas as pl
from jax.experimental.pallas import tpu as pltpu
from jax.sharding import PartitionSpec as P

F32, BF16 = jnp.float32, jnp.bfloat16


class Links:
    def __init__(self, send, recv):
        self.send, self.recv, self.used, self.all = send, recv, 0, []

    def start(self, src, dst, device):
        copy = pltpu.make_async_remote_copy(
            src_ref=src,
            dst_ref=dst,
            send_sem=self.send.at[self.used],
            recv_sem=self.recv.at[self.used],
            device_id=device,
            device_id_type=pl.DeviceIdType.MESH,
        )
        copy.start()
        self.used += 1
        self.all.append(copy)
        return copy

    def drain(self):
        for copy in self.all:
            copy.wait_send()


class Place:
    def __init__(self):
        gy, gx, self.z = lax.axis_index("gy"), lax.axis_index("gx"), lax.axis_index("img")
        self.gy, self.gx = gy, gx
        self.ngy, self.ngx, self.nz = (lax.axis_size(a) for a in ("gy", "gx", "img"))
        self.nx = self.ngx // 2
        self.ny = self.ngy
        self.core, self.x = gy % 2, gx % self.nx
        self.y = (gy // 2) * 2 + gx // self.nx

    def other_core(self):
        return (self.gy + 1 - 2 * self.core, self.gx, self.z)

    def x_peer(self, k):
        to = (self.x + k) % self.nx
        return to, (self.gy, self.gx - self.x + to, self.z)

    def y_peer(self, k):
        to = (self.y + k) % self.ny
        return to, ((to // 2) * 2 + self.core, (to % 2) * self.nx + self.x, self.z)

    def z_peer(self, k):
        to = (self.z + k) % self.nz
        return to, (self.gy, self.gx, to)

    def reduce_peers(self):
        return (
            [self.other_core()]
            + [self.x_peer(k)[1] for k in range(1, self.nx)]
            + [self.y_peer(k)[1] for k in range(1, self.ny)]
            + [self.z_peer(k)[1] for k in range(1, self.nz)]
        )


def enter(devices):
    barrier = pltpu.get_barrier_semaphore()
    for device in devices:
        pl.semaphore_signal(barrier, inc=1, device_id=device, device_id_type=pl.DeviceIdType.MESH)
    return lambda: pl.semaphore_wait(barrier, len(devices))


def reduce_scratch(nx, ny, nz):
    v = pltpu.VMEM
    return dict(
        r0a=v((ny, nx, 4, 16, 128), BF16),
        r0b=v((ny, 2, 8, 16, 128), BF16),
        s1a=v((ny, nx, 4, 16, 128), BF16),
        s1b=v((ny, 2, 8, 16, 128), BF16),
        rxa=v((nx - 1, ny, 4, 16, 128), BF16),
        s2a=v((ny, 4, 16, 128), BF16),
        rya=v((ny - 1, 4, 16, 128), BF16),
        za=v((nz, 4, 16, 128), BF16),
        ryb=v((ny - 1, 8, 16, 128), BF16),
        rzb=v((nz - 1, ny, 16, 128), BF16),
        syb=v((2, nz, 8, 128), F32),
        szb=v((2, ny, 8, 128), F32),
        mb=v((nx * nz, 8, 128), F32),
        gb=v((nz, 8, 128), F32),
    )


def reduce_count(nx, ny, nz):
    return 4 + 2 * (nx - 1) + 3 * (ny - 1) + 4 * (nz - 1)


def core_add(s1, own, got, tiles):
    def add(i, _):
        s1[i, :, tiles] = (own[i, :, tiles].astype(F32) + got[i, :, tiles].astype(F32)).astype(BF16)
        return 0

    lax.fori_loop(0, s1.shape[0], add, 0)


CHUNKS = (slice(0, 2), slice(2, 4))
HALVES = (slice(4, 8), slice(0, 4))


def start_a(p, links, b, firsts):
    xs = []
    for first, tiles in zip(firsts, CHUNKS):
        first.wait_recv()
        core_add(b["s1a"], b["own_a"], b["r0a"], tiles)
        sent = []
        for k in far_first(p.nx):
            to, device = p.x_peer(k)
            sent.append(links.start(b["s1a"].at[:, to, tiles], b["rxa"].at[k - 1, :, tiles], device))
        xs.append(sent)
    return xs


def far_first(n):
    return sorted(range(1, n), key=lambda k: -min(k, n - k))


def start_b(p, links, b, firsts):
    for first, tiles in zip(firsts, HALVES):
        first.wait_recv()
        core_add(b["s1b"], b["own_b"], b["r0b"], tiles)
    ys, zs = [], []
    for k in far_first(p.ny):
        to, device = p.y_peer(k)
        ys.append(links.start(b["s1b"].at[to, 0], b["ryb"].at[k - 1], device))
        to, device = p.z_peer(k)
        zs.append(links.start(b["s1b"].at[:, 1, to], b["rzb"].at[k - 1], device))
    return ys, zs


def reduce_tail(p, links, b, ys, zs, first_a, owner_sems, meanwhile, send_grads, finish, factor, qkv_ref, out_ref):
    nx, ny, nz = p.nx, p.ny, p.nz
    xs = start_a(p, links, b, first_a)
    meanwhile()

    y2 = []
    for arriving, tiles in zip(xs, CHUNKS):
        for c in arriving:
            c.wait_recv()

        def add_x(i, _):
            total = b["s1a"][i, p.x, tiles].astype(F32)
            for k in range(nx - 1):
                total += b["rxa"][k, i, tiles].astype(F32)
            b["s2a"][i, tiles] = total.astype(BF16)
            return 0

        lax.fori_loop(0, ny, add_x, 0)
        sent = []
        for k in far_first(ny):
            to, device = p.y_peer(k)
            sent.append(links.start(b["s2a"].at[to, tiles], b["rya"].at[k - 1, tiles], device))
        y2.append(sent)

    for c in ys:
        c.wait_recv()

    def add_y(i, _):
        total = b["s1b"][p.y, 0, i].astype(F32)
        for k in range(ny - 1):
            total += b["ryb"][k, i].astype(F32)
        b["syb"][0, i] = total[0:8]
        b["syb"][1, i] = total[8:16]
        return 0

    lax.fori_loop(0, nz, add_y, 0)

    def to_owner(tile, slot, device):
        return pltpu.make_async_remote_copy(
            src_ref=tile,
            dst_ref=b["mb"].at[slot],
            send_sem=owner_sems.at[0],
            recv_sem=owner_sems.at[1],
            device_id=device,
            device_id_type=pl.DeviceIdType.MESH,
        )

    def spread(tiles, first, peers, mine):
        for j in range(2):
            column = p.gx - p.x + first + j
            for k in far_first(peers) + [0]:
                if first == 0:
                    to, device = p.z_peer(k)
                    device = (p.gy, column, device[2])
                else:
                    to, device = p.y_peer(k)
                    device = (device[0], device[1] - p.x + first + j, p.z)
                copy = to_owner(tiles.at[j, to], p.x * peers + mine, device)
                if k > 0:
                    copy.start()
                else:
                    pl.when(p.x != first + j)(copy.start)

    spread(b["syb"], 0, nz, p.z)

    for c in zs:
        c.wait_recv()

    def add_z(i, _):
        total = b["s1b"][i, 1, p.z].astype(F32)
        for k in range(nz - 1):
            total += b["rzb"][k, i].astype(F32)
        b["szb"][0, i] = total[0:8]
        b["szb"][1, i] = total[8:16]
        return 0

    lax.fori_loop(0, ny, add_z, 0)
    spread(b["szb"], 2, ny, p.y)

    @pl.when(p.x < 2)
    def _():
        b["mb"][p.x * nz + p.z] = b["syb"][p.x % 2, p.z]

    @pl.when(p.x >= 2)
    def _():
        b["mb"][p.x * ny + p.y] = b["szb"][p.x % 2, p.y]

    send_grads()

    last_a = []
    for arriving, tiles in zip(y2, CHUNKS):
        for c in arriving:
            c.wait_recv()
        total = b["s2a"][p.y, tiles].astype(F32)
        for k in range(ny - 1):
            total += b["rya"][k, tiles].astype(F32)
        b["za"][p.z, tiles] = total.astype(BF16)
        for k in far_first(nz):
            to, device = p.z_peer(k)
            last_a.append(links.start(b["za"].at[p.z, tiles], b["za"].at[p.z, tiles], device))

    others = b["mb"].at[0 : nx * nz - 1]
    pltpu.make_async_copy(others, others, owner_sems.at[1]).wait()
    total = jnp.sum(b["mb"][...], axis=0)
    b["gb"][p.z] = total * factor
    last = []
    for k in far_first(nz):
        to, device = p.z_peer(k)
        last.append(links.start(b["gb"].at[p.z], b["gb"].at[p.z], device))
    finish()
    for c in last_a:
        c.wait_recv()
    total = b["za"][0].astype(F32)
    for z in range(1, nz):
        total += b["za"][z].astype(F32)
    total = total * factor
    for t in range(4):
        qkv_ref[:, t * 128 : t * 128 + 128] = total[t, 0:8]
        out_ref[:, t * 128 : t * 128 + 128] = total[t, 8:16]
    for c in last:
        c.wait_recv()
    pltpu.make_async_copy(others, others, owner_sems.at[0]).wait()
    for t in range(8):
        qkv_ref[:, 512 + t * 128 : 640 + t * 128] = b["gb"][t]


def dot(a, b, dims=((1,), (0,))):
    return lax.dot_general(a, b, (dims, ((), ())), preferred_element_type=F32)


TURN = ((1,), (1,))
FIRST = ((0,), (0,))


def iota(shape, dim):
    return lax.broadcasted_iota(jnp.int32, shape, dim)


def edge_tokens(j):
    side = j & 31
    side_token = jnp.where((side >> 3) < 3, (side & 7) * 16 + (side >> 3) + 13 * ((j >> 5) & 1), -1)
    corner = (j - 64) >> 4
    down, across = (j >> 2) & 3, j & 3
    token = (down + 5 * (corner >> 1)) * 16 + across + 13 * (corner & 1)
    corner_token = jnp.where((down < 3) & (across < 3), token, -1)
    return jnp.where(j < 64, side_token, corner_token)


def halo_place(j):
    row = jnp.where(j < 48, (j >> 4) - 3, (j >> 4) + 5)
    col = j & 15
    side = j & 31
    is_side = (j >= 96) & (j < 160)
    row = jnp.where(is_side, side & 7, row)
    col = jnp.where(is_side, (side >> 3) + jnp.where(j < 128, -3, 16), col)
    corner = (j - 160) >> 4
    down, across = (j >> 2) & 3, j & 3
    is_corner = j >= 160
    row = jnp.where(is_corner, down + jnp.where(corner < 2, -3, 8), row)
    col = jnp.where(is_corner, across + jnp.where((corner & 1) == 0, -3, 16), col)
    filled = jnp.where(is_side, side >> 3, jnp.where(is_corner, jnp.maximum(down, across), 0))
    return row, col, filled < 3


def near(row, col, shape):
    query = iota(shape, 1)
    return (jnp.abs(row - (query >> 4)) <= 3) & (jnp.abs(col - (query & 15)) <= 3)


def twice(a):
    return jnp.concatenate([a, a], axis=1)


def head_sum(a, ones):
    top = a.astype(BF16)
    rest = (a - top.astype(F32)).astype(BF16)
    return dot(top, ones) + dot(rest, ones)


def pick(a):
    return jnp.concatenate([a[0:64, 0:128], a[64:128, 128:256]], axis=0)


BLOCKS = (
    (160, 16, 208, -1, -1),
    (176, 16, 192, -1, 1),
    (192, 16, 176, 1, -1),
    (208, 16, 160, 1, 1),
    (96, 32, 128, 0, -1),
    (128, 32, 96, 0, 1),
    (0, 48, 48, -1, 0),
    (48, 48, 0, 1, 0),
)


def block_call(x, dy, gain, w_qkv, w_out, head_scale, factor):
    nx, ny, nz = lax.axis_size("gx") // 2, lax.axis_size("gy"), lax.axis_size("img")
    v = pltpu.VMEM
    scratch = reduce_scratch(nx, ny, nz)
    scratch.update(
        own_a=v((ny, nx, 4, 16, 128), F32),
        own_b=v((ny, 2, 8, 16, 128), F32),
        s0a=v((ny, nx, 4, 16, 128), BF16),
        s0b=v((ny, 2, 8, 16, 128), BF16),
        normed=v((128, 512), BF16),
        normed_h=v((224, 512), BF16),
        normed_t=v((ny // 2, 2, 64, 128), BF16),
        uq=v((128, 512), F32),
        uk=v((128, 512), F32),
        nq=v((128, 512), F32),
        nk=v((128, 512), F32),
        x=v((128, 512), BF16),
        dy=v((128, 512), BF16),
        wqkv=v((512, 1536), BF16),
        wout=v((512, 512), BF16),
        kv=v((128, 1024), BF16),
        packed=v((128, 512), BF16),
        halo_x=v((224, 512), BF16),
        halo=v((224, 1024), BF16),
        uk_h=v((224, 512), F32),
        nk_h=v((224, 512), F32),
        normed_th=v((ny // 2, 2, 64, 224), BF16),
        act_h=v((224, 1024), BF16),
        qm=v((4, 256, 128), BF16),
        gm=v((4, 256, 128), BF16),
        mask=v((128, 128), F32),
        mask_h=v((224, 128), F32),
        e_l=v((4, 128, 256), F32),
        d_l=v((4, 128, 256), F32),
        p_h=v((4, 224, 256), BF16),
        p_l=v((4, 128, 256), BF16),
        ds_l=v((4, 128, 256), BF16),
        ds_h=v((4, 224, 256), BF16),
        gsend=v((224, 512), BF16),
        gn=v((128, 512), F32),
        grecv=v((224, 512), BF16),
        att=v((128, 512), BF16),
        att_t=v((ny // 2, 2, 64, 128), BF16),
        act=v((128, 1536), BF16),
        inv=v((128, 128), F32),
    )
    names = list(scratch)
    count = reduce_count(nx, ny, nz) + 16

    def kernel(x_hbm, dy_hbm, gain_ref, wqkv_hbm, wout_hbm, scale_ref, mixed_ref, gin_ref, gqkv_ref, gout_ref, *rest):
        b = dict(zip(names, rest))
        links = Links(*rest[len(names) : len(names) + 2])
        load_sem, owner_sems = rest[len(names) + 2 :]
        x_ref, dy_ref, wqkv_ref, wout_ref = b["x"], b["dy"], b["wqkv"], b["wout"]
        loads = [
            pltpu.make_async_copy(source, target, load_sem.at[i])
            for i, (source, target) in enumerate(
                ((x_hbm, x_ref), (wqkv_hbm, wqkv_ref), (dy_hbm, dy_ref), (wout_hbm, wout_ref))
            )
        ]
        for c in loads:
            c.start()
        p = Place()

        def neighbour(dy_step, dx_step):
            return ((p.gy + dy_step) % p.ngy, (p.gx + dx_step) % p.ngx, p.z)

        arrive = enter([neighbour(*block[3:]) for block in BLOCKS] + p.reduce_peers())

        def exchange(source, target):
            return [
                links.start(source(start, size), target.at[land : land + size], neighbour(*step))
                for start, size, land, *step in BLOCKS
            ]

        low = iota((128, 128), 1) < 64
        ones = jnp.where((iota((128, 128), 0) < 64) == low, 1.0, 0.0).astype(BF16)

        def masked(a):
            zero = jnp.zeros_like(a)
            return jnp.concatenate([jnp.where(low, a, zero), jnp.where(low, zero, a)], axis=0).astype(BF16)

        choose = jnp.where(edge_tokens(iota((128, 128), 0)) == iota((128, 128), 1), 1.0, 0.0)
        loads[0].wait()
        b["packed"][...] = dot(choose.astype(BF16), x_ref[...]).astype(BF16)
        arrive()

        def edge_block(start, size):
            if start == 0:
                return x_ref.at[0:48]
            if start == 48:
                return x_ref.at[80:128]
            return b["packed"].at[start - 96 : start - 96 + size]

        edges = exchange(edge_block, b["halo_x"])

        def norm(source, normed_ref, turned_ref):
            xf = source[...].astype(F32)
            inv_rms = lax.rsqrt(jnp.sum(xf * xf, -1, keepdims=True) * (1.0 / 512) + 1e-6)
            normed = xf * inv_rms * gain_ref[...]
            normed_ref[...] = normed.astype(BF16)
            for i in range(4):
                turned = normed[:, i * 128 : i * 128 + 128].T.astype(BF16)
                turned_ref[i] = turned.reshape(2, 64, turned.shape[1])
            return inv_rms

        def keys_values(normed_ref, uk_ref, nk_ref, kv_ref):
            normed = normed_ref[...]
            for i in range(4):
                lanes = slice(i * 128, i * 128 + 128)
                k_raw = dot(normed, wqkv_ref[:, 512 + i * 128 : 640 + i * 128])
                nk = lax.rsqrt(head_sum(k_raw * k_raw, ones) + 1e-6)
                uk = k_raw * nk
                nk_ref[:, lanes] = nk
                uk_ref[:, lanes] = uk
                kv_ref[:, lanes] = uk.astype(BF16)
            kv_ref[:, 512:1024] = dot(normed, wqkv_ref[:, 1024:1536]).astype(BF16)

        inv_rms = norm(x_ref, b["normed"], b["normed_t"])
        b["inv"][...] = jnp.broadcast_to(inv_rms, (128, 128))
        token = iota((128, 128), 0)
        b["mask"][...] = jnp.where(near(token >> 4, token & 15, (128, 128)), 1.0, 0.0)
        row, col, there = halo_place(iota((224, 128), 0))
        all_row, all_col = row + p.gy * 8, col + p.gx * 16
        there = there & (all_row >= 0) & (all_row < 8 * p.ngy) & (all_col >= 0) & (all_col < 16 * p.ngx)
        b["mask_h"][...] = jnp.where(there & near(row, col, (224, 128)), 1.0, 0.0)
        loads[1].wait()
        keys_values(b["normed"], b["uk"], b["nk"], b["kv"])
        loads[2].wait()
        loads[3].wait()
        for i in range(4):
            lanes = slice(i * 128, i * 128 + 128)
            q_raw = dot(b["normed"][...], wqkv_ref[:, lanes])
            nq = lax.rsqrt(head_sum(q_raw * q_raw, ones) + 1e-6)
            uq = q_raw * nq
            scale = jnp.where(low, scale_ref[2 * i], scale_ref[2 * i + 1])
            b["nq"][:, lanes] = nq * scale
            b["uq"][:, lanes] = uq
            b["qm"][i] = masked(uq * scale)
            b["gm"][i] = masked(dot(dy_ref[...], wout_ref[lanes, :], TURN))

        sums, mids = [], []
        for i in range(4):
            lanes, more = slice(i * 128, i * 128 + 128), slice(512 + i * 128, 640 + i * 128)
            e = jnp.exp(dot(b["kv"][:, lanes], b["qm"][i], TURN)) * twice(b["mask"][...])
            d = dot(b["kv"][:, more], b["gm"][i], TURN)
            b["e_l"][i] = e
            b["d_l"][i] = d
            sums.append(jnp.sum(e, 0, keepdims=True))
            mids.append(jnp.sum(e * d, 0, keepdims=True))
        for c in edges:
            c.wait_recv()

        norm(b["halo_x"], b["normed_h"], b["normed_th"])
        keys_values(b["normed_h"], b["uk_h"], b["nk_h"], b["halo"])

        def key_gradient(uk, nk, gku):
            return (nk * (gku - uk * head_sum(uk * gku, ones))).astype(BF16)

        for i in range(4):
            lanes, more = slice(i * 128, i * 128 + 128), slice(512 + i * 128, 640 + i * 128)
            e = jnp.exp(dot(b["halo"][:, lanes], b["qm"][i], TURN)) * twice(b["mask_h"][...])
            d = dot(b["halo"][:, more], b["gm"][i], TURN)
            inverse = 1.0 / (sums[i] + jnp.sum(e, 0, keepdims=True))
            mid = (mids[i] + jnp.sum(e * d, 0, keepdims=True)) * inverse
            probs_h = e * inverse
            ds_h = (probs_h * (d - mid)).astype(BF16)
            probs_h = probs_h.astype(BF16)
            probs = b["e_l"][i] * inverse
            ds = (probs * (b["d_l"][i] - mid)).astype(BF16)
            probs = probs.astype(BF16)
            b["p_h"][i] = probs_h
            b["ds_h"][i] = ds_h
            b["p_l"][i] = probs
            b["ds_l"][i] = ds

        rows = 32 * ny

        def part_b(core, tiles):
            lanes = slice(tiles.start * 128, tiles.stop * 128)
            a = dot(b["normed_t"][:, core].reshape(rows, 128), b["act"][:, 512 + lanes.start : 512 + lanes.stop])
            a += dot(b["normed_th"][:, core].reshape(rows, 224), b["act_h"][:, lanes])
            return [(tiles.start + t, a[:, t * 128 : t * 128 + 128].reshape(ny, 2, 16, 128)) for t in range(4)]

        def send_b(tiles):
            for t, tile in part_b(1 - p.core, tiles):
                b["s0b"][:, :, t] = tile.astype(BF16)
            return links.start(b["s0b"].at[:, :, tiles], b["r0b"].at[:, :, tiles], p.other_core())

        for i in range(4):
            more = slice(512 + i * 128, 640 + i * 128)
            b["act_h"][:, more] = dot(b["p_h"][i], b["gm"][i]).astype(BF16)
            b["act"][:, 1024 + i * 128 : 1152 + i * 128] = dot(b["p_l"][i], b["gm"][i]).astype(BF16)
        first_b = [send_b(HALVES[0])]
        for i in range(4):
            lanes, more = slice(i * 128, i * 128 + 128), slice(512 + i * 128, 640 + i * 128)
            b["act_h"][:, lanes] = key_gradient(b["uk_h"][:, lanes], b["nk_h"][:, lanes], dot(b["ds_h"][i], b["qm"][i]))
            b["act"][:, more] = key_gradient(b["uk"][:, lanes], b["nk"][:, lanes], dot(b["ds_l"][i], b["qm"][i]))
        first_b.append(send_b(HALVES[1]))
        for tiles in HALVES:
            for t, tile in part_b(p.core, tiles):
                b["own_b"][:, :, t] = tile

        for i in range(4):
            lanes, more = slice(i * 128, i * 128 + 128), slice(512 + i * 128, 640 + i * 128)
            att_t = pick(dot(b["kv"][:, more], b["p_l"][i], FIRST) + dot(b["halo"][:, more], b["p_h"][i], FIRST))
            gqs_t = pick(dot(b["kv"][:, lanes], b["ds_l"][i], FIRST) + dot(b["halo"][:, lanes], b["ds_h"][i], FIRST))
            b["att_t"][i] = att_t.astype(BF16).reshape(2, 64, 128)
            b["att"][:, lanes] = att_t.T.astype(BF16)
            gqs = gqs_t.T
            uq = b["uq"][:, lanes]
            b["act"][:, lanes] = (b["nq"][:, lanes] * (gqs - uq * head_sum(uq * gqs, ones))).astype(BF16)

        def part_a(core, tiles):
            lanes = slice(tiles.start * 128, tiles.stop * 128)
            q_part = dot(b["normed_t"][:, core].reshape(rows, 128), b["act"][:, lanes])
            out_part = dot(b["att_t"][:, core].reshape(rows, 128), dy_ref[:, lanes])
            return [
                jnp.concatenate(
                    [a[:, t * 128 : t * 128 + 128].reshape(ny, nx, 8, 128) for a in (q_part, out_part)], axis=2
                )
                for t in range(tiles.stop - tiles.start)
            ]

        first_a = []
        for tiles in CHUNKS:
            for t, tile in enumerate(part_a(1 - p.core, tiles)):
                b["s0a"][:, :, tiles.start + t] = tile.astype(BF16)
            first_a.append(links.start(b["s0a"].at[:, :, tiles], b["r0a"].at[:, :, tiles], p.other_core()))
        ys, zs = start_b(p, links, b, first_b)
        for tiles in CHUNKS:
            for t, tile in enumerate(part_a(p.core, tiles)):
                b["own_a"][:, :, tiles.start + t] = tile

        grads = []

        def send_grads():
            grads.extend(exchange(lambda start, size: b["gsend"].at[start : start + size], b["grecv"]))

        def meanwhile():
            b["gsend"][...] = dot(b["act_h"][...], wqkv_ref[:, 512:1536], TURN).astype(BF16)
            b["gn"][...] = dot(b["act"][...], wqkv_ref[...], TURN)
            mixed_ref[...] = (x_ref[...].astype(F32) + dot(b["att"][...], wout_ref[...])).astype(BF16)

        def finish():
            back = jnp.where(edge_tokens(iota((128, 128), 1)) == iota((128, 128), 0), 1.0, 0.0)
            for c in grads:
                c.wait_recv()
            grad_n = b["gn"][...] + dot(back.astype(BF16), b["grecv"][96:224, :])
            grad_n = jnp.concatenate(
                [
                    grad_n[0:48] + b["grecv"][0:48, :].astype(F32),
                    grad_n[48:80],
                    grad_n[80:128] + b["grecv"][48:96, :].astype(F32),
                ],
                axis=0,
            )
            g = grad_n * gain_ref[...]
            xf = x_ref[...].astype(F32)
            inv = b["inv"][:, 0:1]
            mean = jnp.sum(xf * g, -1, keepdims=True) * (1.0 / 512)
            gin_ref[...] = (dy_ref[...].astype(F32) + inv * g - xf * (inv * inv * inv * mean)).astype(BF16)

        reduce_tail(p, links, b, ys, zs, first_a, owner_sems, meanwhile, send_grads, finish, factor, gqkv_ref, gout_ref)
        links.drain()

    vm, anywhere = pl.BlockSpec(memory_space=pltpu.VMEM), pl.BlockSpec(memory_space=pl.ANY)
    return pl.pallas_call(
        kernel,
        out_shape=(
            jax.ShapeDtypeStruct((128, 512), BF16),
            jax.ShapeDtypeStruct((128, 512), BF16),
            jax.ShapeDtypeStruct((8, 1536), F32),
            jax.ShapeDtypeStruct((8, 512), F32),
        ),
        in_specs=[anywhere, anywhere, vm, anywhere, anywhere, pl.BlockSpec(memory_space=pltpu.SMEM)],
        out_specs=(vm, vm, vm, vm),
        scratch_shapes=[scratch[n] for n in names]
        + [pltpu.SemaphoreType.DMA((count,)), pltpu.SemaphoreType.DMA((count,))]
        + [pltpu.SemaphoreType.DMA((4,)), pltpu.SemaphoreType.DMA((2,))],
        compiler_params=pltpu.CompilerParams(
            collective_id=1, has_side_effects=True, vmem_limit_bytes=56 * 1024 * 1024
        ),
        cost_estimate=pl.CostEstimate(flops=10**9, bytes_accessed=4 * 10**6, transcendentals=10**6),
        name="block",
    )(x, dy, gain, w_qkv, w_out, head_scale)


def hand_over(*arrays):
    count = len(arrays)

    def kernel(*refs):
        for i in range(count):
            refs[count + i][...] = refs[i][...]

    vm = pl.BlockSpec(memory_space=pltpu.VMEM)
    return pl.pallas_call(
        kernel,
        out_shape=tuple(jax.ShapeDtypeStruct(a.shape, a.dtype) for a in arrays),
        in_specs=[vm] * count,
        out_specs=(vm,) * count,
        name="hand_over",
    )(*arrays)


def per_device(inputs, cotangent, norm_gain, w_qkv, w_out, head_scale):
    shape, width = inputs.shape, inputs.shape[-1]
    tokens = shape[1] * shape[2]
    factor = 1.0 / math.sqrt(
        lax.axis_size("img") * lax.axis_size("gy") * lax.axis_size("gx") * tokens
    )
    results = block_call(
        inputs.reshape(tokens, width),
        cotangent.reshape(tokens, width),
        norm_gain.reshape(1, width),
        w_qkv,
        w_out,
        head_scale,
        factor,
    )
    mixed, grad_input, grad_qkv, grad_out = hand_over(*results)
    return (mixed.reshape(shape), grad_input.reshape(shape), grad_qkv, grad_out)


def solution(mesh):
    tokens, rows = P("img", "gy", "gx", None), P(("gy", "gx"), None)
    return jax.shard_map(
        per_device,
        mesh=mesh,
        in_specs=(tokens, tokens, P(), P(), P(), P()),
        out_specs=(tokens, tokens, rows, rows),
        check_vma=False,
    )
```
